32 devices in a mesh: pipe: 4 (over z), expert: 8 (over y, x, core).
Axes of the slice: x: 2, y: 2, z: 4, core: 2. Of those that a mesh axis runs over, the one named last changes fastest.
Arguments:
- out_grad: bfloat16 [1024, 5120], P('expert'), may hold values from -0.59765625 to 0.59765625
- saved_inputs: bfloat16 [4, 1024, 5120], P('pipe', 'expert'), may hold values from -6 to 6
- router: bfloat16 [4, 5120, 160], P('pipe'), may hold values from -0.078125 to 0.078125
- routes: int32 [4, 1024, 6], P('pipe', 'expert'), may hold values from 0 to 159, all different within a row; in each aligned block of 128 rows (0 to 127, 128 to 255, ..., all dimensions but the last counted through in order) at most 9 rows name the same one
- hidden_saved: bfloat16 [4, 8, 72, 768], P('pipe', 'expert'), may hold values from -6 to 6
- codes: int32 [4, 8, 2, 768, 640], P('pipe', 'expert'), may hold values from 0 to 255
- codebook: bfloat16 [4, 8, 2, 256, 8], P('pipe', 'expert'), may hold values from -0.29882812 to 0.29882812
- scale: float32 [4, 8, 5120], P('pipe', 'expert'), may hold values from 0.25 to 1
Outputs:
- section_grads: bfloat16 [4, 1024, 5120], P('pipe', 'expert')
- codebook_grad: float32 [4, 8, 2, 256, 8], P('pipe', 'expert')
- scale_grad: float32 [4, 8, 5120], P('pipe', 'expert')
The draws below stay inside these ranges and needn't reach their ends.
Inputs may be any that keep to these rules, and one draw needn't show every extreme that they name: `routes`: each row names 6 different experts; in each aligned block of 128 rows (one device's tokens of one layer) no expert is named by more than 9 rows.
All inputs are finite; a program needn't handle non-finite values.
Results may differ from the reference program's by a relative error of at most 0.0063.
Values may be sent and summed in bfloat16 or wider, within the bound.
No kernel may reach another device: no remote copies, remote signals or barrier semaphores. Data moves between devices by JAX's collectives and lax.ppermute only.
A program may use at most 192 MiB of HBM per device.

```python
import math
from functools import partial
import jax
import jax.numpy as jnp
import numpy as np
from jax import lax

D = 5120
FF = 768
ROUTED = 160
TOP = 6
BOOKS = 2
CODES = 256
GROUP = 8
TOK_DEV = 128
MOST = 9
LAYERS = 4
EXPERTS = 8
TOKENS = 1024
RECV = 72


def with_ends(array, own_key, low, largest):
    extent = array.shape
    place = [jax.random.randint(jax.random.fold_in(own_key, axis), (), 0, extent[axis]) for axis in range(len(extent))]
    array = array.at[tuple(place)].set(low)
    longest = extent.index(max(extent))
    place[longest] = (place[longest] + 1) % extent[longest]
    return array.at[tuple(place)].set(largest)


def shard_levels(own_key, dims, pieces, least, largest):
    level = 1.0
    for dim, parts in pieces:
        draws = jax.random.uniform(jax.random.fold_in(jax.random.fold_in(own_key, 6), dim), (parts,), jnp.float32, least / len(pieces), largest / len(pieces))
        level = level * jnp.repeat(jnp.exp(draws), dims[dim] // parts).reshape((-1,) + (1,) * (len(dims) - 1 - dim))
    return level


def shared_out(rng, own, number, rows, number_of, top, limit, lean):
    sequence = jax.random.permutation(rng, number_of)
    packed, common = shares(number_of, rows * top, limit, lean, True), shares(number_of, rows * top, limit, lean, False)
    places = jnp.arange(number_of)

    def named(sizes, offset_by):
        used = int((sizes > 0).sum())
        fixed = max(1, used // 4)
        moved = fixed + (places - fixed + offset_by * (used - fixed)) % max(1, number_of - fixed)
        return jnp.zeros((number_of,), jnp.int32).at[sequence[jnp.where(places < fixed, places, moved)]].set(jnp.asarray(sizes, jnp.int32))

    sizes = jnp.where(number % 4 == 0, named(packed, number // 4), named(common, number - number // 4 - 1))
    mixed = jax.random.permutation(jax.random.fold_in(own, 3), number_of)
    source_of, receiver = mixed[0:number_of // 2 * 2:2], mixed[1:number_of // 2 * 2:2]
    margin = jnp.minimum(sizes[source_of] - 1, limit - sizes[receiver]) // 2
    margin = jnp.where((source_of == sequence[0]) | (receiver == sequence[0]) | (sizes[receiver] == 0), 0, jnp.maximum(margin, 0))
    moved = jax.random.randint(jax.random.fold_in(own, 4), (number_of // 2,), 0, 1 << 20) % (margin + 1)
    sizes = sizes.at[source_of].add(-moved).at[receiver].add(moved)
    labels = jnp.searchsorted(jnp.cumsum(sizes), jnp.arange(rows * top), side="right").astype(jnp.int32)
    grid = labels.reshape(top, rows).T
    grid = grid[jax.random.permutation(jax.random.fold_in(own, 1), rows)]
    offset_by = jax.random.randint(jax.random.fold_in(own, 2), (rows, 1), 0, top)
    return jnp.take_along_axis(grid, (jnp.arange(top)[None, :] + offset_by) % top, axis=1)


def shares(number_of, total, reach, slope, full):
    weights = [(1 << 20) // math.isqrt(rank ** slope) + 1 for rank in range(1, number_of + 1)]
    largest = reach if full else min(reach, max(-(-total // number_of), total * weights[0] // sum(weights)))
    least = 1 if total - largest >= number_of - 1 else 0
    holding, spare = [largest] + [least] * (number_of - 1), total - largest - least * (number_of - 1)
    while spare > 0:
        candidates = [i for i in range(1, number_of) if holding[i] < largest] or [i for i in range(1, number_of) if holding[i] < reach]
        whole, left = sum([weights[i] for i in candidates]), spare
        for i in candidates:
            addition = min(reach - holding[i], max(1, left * weights[i] // whole), spare)
            holding[i] = holding[i] + addition
            spare = spare - addition
    return np.array(holding)


def normal_values(stream_key, extent, width, bound, shards=(), kind=jnp.bfloat16):
    gain = shard_levels(stream_key, extent, shards, -0.22, 0.18) if shards else 1.0
    values = jax.random.normal(stream_key, extent, jnp.float32) * width * gain
    return jnp.minimum(jnp.maximum(values, -bound), bound).astype(kind)


def setup_inputs(seed: int = 0) -> dict:
    keys = jax.random.split(jax.random.key(seed), 9)
    out_grad = normal_values(keys[0], (TOKENS, D), 0.1, 0.59765625, ((0, 8),))
    saved_inputs = normal_values(keys[1], (LAYERS, TOKENS, D), 1.0, 6.0, ((0, 4), (1, 8)))
    router = normal_values(keys[2], (LAYERS, D, ROUTED), D ** -0.5, 0.078125, ((0, 4),))
    routes_keys = jax.random.split(jax.random.fold_in(keys[3], 1), LAYERS * TOKENS // TOK_DEV)
    routes_turns = jax.random.permutation(jax.random.fold_in(keys[3], 3), LAYERS * TOKENS // TOK_DEV)
    routes = jax.vmap(lambda own, number: shared_out(jax.random.fold_in(keys[3], 2), own, number, TOK_DEV, ROUTED, TOP, MOST, 2))(routes_keys, routes_turns).reshape((LAYERS, TOKENS, TOP))
    hidden_saved = normal_values(keys[4], (LAYERS, EXPERTS, RECV, FF), 1.0, 6.0, ((0, 4), (1, 8)))
    codes = with_ends(jax.random.randint(keys[5], (LAYERS, EXPERTS, BOOKS, FF, D // GROUP), 0, CODES), jax.random.fold_in(keys[5], 1), 0, CODES - 1).astype(jnp.int32)
    codebook = normal_values(keys[6], (LAYERS, EXPERTS, BOOKS, CODES, GROUP), 0.05, 0.29882812, ((0, 4), (1, 8)))
    scale = jnp.clip(jnp.exp(math.log(1.0) - 1.3862944 * jax.random.uniform(keys[7], (LAYERS, EXPERTS, D), jnp.float32) ** shard_levels(keys[7], (LAYERS, EXPERTS, D), ((0, 4), (1, 8)), -0.2, 0.2)), 0.25, 1.0)
    return dict(out_grad=out_grad, saved_inputs=saved_inputs, router=router, routes=routes, hidden_saved=hidden_saved, codes=codes, codebook=codebook, scale=scale)


ROUTE_SCALE = 16.0


def slot_tables(route_ids, experts, most):
    flat_ids = route_ids.reshape(-1)
    hit_table = (flat_ids[:, None] == jnp.arange(experts, dtype=jnp.int32)[None, :]).astype(jnp.int32)
    position = jnp.sum(hit_table * (jnp.cumsum(hit_table, axis=0) - 1), axis=1)
    slot_index = jnp.where(flat_ids < experts, flat_ids * most + position, -1)
    selector = (slot_index[None, :] == jnp.arange(experts * most, dtype=jnp.int32)[:, None]).astype(jnp.float32)
    tok_select = jnp.sum(selector.reshape(experts * most, route_ids.shape[0], route_ids.shape[1]), axis=2)
    return selector, tok_select


def router_back(current, score_pick, softmax_out, route_hits, router_w):
    spread = jnp.einsum("tk,tkr->tr", score_pick, route_hits, precision=lax.Precision.HIGHEST)
    weighted = jnp.sum(softmax_out * spread, axis=1, keepdims=True)
    dlogit = (ROUTE_SCALE * softmax_out * (spread - weighted)).astype(jnp.bfloat16)
    returned = lax.dot_general(dlogit, router_w, (((1,), (1,)), ((), ())), preferred_element_type=jnp.float32)
    return (current.astype(jnp.float32) + returned).astype(jnp.bfloat16)


def one_expert(items):
    codes_e, book_e, gains_e, hidden_e, rows_e, gates_e = items
    plain_part = jnp.zeros((FF, D), jnp.float32)
    for book_index in range(BOOKS):
        plain_part = plain_part + book_e[book_index][codes_e[book_index]].reshape(FF, D).astype(jnp.float32)
    weight = (plain_part * gains_e[None, :]).astype(jnp.bfloat16)
    expert_out = jnp.dot(hidden_e, weight, preferred_element_type=jnp.float32).astype(jnp.bfloat16)
    scores = jnp.sum(rows_e.astype(jnp.float32) * expert_out.astype(jnp.float32), axis=1).astype(jnp.bfloat16).astype(jnp.float32)
    slot_grad = (gates_e.astype(jnp.float32)[:, None] * rows_e.astype(jnp.float32)).astype(jnp.bfloat16)
    grad_w = jnp.dot(hidden_e.T, slot_grad, preferred_element_type=jnp.float32)
    scale_part = jnp.sum(grad_w * plain_part, axis=0)
    scaled = lax.optimization_barrier((grad_w * gains_e[None, :]).astype(jnp.bfloat16)).astype(jnp.float32)
    scaled = scaled.reshape(-1, GROUP)
    book_part = jnp.stack([jax.ops.segment_sum(scaled, codes_e[book_index].reshape(-1), num_segments=CODES) for book_index in range(BOOKS)])
    return scores, scale_part, book_part


def reference(out_grad, saved_inputs, router, routes, hidden_saved, codes, codebook, scale):
    blocks = TOKENS // TOK_DEV
    current = out_grad
    grads_list = [None] * LAYERS
    books_list = [None] * LAYERS
    scales_list = [None] * LAYERS
    for layer_index in range(LAYERS - 1, -1, -1):
        route_ids = routes[layer_index]
        selector, tok_select = jax.vmap(partial(slot_tables, experts=EXPERTS, most=MOST))(route_ids.reshape(blocks, TOK_DEV, TOP))
        logits = jnp.dot(saved_inputs[layer_index], router[layer_index], preferred_element_type=jnp.float32)
        raised = jnp.exp(logits)
        softmax_out = raised / jnp.sum(raised, axis=1, keepdims=True)
        route_hits = (route_ids[:, :, None] == jnp.arange(ROUTED, dtype=jnp.int32)[None, None, :]).astype(jnp.float32)
        chosen = jnp.sum(softmax_out[:, None, :] * route_hits, axis=2)
        gate_weight = (ROUTE_SCALE * chosen).astype(jnp.bfloat16)
        grad_blocks = current.reshape(blocks, TOK_DEV, D).astype(jnp.float32)
        outgoing = jnp.einsum("bst,btd->bsd", tok_select, grad_blocks, precision=lax.Precision.HIGHEST).astype(jnp.bfloat16)
        gate_slots = jnp.einsum("bsp,bp->bs", selector, gate_weight.astype(jnp.float32).reshape(blocks, TOK_DEV * TOP), precision=lax.Precision.HIGHEST).astype(jnp.bfloat16)
        slot_rows = outgoing.reshape(blocks, EXPERTS, MOST, D).transpose(1, 0, 2, 3).reshape(EXPERTS, RECV, D)
        gates_in = gate_slots.reshape(blocks, EXPERTS, MOST).transpose(1, 0, 2).reshape(EXPERTS, RECV)
        scores, scale_part, book_part = lax.map(one_expert, (codes[layer_index], codebook[layer_index], scale[layer_index], hidden_saved[layer_index], slot_rows, gates_in))
        returned = scores.reshape(EXPERTS, blocks, MOST).transpose(1, 0, 2).reshape(blocks, EXPERTS * MOST)
        score_pick = jnp.einsum("bs,bsp->bp", returned, selector, precision=lax.Precision.HIGHEST).reshape(TOKENS, TOP)
        current = router_back(current, score_pick, softmax_out, route_hits, router[layer_index])
        grads_list[layer_index] = current
        books_list[layer_index] = book_part
        scales_list[layer_index] = scale_part
    return jnp.stack(grads_list), jnp.stack(books_list), jnp.stack(scales_list)
```

```python
import functools

import jax
import jax.numpy as jnp
from jax import lax
from jax.experimental import pallas as pl
from jax.experimental.pallas import tpu as pltpu
from jax.sharding import PartitionSpec as P

MOST = 9
ROUTE_SCALE = 16.0
LANES = 128
LOW = 8
F32 = jnp.float32
BF16 = jnp.bfloat16


def params(mib):
    return pltpu.CompilerParams(vmem_limit_bytes=mib << 20)


def dot(a, b):
    return jnp.dot(a, b, preferred_element_type=F32)


def dot_nt(a, b):
    return lax.dot_general(a, b, (((1,), (1,)), ((), ())), preferred_element_type=F32)


def dot_tn(a, b):
    return lax.dot_general(a, b, (((0,), (0,)), ((), ())), preferred_element_type=F32)


def iota(shape, axis):
    return lax.broadcasted_iota(jnp.int32, shape, axis)


def lane_gather(table, index):
    return lax.gather(
        table,
        index[..., None],
        lax.GatherDimensionNumbers(
            offset_dims=(),
            collapsed_slice_dims=(1,),
            start_index_map=(1,),
            operand_batching_dims=(0,),
            start_indices_batching_dims=(0,),
        ),
        slice_sizes=(1, 1),
        mode=lax.GatherScatterMode.PROMISE_IN_BOUNDS,
    )


def slot_expert(rows, columns):
    first = MOST * iota((rows, columns), 1)
    row = iota((rows, columns), 0)
    return (row >= first) & (row < first + MOST)


def prepare_kernel(experts, logits_ref, routes_ref, grad_ref, probs_ref, select_ref, rows_ref):
    tokens, routed = logits_ref.shape
    top = routes_ref.shape[0]
    width = grad_ref.shape[1]
    rows = experts * MOST
    raised = jnp.exp(logits_ref[...])
    probs = raised / jnp.sum(raised, axis=1, keepdims=True)
    probs_ref[...] = probs
    expert = iota((experts, tokens), 0)
    hits = jnp.zeros((experts, tokens), F32)
    for k in range(top):
        hits = hits + (routes_ref[k : k + 1, :] == expert).astype(F32)
    hits = hits.astype(BF16)
    earlier = (iota((tokens, tokens), 0) < iota((tokens, tokens), 1)).astype(F32).astype(BF16)
    position = dot(hits, earlier).astype(BF16)
    owner = slot_expert(rows, experts)
    spread_out = owner.astype(F32).astype(BF16)
    slot_hit = dot(spread_out, hits)
    slot_position = dot(spread_out, position)
    first = jnp.sum(
        jnp.where(owner, (MOST * iota((rows, experts), 1)).astype(F32), 0.0), axis=1, keepdims=True
    )
    place = iota((rows, tokens), 0).astype(F32) - first
    select = jnp.where(
        (slot_hit > 0.5) & (jnp.abs(slot_position - place) < 0.5), 1.0, 0.0
    ).astype(BF16)
    select_ref[...] = select
    gate = (ROUTE_SCALE * probs).astype(BF16)
    slot_gate = jnp.sum(
        jnp.where(slot_expert(rows, routed), dot(select, gate), 0.0), axis=1, keepdims=True
    )
    rows_ref[:, :width] = dot(select, grad_ref[...]).astype(BF16)
    rows_ref[:, width:] = jnp.broadcast_to(slot_gate, (rows, LANES)).astype(BF16)


def decode_kernel(codes_ref, table_ref, hidden_ref, scale_ref, plain_out_ref, out_ref, weight_ref):
    step = pl.program_id(0)
    books, block, groups = codes_ref.shape
    entries = table_ref.shape[1]
    size = table_ref.shape[2]
    rows = hidden_ref.shape[0]

    @pl.when(step == 0)
    def _():
        plain_out_ref[...] = jnp.zeros_like(plain_out_ref)

    for chunk in range(groups // LANES):
        lanes = slice(chunk * LANES, (chunk + 1) * LANES)

        def decode_rows(index, carry):
            values = [[] for _ in range(size)]
            for half in range(2):
                at = pl.ds(pl.multiple_of(index * 16 + 8 * half, 8), 8)
                codes = [codes_ref[b, at, lanes] for b in range(books)]
                low = [c & (LANES - 1) for c in codes]
                part = [c >= LANES for c in codes]
                for i in range(size):
                    total = None
                    for b in range(books):
                        value = jnp.where(
                            part[b],
                            lane_gather(table_ref[b, 1, i], low[b]),
                            lane_gather(table_ref[b, 0, i], low[b]),
                        )
                        total = value if total is None else total + value
                    values[i].append(total)
            at = pl.ds(pl.multiple_of(index * 16, 16), 16)
            for i in range(size):
                weight_ref[at, i * LANES : (i + 1) * LANES] = jnp.concatenate(values[i], 0).astype(
                    BF16
                )
            return carry

        lax.fori_loop(0, block // 16, decode_rows, 0)
        product = dot(hidden_ref[...], weight_ref[...])
        for i in range(size):
            plain_out_ref[i, :, lanes] += product[:, i * LANES : (i + 1) * LANES]

    @pl.when(step == pl.num_programs(0) - 1)
    def _():
        span = size * LANES
        column = iota((span, span), 0)
        source = size * (column & (LANES - 1)) + column // LANES
        back = (source == iota((span, span), 1)).astype(F32).astype(BF16)
        for chunk in range(groups // LANES):
            lanes = slice(chunk * LANES, (chunk + 1) * LANES)
            split = jnp.concatenate(
                [plain_out_ref[i, :, lanes] * scale_ref[i : i + 1, lanes] for i in range(size)], 1
            ).astype(BF16)
            out_ref[:, chunk * span : (chunk + 1) * span] = dot(split, back).astype(BF16)


def score_kernel(out_ref, slots_ref, router_ref, score_ref):
    rows, width = out_ref.shape
    wide = router_ref.shape[1]
    extra = score_ref.shape[1] - wide
    out = out_ref[...]
    base = jnp.sum(slots_ref[:, :width].astype(F32) * out.astype(F32), axis=1, keepdims=True)
    high = base.astype(BF16)
    rest = base - high.astype(F32)
    middle = rest.astype(BF16)
    low = (rest - middle.astype(F32)).astype(BF16)
    score_ref[:, :wide] = dot(out, router_ref[...]).astype(BF16)
    column = iota((rows, extra), 1)
    score_ref[:, wide:] = jnp.where(
        column == 0,
        high.astype(F32),
        jnp.where(
            column == 1, middle.astype(F32), jnp.where(column == 2, low.astype(F32), 0.0)
        ),
    ).astype(BF16)


def chain_kernel(scores_ref, later_ref, probs_ref, select_ref, own_ref, send_ref, picked_ref):
    rows = scores_ref.shape[0]
    tokens, wide = later_ref.shape
    routed = probs_ref.shape[1]
    later = later_ref[...]
    select = select_ref[...]
    picked = dot(select, later)
    picked_ref[...] = picked.astype(BF16)
    score = jnp.sum(picked * scores_ref[:, :wide].astype(F32), axis=1, keepdims=True) + jnp.sum(
        scores_ref[:, wide:].astype(F32), axis=1, keepdims=True
    )
    score = score.astype(BF16).astype(F32)
    placed = jnp.where(slot_expert(rows, routed), score, 0.0).astype(BF16)
    spread = dot_tn(select, placed)
    probs = probs_ref[...]
    weighted = jnp.sum(probs * spread, axis=1, keepdims=True)
    own = (ROUTE_SCALE * probs * (spread - weighted)).astype(BF16)
    own_ref[...] = own
    put = (iota((routed, wide), 0) == iota((routed, wide), 1)).astype(F32).astype(BF16)
    shift = (iota((wide, wide), 0) + routed == iota((wide, wide), 1)).astype(F32).astype(BF16)
    send_ref[...] = (dot(own, put) + dot(later, shift)).astype(BF16)


def add_layers(current, later, router, routed):
    count = later.shape[1] // routed
    column = iota(later.shape, 1)
    for s in range(count - 1, -1, -1):
        part = jnp.where(
            (column >= s * routed) & (column < (s + 1) * routed), later.astype(F32), 0.0
        ).astype(BF16)
        current = (current.astype(F32) + dot_nt(part, router)).astype(BF16)
    return current


def finish_kernel(grad_ref, later_ref, own_ref, routers_ref, router_ref, result_ref):
    current = add_layers(grad_ref[...], later_ref[...], routers_ref[...], own_ref.shape[1])
    added = dot_nt(own_ref[...], router_ref[...])
    result_ref[...] = (current.astype(F32) + added).astype(BF16)


def slots_kernel(
    routed, slots_ref, gates_ref, later_ref, routers_ref, plain_out_ref, split_ref, scale_grad_ref
):
    span = slots_ref.shape[1]
    size = span // LANES
    current = add_layers(slots_ref[...], later_ref[...], routers_ref[...], routed)
    gate = gates_ref[:, :1].astype(F32)
    grad = (gate * current.astype(F32)).astype(BF16)
    column = iota((span, span), 1)
    source = size * (column & (LANES - 1)) + column // LANES
    split = dot(grad, (source == iota((span, span), 0)).astype(F32).astype(BF16))
    for i in range(size):
        part = split[:, i * LANES : (i + 1) * LANES]
        split_ref[i] = part.astype(BF16)
        scale_grad_ref[i : i + 1, :] = jnp.sum(part * plain_out_ref[i], axis=0, keepdims=True)


def book_kernel(
    unroll, hidden_ref, slots_ref, scale_ref, codes_ref, out_ref, grad_ref, high_ref, low_ref
):
    books, block, groups = codes_ref.shape
    size = slots_ref.shape[0]
    high_count = out_ref.shape[1]
    chunks = groups // LANES

    @pl.when(pl.program_id(0) == 0)
    def _():
        out_ref[...] = jnp.zeros_like(out_ref)

    hidden = hidden_ref[...]
    for i in range(size):
        grad = dot(hidden, slots_ref[i]) * scale_ref[i : i + 1, :]
        for c in range(chunks):
            grad_ref[c, pl.ds(i, block, stride=size), :] = grad[:, c * LANES : (c + 1) * LANES]
    for b in range(books):
        codes = codes_ref[b]
        high_ref[b] = (codes >> 3).astype(F32)
        low_ref[b] = (codes & (LOW - 1)).astype(F32)
    row = iota((16, groups), 0)
    high_rows = [(row + 16 * k).astype(F32).astype(BF16) for k in range(high_count // 16)]
    low_rows = [((row >> 3) + 2 * k).astype(F32).astype(BF16) for k in range(LOW // 2)]
    one = jnp.ones((16, groups), BF16)
    zero = jnp.zeros((16, groups), BF16)

    def add_rows(index, totals):
        totals = list(totals)
        for pair in range(unroll // 2):
            left = [[] for _ in range(books)]
            right = [[] for _ in range(books)]
            for member in range(2):
                f = index * unroll + pair * 2 + member
                at = pl.ds(pl.multiple_of(f * size, size), size)
                values = jnp.concatenate([grad_ref[c, at, :] for c in range(chunks)], 1)
                values = jnp.concatenate([values, values], 0).astype(BF16)
                for b in range(books):
                    high = jnp.broadcast_to(high_ref[b, pl.ds(f, 1), :], (16, groups)).astype(BF16)
                    low = jnp.broadcast_to(low_ref[b, pl.ds(f, 1), :], (16, groups)).astype(BF16)
                    left[b].append(
                        jnp.concatenate([jnp.where(high == r, one, zero) for r in high_rows], 0)
                    )
                    right[b].append(
                        jnp.concatenate([jnp.where(low == r, values, zero) for r in low_rows], 0)
                    )
            for b in range(books):
                totals[b] = totals[b] + dot_nt(
                    jnp.concatenate(left[b], 1), jnp.concatenate(right[b], 1)
                )
        return tuple(totals)

    start = tuple(jnp.zeros(out_ref.shape[1:], F32) for _ in range(books))
    totals = lax.fori_loop(0, block // unroll, add_rows, start)
    for b in range(books):
        out_ref[b] += totals[b]


def whole(shape):
    return pl.BlockSpec(shape, lambda s: (0,) * len(shape))


def exchange(value):
    return lax.all_to_all(value, "expert", split_axis=0, concat_axis=0, tiled=True)


def on_device(out_grad, saved_inputs, router, routes, hidden_saved, codes, codebook, scale):
    experts = lax.axis_size("expert")
    layers = lax.axis_size("pipe")
    tokens, width = out_grad.shape
    routed = router.shape[2]
    codes = codes[0, 0]
    codebook = codebook[0, 0]
    hidden = hidden_saved[0, 0]
    router = router[0]
    inner = hidden.shape[1]
    books, _, groups = codes.shape
    entries, size = codebook.shape[1:]
    rows = experts * MOST
    later_count = layers - 1
    wide = later_count * routed
    score_wide = -(-(wide + 3) // LANES) * LANES
    scale_split = scale[0, 0].reshape(groups, size).T

    share = width // experts
    own_share = lax.dynamic_slice_in_dim(router, lax.axis_index("expert") * share, share, 0)
    shares = [
        lax.ppermute(own_share, "pipe", [(p, p - s) for p in range(s, layers)])
        for s in range(1, layers)
    ]
    routers = lax.all_gather(jnp.concatenate(shares, 1), "expert", axis=0, tiled=True)

    logits = dot(saved_inputs[0], router)
    probs, select, outgoing = pl.pallas_call(
        functools.partial(prepare_kernel, experts),
        out_shape=(
            jax.ShapeDtypeStruct((tokens, routed), F32),
            jax.ShapeDtypeStruct((rows, tokens), BF16),
            jax.ShapeDtypeStruct((rows, width + LANES), BF16),
        ),
        compiler_params=params(32),
        name="prepare",
    )(logits, routes[0].T, out_grad)
    slots = exchange(outgoing.reshape(experts, MOST, width + LANES)).reshape(rows, width + LANES)

    halves = entries // LANES
    table = codebook.astype(F32).transpose(0, 2, 1).reshape(books, size, halves, LANES)
    table = jnp.broadcast_to(
        table.transpose(0, 2, 1, 3)[:, :, :, None, :], (books, halves, size, 8, LANES)
    )
    block = 256
    plain_out, expert_out = pl.pallas_call(
        decode_kernel,
        grid=(inner // block,),
        in_specs=[
            pl.BlockSpec((books, block, groups), lambda s: (0, s, 0)),
            whole((books, halves, size, 8, LANES)),
            pl.BlockSpec((rows, block), lambda s: (0, s)),
            whole((size, groups)),
        ],
        out_specs=[whole((size, rows, groups)), whole((rows, width))],
        out_shape=[
            jax.ShapeDtypeStruct((size, rows, groups), F32),
            jax.ShapeDtypeStruct((rows, width), BF16),
        ],
        scratch_shapes=[pltpu.VMEM((block, size * LANES), BF16)],
        compiler_params=params(48),
        cost_estimate=pl.CostEstimate(
            flops=50_000_000_000, bytes_accessed=10_000_000, transcendentals=0
        ),
        name="decode",
    )(codes, table, hidden, scale_split)

    scores = pl.pallas_call(
        score_kernel,
        out_shape=jax.ShapeDtypeStruct((rows, score_wide), BF16),
        compiler_params=params(48),
        name="scores",
    )(expert_out, slots, routers)
    scores = exchange(scores.reshape(experts, MOST, score_wide)).reshape(rows, score_wide)

    chain = pl.pallas_call(
        chain_kernel,
        out_shape=(
            jax.ShapeDtypeStruct((tokens, routed), BF16),
            jax.ShapeDtypeStruct((tokens, wide), BF16),
            jax.ShapeDtypeStruct((rows, wide), BF16),
        ),
        compiler_params=params(32),
        name="chain",
    )
    later = jnp.zeros((tokens, wide), BF16)
    for step in range(layers):
        own, send, picked = chain(scores, later, probs, select)
        if step + 1 < layers:
            later = lax.ppermute(send, "pipe", [(p, p - 1) for p in range(1, layers)])

    slot_later = exchange(picked.reshape(experts, MOST, wide)).reshape(rows, wide)

    span = size * LANES
    result = pl.pallas_call(
        finish_kernel,
        grid=(width // span,),
        in_specs=[
            pl.BlockSpec((tokens, span), lambda s: (0, s)),
            whole((tokens, wide)),
            whole((tokens, routed)),
            pl.BlockSpec((span, wide), lambda s: (s, 0)),
            pl.BlockSpec((span, routed), lambda s: (s, 0)),
        ],
        out_specs=pl.BlockSpec((tokens, span), lambda s: (0, s)),
        out_shape=jax.ShapeDtypeStruct((tokens, width), BF16),
        compiler_params=params(32),
        name="finish",
    )(out_grad, later, own, routers, router)

    slot_split, scale_grad = pl.pallas_call(
        functools.partial(slots_kernel, routed),
        grid=(width // span,),
        in_specs=[
            pl.BlockSpec((rows, span), lambda s: (0, s)),
            pl.BlockSpec((rows, LANES), lambda s: (0, width // LANES)),
            whole((rows, wide)),
            pl.BlockSpec((span, wide), lambda s: (s, 0)),
            pl.BlockSpec((size, rows, LANES), lambda s: (0, 0, s)),
        ],
        out_specs=[
            pl.BlockSpec((size, rows, LANES), lambda s: (0, 0, s)),
            pl.BlockSpec((size, LANES), lambda s: (0, s)),
        ],
        out_shape=[
            jax.ShapeDtypeStruct((size, rows, groups), BF16),
            jax.ShapeDtypeStruct((size, groups), F32),
        ],
        compiler_params=params(48),
        name="slot_grads",
    )(slots, slots, slot_later, routers, plain_out)

    block = 64
    unroll = 16
    high_count = entries // LOW
    book_grad = pl.pallas_call(
        functools.partial(book_kernel, unroll),
        grid=(inner // block,),
        in_specs=[
            pl.BlockSpec((block, rows), lambda s: (s, 0)),
            whole((size, rows, groups)),
            whole((size, groups)),
            pl.BlockSpec((books, block, groups), lambda s: (0, s, 0)),
        ],
        out_specs=whole((books, high_count, LOW * size)),
        out_shape=jax.ShapeDtypeStruct((books, high_count, LOW * size), F32),
        scratch_shapes=[
            pltpu.VMEM((groups // LANES, block * size, LANES), F32),
            pltpu.VMEM((books, block, groups), F32),
            pltpu.VMEM((books, block, groups), F32),
        ],
        compiler_params=params(48),
        name="book_grads",
    )(hidden.T, slot_split, scale_split, codes)

    book_grad = book_grad.reshape(books, entries, size)
    scale_grad = scale_grad.T.reshape(width)
    return (result[None], book_grad[None, None], scale_grad[None, None])


def solution(mesh):
    placed = (
        P("expert", None),
        P("pipe", "expert", None),
        P("pipe", None, None),
        P("pipe", "expert", None),
        P("pipe", "expert", None, None),
        P("pipe", "expert", None, None, None),
        P("pipe", "expert", None, None, None),
        P("pipe", "expert", None),
    )
    return jax.shard_map(
        on_device,
        mesh=mesh,
        in_specs=placed,
        out_specs=(
            P("pipe", "expert", None),
            P("pipe", "expert", None, None, None),
            P("pipe", "expert", None),
        ),
        check_vma=False,
    )
```

```python
import functools
import math

import jax
import jax.numpy as jnp
from jax import lax
from jax.experimental import pallas as pl
from jax.experimental.pallas import tpu as pltpu
from jax.sharding import PartitionSpec as P

MOST = 9
SLOT = 16
ROUTE_SCALE = 16.0
LANES = 128
WIDE = 256
LOW = 8
F32 = jnp.float32
BF16 = jnp.bfloat16


def params(mib):
    return pltpu.CompilerParams(vmem_limit_bytes=mib << 20)


def dot(a, b):
    return jnp.dot(a, b, preferred_element_type=F32)


def dot_nt(a, b):
    return lax.dot_general(a, b, (((1,), (1,)), ((), ())), preferred_element_type=F32)


def dot_tn(a, b):
    return lax.dot_general(a, b, (((0,), (0,)), ((), ())), preferred_element_type=F32)


def iota(shape, axis):
    return lax.broadcasted_iota(jnp.int32, shape, axis)


def lane_gather(table, index):
    return lax.gather(
        table,
        index[..., None],
        lax.GatherDimensionNumbers(
            offset_dims=(),
            collapsed_slice_dims=(1,),
            start_index_map=(1,),
            operand_batching_dims=(0,),
            start_indices_batching_dims=(0,),
        ),
        slice_sizes=(1, 1),
        mode=lax.GatherScatterMode.PROMISE_IN_BOUNDS,
    )


def slot_expert(rows, columns):
    return iota((rows, columns), 0) // SLOT == iota((rows, columns), 1)


def one_hot(mask):
    return mask.astype(F32).astype(BF16)


def prepare_kernel(logits_ref, routes_ref, grad_ref, probs_ref, select_ref, rows_ref):
    tokens, routed = logits_ref.shape
    top = routes_ref.shape[0]
    width = grad_ref.shape[1]
    rows = rows_ref.shape[0]
    experts = rows // SLOT
    raised = jnp.exp(logits_ref[...])
    probs = raised / jnp.sum(raised, axis=1, keepdims=True)
    probs_ref[...] = probs
    expert = iota((experts, tokens), 0)
    hits = jnp.zeros((experts, tokens), F32)
    for k in range(top):
        hits = hits + (routes_ref[k : k + 1, :] == expert).astype(F32)
    hits = hits.astype(BF16)
    earlier = one_hot(iota((tokens, tokens), 0) < iota((tokens, tokens), 1))
    position = dot(hits, earlier).astype(BF16)
    owner = one_hot(slot_expert(rows, experts))
    slot_hit = dot(owner, hits)
    slot_position = dot(owner, position)
    place = (iota((rows, tokens), 0) % SLOT).astype(F32)
    select = one_hot(
        (slot_hit > 0.5) & (jnp.abs(slot_position - place) < 0.5) & (place < MOST - 0.5)
    )
    select_ref[...] = select
    gate = (ROUTE_SCALE * probs).astype(BF16)
    slot_gate = jnp.sum(
        jnp.where(slot_expert(rows, routed), dot(select, gate), 0.0), axis=1, keepdims=True
    )
    rows_ref[:, :width] = dot(select, grad_ref[...]).astype(BF16)
    rows_ref[:, width:] = jnp.broadcast_to(slot_gate, (rows, LANES)).astype(BF16)


def decode_kernel(first, last, codes_ref, table_ref, hidden_ref, *rest):
    if not first:
        before_ref, scale_ref, *rest = rest
    plain_out_ref, *rest = rest
    weight_ref = rest[-1]
    step = pl.program_id(0)
    books, block, groups = codes_ref.shape
    entries = table_ref.shape[1]
    size = table_ref.shape[2]

    @pl.when(step == 0)
    def _():
        plain_out_ref[...] = jnp.zeros_like(plain_out_ref) if first else before_ref[...]

    for chunk in range(groups // LANES):
        lanes = slice(chunk * LANES, (chunk + 1) * LANES)

        def decode_rows(index, carry):
            values = [[] for _ in range(size)]
            for half in range(2):
                at = pl.ds(pl.multiple_of(index * 16 + 8 * half, 8), 8)
                codes = [codes_ref[b, at, lanes] for b in range(books)]
                low = [c & (LANES - 1) for c in codes]
                part = [c >= LANES for c in codes]
                for i in range(size):
                    total = None
                    for b in range(books):
                        value = jnp.where(
                            part[b],
                            lane_gather(table_ref[b, 1, i], low[b]),
                            lane_gather(table_ref[b, 0, i], low[b]),
                        )
                        total = value if total is None else total + value
                    values[i].append(total)
            at = pl.ds(pl.multiple_of(index * 16, 16), 16)
            for i in range(size):
                weight_ref[at, i * LANES : (i + 1) * LANES] = jnp.concatenate(values[i], 0).astype(
                    BF16
                )
            return carry

        lax.fori_loop(0, block // 16, decode_rows, 0)
        product = dot(hidden_ref[...], weight_ref[...])
        for i in range(size):
            plain_out_ref[i, :, lanes] += product[:, i * LANES : (i + 1) * LANES]

    if not last:
        return
    out_ref = rest[0]

    @pl.when(step == pl.num_programs(0) - 1)
    def _():
        span = size * LANES
        column = iota((span, span), 0)
        source = size * (column & (LANES - 1)) + column // LANES
        back = (source == iota((span, span), 1)).astype(F32).astype(BF16)
        for chunk in range(groups // LANES):
            lanes = slice(chunk * LANES, (chunk + 1) * LANES)
            split = jnp.concatenate(
                [plain_out_ref[i, :, lanes] * scale_ref[i : i + 1, lanes] for i in range(size)], 1
            ).astype(BF16)
            out_ref[:, chunk * span : (chunk + 1) * span] = dot(split, back).astype(BF16)


def score_kernel(twist_ref, out_ref, slots_ref, near_ref, far_ref, score_ref, total_ref):
    i, j = pl.program_id(0), pl.program_id(1)
    rows = out_ref.shape[0]
    later_count, routed = near_ref.shape[1:3]

    @pl.when((i == 0) & (j == 0))
    def _():
        total_ref[...] = jnp.zeros_like(total_ref)

    out = out_ref[...]
    base = jnp.sum(slots_ref[...].astype(F32) * out.astype(F32), axis=1, keepdims=True)
    total_ref[:, later_count * WIDE :] += jnp.broadcast_to(base, (rows, LANES))

    def add(router_ref):
        for s in range(later_count):
            total_ref[:, s * WIDE : s * WIDE + routed] += dot_nt(out, router_ref[0, s])

    @pl.when(j == 0)
    def _():
        add(near_ref)

    @pl.when(j == 1)
    def _():
        add(far_ref)

    @pl.when((i == pl.num_programs(0) - 1) & (j == 1))
    def _():
        score_ref[:, : later_count * WIDE] = total_ref[:, : later_count * WIDE].astype(BF16)
        base = total_ref[:, later_count * WIDE :]
        high = base.astype(BF16).astype(F32)
        middle = (base - high).astype(BF16).astype(F32)
        low = base - high - middle
        column = iota((rows, LANES), 1)
        score_ref[:, later_count * WIDE :] = jnp.where(
            column == 0,
            high,
            jnp.where(column == 1, middle, jnp.where(column == 2, low, 0.0)),
        ).astype(BF16)


def chain_kernel(scores_ref, later_ref, probs_ref, select_ref, own_ref, send_ref, picked_ref):
    rows = scores_ref.shape[0]
    tokens, wide = later_ref.shape
    routed = probs_ref.shape[1]
    later = later_ref[...]
    select = select_ref[...]
    picked = dot(select, later)
    picked_ref[...] = picked.astype(BF16)
    score = jnp.sum(picked * scores_ref[:, :wide].astype(F32), axis=1, keepdims=True) + jnp.sum(
        scores_ref[:, wide:].astype(F32), axis=1, keepdims=True
    )
    score = score.astype(BF16).astype(F32)
    placed = jnp.where(slot_expert(rows, routed), score, 0.0).astype(BF16)
    spread = dot_tn(select, placed)
    probs = probs_ref[...]
    weighted = jnp.sum(probs * spread, axis=1, keepdims=True)
    own = (ROUTE_SCALE * probs * (spread - weighted)).astype(BF16)
    own_ref[...] = own
    send_ref[:, :WIDE] = jnp.zeros((tokens, WIDE), BF16)
    send_ref[:, :routed] = own
    send_ref[:, WIDE:] = later[:, : wide - WIDE]


def add_layers(current, later_ref, router_ref):
    later_count, routed = router_ref.shape[1:3]
    for s in range(later_count - 1, -1, -1):
        part = later_ref[:, s * WIDE : s * WIDE + routed]
        current = (current.astype(F32) + dot(part, router_ref[0, s])).astype(BF16)
    return current


def finish_kernel(
    twist_ref, grad_ref, later_ref, own_ref, router_ref, near_ref, far_ref, result_ref
):
    def finish(routers_ref):
        current = add_layers(grad_ref[...], later_ref, routers_ref)
        result_ref[...] = (current.astype(F32) + dot(own_ref[...], router_ref[...])).astype(BF16)

    @pl.when(pl.program_id(1) == 0)
    def _():
        finish(near_ref)

    @pl.when(pl.program_id(1) == 1)
    def _():
        finish(far_ref)


def slots_kernel(
    twist_ref, slots_ref, gates_ref, later_ref, near_ref, far_ref, plain_out_ref, split_ref,
    scale_grad_ref, grad_ref
):
    i, j = pl.program_id(0), pl.program_id(1)
    part_width = slots_ref.shape[1]
    size = plain_out_ref.shape[0]
    groups = plain_out_ref.shape[2]
    span = size * LANES
    at = pl.ds(pl.multiple_of((twist_ref[0] ^ (2 * i + j)) * part_width, LANES), part_width)
    gate = gates_ref[:, :1].astype(F32)

    def put(routers_ref):
        current = add_layers(slots_ref[...], later_ref, routers_ref)
        grad_ref[:, at] = (gate * current.astype(F32)).astype(BF16)

    @pl.when(j == 0)
    def _():
        put(near_ref)

    @pl.when(j == 1)
    def _():
        put(far_ref)

    @pl.when((i == pl.num_programs(0) - 1) & (j == 1))
    def _():
        column = iota((span, span), 1)
        source = size * (column & (LANES - 1)) + column // LANES
        order = one_hot(source == iota((span, span), 0))
        for chunk in range(groups // LANES):
            lanes = slice(chunk * LANES, (chunk + 1) * LANES)
            split = dot(grad_ref[:, chunk * span : (chunk + 1) * span], order)
            for i in range(size):
                part = split[:, i * LANES : (i + 1) * LANES]
                split_ref[i, :, lanes] = part.astype(BF16)
                scale_grad_ref[i : i + 1, lanes] = jnp.sum(
                    part * plain_out_ref[i, :, lanes], axis=0, keepdims=True
                )


def book_kernel(
    unroll, hidden_ref, slots_ref, scale_ref, codes_ref, out_ref, grad_ref, high_ref, low_ref
):
    books, block, groups = codes_ref.shape
    size = slots_ref.shape[0]
    high_count = out_ref.shape[1]
    chunks = groups // LANES

    @pl.when(pl.program_id(0) == 0)
    def _():
        out_ref[...] = jnp.zeros_like(out_ref)

    hidden = hidden_ref[...]
    for i in range(size):
        grad = dot_tn(hidden, slots_ref[i]) * scale_ref[i : i + 1, :]
        for c in range(chunks):
            grad_ref[c, pl.ds(i, block, stride=size), :] = grad[:, c * LANES : (c + 1) * LANES]
    for b in range(books):
        codes = codes_ref[b]
        high_ref[b] = (codes >> 3).astype(F32)
        low_ref[b] = (codes & (LOW - 1)).astype(F32)
    row = iota((16, groups), 0)
    high_rows = [(row + 16 * k).astype(F32).astype(BF16) for k in range(high_count // 16)]
    low_rows = [((row >> 3) + 2 * k).astype(F32).astype(BF16) for k in range(LOW // 2)]
    one = jnp.ones((16, groups), BF16)
    zero = jnp.zeros((16, groups), BF16)

    def add_rows(index, totals):
        totals = list(totals)
        for pair in range(unroll // 2):
            left = [[] for _ in range(books)]
            right = [[] for _ in range(books)]
            for member in range(2):
                f = index * unroll + pair * 2 + member
                at = pl.ds(pl.multiple_of(f * size, size), size)
                values = jnp.concatenate([grad_ref[c, at, :] for c in range(chunks)], 1)
                values = jnp.concatenate([values, values], 0).astype(BF16)
                for b in range(books):
                    high = jnp.broadcast_to(high_ref[b, pl.ds(f, 1), :], (16, groups)).astype(BF16)
                    low = jnp.broadcast_to(low_ref[b, pl.ds(f, 1), :], (16, groups)).astype(BF16)
                    left[b].append(
                        jnp.concatenate([jnp.where(high == r, one, zero) for r in high_rows], 0)
                    )
                    right[b].append(
                        jnp.concatenate([jnp.where(low == r, values, zero) for r in low_rows], 0)
                    )
            for b in range(books):
                totals[b] = totals[b] + dot_nt(
                    jnp.concatenate(left[b], 1), jnp.concatenate(right[b], 1)
                )
        return tuple(totals)

    start = tuple(jnp.zeros(out_ref.shape[1:], F32) for _ in range(books))
    totals = lax.fori_loop(0, block // unroll, add_rows, start)
    for b in range(books):
        out_ref[b] += totals[b]


def whole(shape):
    return pl.BlockSpec(shape, lambda *_: (0,) * len(shape))


def exchange(value):
    return lax.all_to_all(value, "expert", split_axis=0, concat_axis=0, tiled=True)


def swap(value, distance):
    count = lax.axis_size("expert")
    return lax.ppermute(value, "expert", [(i, i ^ distance) for i in range(count)])


def gather_exchange(shares):
    count = lax.axis_size("expert")
    return jnp.stack([shares] + [swap(shares, d) for d in range(2, count, 2)])


def on_device(out_grad, saved_inputs, router, routes, hidden_saved, codes, codebook, scale):
    experts = lax.axis_size("expert")
    layers = lax.axis_size("pipe")
    place = lax.axis_index("expert")
    tokens, width = out_grad.shape
    routed = router.shape[2]
    codes = codes[0, 0]
    codebook = codebook[0, 0]
    hidden = hidden_saved[0, 0]
    inner = hidden.shape[1]
    books, _, groups = codes.shape
    entries, size = codebook.shape[1:]
    rows = experts * SLOT
    later_count = layers - 1
    wide = later_count * WIDE
    grow = max(1, rows // 128)
    router_t = router[0].T
    scale_split = scale[0, 0].reshape(groups, size).T
    hidden = jnp.pad(hidden.reshape(experts, MOST, inner), ((0, 0), (0, SLOT - MOST), (0, 0)))
    hidden = hidden.reshape(rows, inner)

    parts = math.gcd(width // LANES, experts)
    direct = parts == experts
    sharers = experts // parts
    part_width = width // parts
    share_rows = routed // sharers
    own_share = lax.dynamic_slice(
        router_t,
        ((place % sharers) * share_rows, (place // sharers) * part_width),
        (share_rows, part_width),
    )
    shares = jnp.stack(
        [
            lax.ppermute(own_share, "pipe", [(p, p - s) for p in range(s, layers)])
            for s in range(1, layers)
        ]
    )
    twist = jnp.full((1,), place if direct else 0, jnp.int32)

    logits = dot(saved_inputs[0], router[0])
    probs, select, outgoing = pl.pallas_call(
        prepare_kernel,
        out_shape=(
            jax.ShapeDtypeStruct((tokens, routed), F32),
            jax.ShapeDtypeStruct((rows, tokens), BF16),
            jax.ShapeDtypeStruct((rows, width + LANES), BF16),
        ),
        compiler_params=params(12 + 6 * grow),
        name="prepare",
    )(logits, routes[0].T, out_grad)
    slots = exchange(outgoing)
    hidden, outgoing = lax.optimization_barrier((hidden, outgoing))

    halves = entries // LANES
    table = codebook.astype(F32).transpose(0, 2, 1).reshape(books, size, halves, LANES)
    table = jnp.broadcast_to(
        table.transpose(0, 2, 1, 3)[:, :, :, None, :], (books, halves, size, 8, LANES)
    )
    block = 128

    def decode(start, count, before):
        first = before is None
        last = start + count == inner // block
        more = [] if first else [before, scale_split]
        return pl.pallas_call(
            functools.partial(decode_kernel, first, last),
            grid=(count,),
            in_specs=[
                pl.BlockSpec((books, block, groups), lambda s: (0, s + start, 0)),
                whole((books, halves, size, 8, LANES)),
                pl.BlockSpec((rows, block), lambda s: (0, s + start)),
            ]
            + [whole(m.shape) for m in more],
            out_specs=[whole((size, rows, groups))] + [whole((rows, width))] * last,
            out_shape=[jax.ShapeDtypeStruct((size, rows, groups), F32)]
            + [jax.ShapeDtypeStruct((rows, width), BF16)] * last,
            scratch_shapes=[pltpu.VMEM((block, size * LANES), BF16)],
            input_output_aliases={} if first else {3: 0},
            compiler_params=params(60),
            cost_estimate=pl.CostEstimate(
                flops=count * 10_000_000_000, bytes_accessed=2_000_000, transcendentals=0
            ),
            name="decode",
        )(codes, table, hidden, *more)

    blocks = inner // block
    first_part, second_part = blocks // 3, blocks // 2
    (plain_out,) = decode(0, first_part, None)
    plain_out, shares = lax.optimization_barrier((plain_out, shares))
    near = gather_exchange(shares) if direct else None
    (plain_out,) = decode(first_part, second_part, plain_out)
    if direct:
        plain_out, near, slots = lax.optimization_barrier((plain_out, near, slots))
        far = swap(near, 1)
    else:
        routers = lax.all_gather(shares, "expert", axis=0, tiled=False)
        routers = routers.reshape(parts, sharers, later_count, share_rows, part_width)
        routers = routers.transpose(0, 2, 1, 3, 4)
        routers = routers.reshape(parts, later_count, routed, part_width)
        near, far = routers[0::2], routers[1::2]
    done = first_part + second_part
    plain_out, expert_out = decode(done, blocks - done, plain_out)

    grid = (parts // 2, 2)

    def columns(height):
        return pl.BlockSpec((height, part_width), lambda i, j, t: (0, t[0] ^ (2 * i + j)))

    router_spec = pl.BlockSpec(
        (1, later_count, routed, part_width), lambda i, j, t: (i, 0, 0, 0)
    )

    def by_columns(kernel, in_specs, out_specs, out_shape, scratch, mib, name):
        return pl.pallas_call(
            kernel,
            grid_spec=pltpu.PrefetchScalarGridSpec(
                num_scalar_prefetch=1,
                grid=grid,
                in_specs=in_specs,
                out_specs=out_specs,
                scratch_shapes=scratch,
            ),
            out_shape=out_shape,
            compiler_params=params(min(56, mib)),
            name=name,
        )

    scores = by_columns(
        score_kernel,
        [columns(rows), columns(rows), router_spec, router_spec],
        whole((rows, wide + LANES)),
        jax.ShapeDtypeStruct((rows, wide + LANES), BF16),
        [pltpu.VMEM((rows, wide + LANES), F32)],
        8 + 4 * grow,
        "scores",
    )(twist, expert_out, slots, near, far)
    scores = exchange(scores)

    chain = pl.pallas_call(
        chain_kernel,
        out_shape=(
            jax.ShapeDtypeStruct((tokens, routed), BF16),
            jax.ShapeDtypeStruct((tokens, wide), BF16),
            jax.ShapeDtypeStruct((rows, wide), BF16),
        ),
        compiler_params=params(8 + 4 * grow),
        name="chain",
    )
    later = jnp.zeros((tokens, wide), BF16)
    for step in range(layers):
        own, send, picked = chain(scores, later, probs, select)
        if step + 1 < layers:
            later = lax.ppermute(send, "pipe", [(p, p - 1) for p in range(1, layers)])

    slot_later = exchange(picked)

    result = by_columns(
        finish_kernel,
        [
            columns(tokens),
            whole((tokens, wide)),
            whole((tokens, routed)),
            columns(routed),
            router_spec,
            router_spec,
        ],
        columns(tokens),
        jax.ShapeDtypeStruct((tokens, width), BF16),
        [],
        12,
        "finish",
    )(twist, out_grad, later, own, router_t, near, far)

    slot_split, scale_grad = by_columns(
        slots_kernel,
        [
            columns(rows),
            pl.BlockSpec((rows, LANES), lambda *_: (0, width // LANES)),
            whole((rows, wide)),
            router_spec,
            router_spec,
            whole((size, rows, groups)),
        ],
        [whole((size, rows, groups)), whole((size, groups))],
        [
            jax.ShapeDtypeStruct((size, rows, groups), BF16),
            jax.ShapeDtypeStruct((size, groups), F32),
        ],
        [pltpu.VMEM((rows, width), BF16)],
        12 + 12 * grow,
        "slot_grads",
    )(twist, slots, slots, slot_later, near, far, plain_out)

    block = 128
    unroll = 16
    high_count = entries // LOW
    book_grad = pl.pallas_call(
        functools.partial(book_kernel, unroll),
        grid=(inner // block,),
        in_specs=[
            pl.BlockSpec((rows, block), lambda s: (0, s)),
            whole((size, rows, groups)),
            whole((size, groups)),
            pl.BlockSpec((books, block, groups), lambda s: (0, s, 0)),
        ],
        out_specs=whole((books, high_count, LOW * size)),
        out_shape=jax.ShapeDtypeStruct((books, high_count, LOW * size), F32),
        scratch_shapes=[
            pltpu.VMEM((groups // LANES, block * size, LANES), F32),
            pltpu.VMEM((books, block, groups), F32),
            pltpu.VMEM((books, block, groups), F32),
        ],
        compiler_params=params(20 + 6 * grow),
        name="book_grads",
    )(hidden, slot_split, scale_split, codes)

    book_grad = book_grad.reshape(books, entries, size)
    scale_grad = scale_grad.T.reshape(width)
    return (result[None], book_grad[None, None], scale_grad[None, None])


def solution(mesh):
    placed = (
        P("expert", None),
        P("pipe", "expert", None),
        P("pipe", None, None),
        P("pipe", "expert", None),
        P("pipe", "expert", None, None),
        P("pipe", "expert", None, None, None),
        P("pipe", "expert", None, None, None),
        P("pipe", "expert", None),
    )
    return jax.shard_map(
        on_device,
        mesh=mesh,
        in_specs=placed,
        out_specs=(
            P("pipe", "expert", None),
            P("pipe", "expert", None, None, None),
            P("pipe", "expert", None),
        ),
        check_vma=False,
    )
```

```python
import functools
import math

import jax
import jax.numpy as jnp
from jax import lax
from jax.experimental import pallas as pl
from jax.experimental.pallas import tpu as pltpu
from jax.sharding import PartitionSpec as P

MOST = 9
SLOT = 16
ROUTE_SCALE = 16.0
LANES = 128
WIDE = 256
LOW = 6
HIGH = 48
F32 = jnp.float32
BF16 = jnp.bfloat16
I16 = jnp.int16


def params(mib):
    return pltpu.CompilerParams(vmem_limit_bytes=mib << 20)


def dot(a, b):
    return jnp.dot(a, b, preferred_element_type=F32)


def dot_nt(a, b):
    return lax.dot_general(a, b, (((1,), (1,)), ((), ())), preferred_element_type=F32)


def dot_tn(a, b):
    return lax.dot_general(a, b, (((0,), (0,)), ((), ())), preferred_element_type=F32)


def iota(shape, axis):
    return lax.broadcasted_iota(jnp.int32, shape, axis)


def lane_gather(table, index):
    return lax.gather(
        table,
        index[..., None],
        lax.GatherDimensionNumbers(
            offset_dims=(),
            collapsed_slice_dims=(1,),
            start_index_map=(1,),
            operand_batching_dims=(0,),
            start_indices_batching_dims=(0,),
        ),
        slice_sizes=(1, 1),
        mode=lax.GatherScatterMode.PROMISE_IN_BOUNDS,
    )


def slot_expert(rows, columns):
    return iota((rows, columns), 0) // SLOT == iota((rows, columns), 1)


def one_hot(mask):
    return mask.astype(F32).astype(BF16)


def prepare_kernel(logits_ref, routes_ref, grad_ref, probs_ref, select_ref, rows_ref):
    tokens, routed = logits_ref.shape
    top = routes_ref.shape[0]
    width = grad_ref.shape[1]
    rows = rows_ref.shape[0]
    experts = rows // SLOT
    raised = jnp.exp(logits_ref[...])
    probs = raised / jnp.sum(raised, axis=1, keepdims=True)
    probs_ref[...] = probs
    expert = iota((experts, tokens), 0)
    hits = jnp.zeros((experts, tokens), F32)
    for k in range(top):
        hits = hits + (routes_ref[k : k + 1, :] == expert).astype(F32)
    hits = hits.astype(BF16)
    earlier = one_hot(iota((tokens, tokens), 0) < iota((tokens, tokens), 1))
    position = dot(hits, earlier).astype(BF16)
    owner = one_hot(slot_expert(rows, experts))
    slot_hit = dot(owner, hits)
    slot_position = dot(owner, position)
    place = (iota((rows, tokens), 0) % SLOT).astype(F32)
    select = one_hot(
        (slot_hit > 0.5) & (jnp.abs(slot_position - place) < 0.5) & (place < MOST - 0.5)
    )
    select_ref[...] = select
    gate = (ROUTE_SCALE * probs).astype(BF16)
    slot_gate = jnp.sum(
        jnp.where(slot_expert(rows, routed), dot(select, gate), 0.0), axis=1, keepdims=True
    )
    rows_ref[:, :width] = dot(select, grad_ref[...]).astype(BF16)
    rows_ref[:, width:] = jnp.broadcast_to(slot_gate, (rows, LANES)).astype(BF16)


def decode_kernel(first, last, codes_ref, table_ref, hidden_ref, *rest):
    if not first:
        before_ref, scale_ref, *rest = rest
    plain_out_ref, *rest = rest
    weight_ref = rest[-1]
    unroll = 8
    step = pl.program_id(0)
    books, block, groups = codes_ref.shape
    entries = table_ref.shape[1]
    size = table_ref.shape[2]

    @pl.when(step == 0)
    def _():
        plain_out_ref[...] = jnp.zeros_like(plain_out_ref) if first else before_ref[...]

    for chunk in range(groups // LANES):
        lanes = slice(chunk * LANES, (chunk + 1) * LANES)

        def decode_rows(index, carry):
            for member in range(unroll):
                at = pl.ds(pl.multiple_of((index * unroll + member) * 16, 16), 16)
                codes = [codes_ref[b, at, lanes].astype(I16) for b in range(books)]
                low = [c & I16(LANES - 1) for c in codes]
                part = [c >= I16(LANES) for c in codes]
                for i in range(size):
                    values = [
                        jnp.where(
                            part[b],
                            lane_gather(table_ref[b, 1, i], low[b]),
                            lane_gather(table_ref[b, 0, i], low[b]),
                        )
                        for b in range(books)
                    ]
                    weight_ref[at, i * LANES : (i + 1) * LANES] = sum(values[1:], values[0])
            return carry

        lax.fori_loop(0, block // 16 // unroll, decode_rows, 0)
        product = dot(hidden_ref[...], weight_ref[...])
        for i in range(size):
            plain_out_ref[i, :, lanes] += product[:, i * LANES : (i + 1) * LANES]

    if not last:
        return
    out_ref = rest[0]

    @pl.when(step == pl.num_programs(0) - 1)
    def _():
        span = size * LANES
        column = iota((span, span), 0)
        source = size * (column & (LANES - 1)) + column // LANES
        back = (source == iota((span, span), 1)).astype(F32).astype(BF16)
        for chunk in range(groups // LANES):
            lanes = slice(chunk * LANES, (chunk + 1) * LANES)
            split = jnp.concatenate(
                [plain_out_ref[i, :, lanes] * scale_ref[i : i + 1, lanes] for i in range(size)], 1
            ).astype(BF16)
            out_ref[:, chunk * span : (chunk + 1) * span] = dot(split, back).astype(BF16)


def score_kernel(last, twist_ref, out_ref, slots_ref, router_ref, *rest):
    i = pl.program_id(0)
    rows = out_ref.shape[0]
    later_count, routed, part_width = router_ref.shape[1:]
    if last:
        total_before_ref, base_before_ref, score_ref, total_ref, base_ref = rest
    else:
        total_ref, base_ref = rest

    @pl.when(i == 0)
    def _():
        total_ref[...] = total_before_ref[...] if last else jnp.zeros_like(total_ref)
        base_ref[...] = base_before_ref[...] if last else jnp.zeros_like(base_ref)

    out = out_ref[...]
    base = jnp.sum(slots_ref[...].astype(F32) * out.astype(F32), axis=1, keepdims=True)
    base_ref[...] += jnp.broadcast_to(base, (rows, LANES))
    total_ref[...] += dot_nt(router_ref[0].reshape(later_count * routed, part_width), out)

    if not last:
        return

    @pl.when(i == pl.num_programs(0) - 1)
    def _():
        wide = later_count * WIDE
        score_ref[:, :wide] = jnp.zeros((rows, wide), BF16)
        for s in range(later_count):
            score_ref[:, s * WIDE : s * WIDE + routed] = total_ref[
                s * routed : (s + 1) * routed, :
            ].T.astype(BF16)
        base = base_ref[...]
        high = base.astype(BF16).astype(F32)
        middle = (base - high).astype(BF16).astype(F32)
        low = base - high - middle
        column = iota((rows, LANES), 1)
        score_ref[:, wide:] = jnp.where(
            column == 0,
            high,
            jnp.where(column == 1, middle, jnp.where(column == 2, low, 0.0)),
        ).astype(BF16)


def chain_kernel(scores_ref, later_ref, probs_ref, select_ref, own_ref, send_ref, picked_ref):
    rows = scores_ref.shape[0]
    tokens, wide = later_ref.shape
    routed = probs_ref.shape[1]
    later = later_ref[...]
    select = select_ref[...]
    picked = dot(select, later)
    picked_ref[...] = picked.astype(BF16)
    score = jnp.sum(picked * scores_ref[:, :wide].astype(F32), axis=1, keepdims=True) + jnp.sum(
        scores_ref[:, wide:].astype(F32), axis=1, keepdims=True
    )
    score = score.astype(BF16).astype(F32)
    placed = jnp.where(slot_expert(rows, routed), score, 0.0).astype(BF16)
    spread = dot_tn(select, placed)
    probs = probs_ref[...]
    weighted = jnp.sum(probs * spread, axis=1, keepdims=True)
    own = (ROUTE_SCALE * probs * (spread - weighted)).astype(BF16)
    own_ref[...] = own
    send_ref[:, :WIDE] = jnp.zeros((tokens, WIDE), BF16)
    send_ref[:, :routed] = own
    send_ref[:, WIDE:] = later[:, : wide - WIDE]


def add_layers(current, later_ref, router_ref):
    later_count, routed = router_ref.shape[1:3]
    for s in range(later_count - 1, -1, -1):
        part = later_ref[:, s * WIDE : s * WIDE + routed]
        current = (current.astype(F32) + dot(part, router_ref[0, s])).astype(BF16)
    return current


def finish_kernel(
    twist_ref, grad_ref, later_ref, own_ref, router_ref, near_ref, far_ref, result_ref
):
    def finish(routers_ref):
        current = add_layers(grad_ref[...], later_ref, routers_ref)
        result_ref[...] = (current.astype(F32) + dot(own_ref[...], router_ref[...])).astype(BF16)

    @pl.when(pl.program_id(1) == 0)
    def _():
        finish(near_ref)

    @pl.when(pl.program_id(1) == 1)
    def _():
        finish(far_ref)


def slots_kernel(
    twist_ref, slots_ref, gates_ref, later_ref, near_ref, far_ref, plain_out_ref, split_ref,
    scale_grad_ref, grad_ref
):
    i, j = pl.program_id(0), pl.program_id(1)
    part_width = slots_ref.shape[1]
    size = plain_out_ref.shape[0]
    groups = plain_out_ref.shape[2]
    span = size * LANES
    at = pl.ds(pl.multiple_of((twist_ref[0] ^ (2 * i + j)) * part_width, LANES), part_width)
    gate = gates_ref[:, :1].astype(F32)

    def put(routers_ref):
        current = add_layers(slots_ref[...], later_ref, routers_ref)
        grad_ref[:, at] = (gate * current.astype(F32)).astype(BF16)

    @pl.when(j == 0)
    def _():
        put(near_ref)

    @pl.when(j == 1)
    def _():
        put(far_ref)

    @pl.when((i == pl.num_programs(0) - 1) & (j == 1))
    def _():
        column = iota((span, span), 1)
        source = size * (column & (LANES - 1)) + column // LANES
        order = one_hot(source == iota((span, span), 0))
        for chunk in range(groups // LANES):
            lanes = slice(chunk * LANES, (chunk + 1) * LANES)
            split = dot(grad_ref[:, chunk * span : (chunk + 1) * span], order)
            for i in range(size):
                part = split[:, i * LANES : (i + 1) * LANES]
                split_ref[i, :, lanes] = part.astype(BF16)
                scale_grad_ref[i : i + 1, lanes] = jnp.sum(
                    part * plain_out_ref[i, :, lanes], axis=0, keepdims=True
                )


def book_kernel(
    unroll, hidden_ref, slots_ref, scale_ref, codes_ref, out_ref, grad_ref, pair_ref
):
    books, block, groups = codes_ref.shape
    size = slots_ref.shape[0]
    chunks = groups // LANES

    @pl.when(pl.program_id(0) == 0)
    def _():
        out_ref[...] = jnp.zeros_like(out_ref)

    hidden = hidden_ref[...]
    for i in range(size):
        grad = dot_tn(hidden, slots_ref[i]) * scale_ref[i : i + 1, :]
        for c in range(chunks):
            grad_ref[c, pl.ds(i, block, stride=size), :] = grad[:, c * LANES : (c + 1) * LANES]
    for b in range(books):
        for c in range(chunks):
            codes = codes_ref[b, :, c * LANES : (c + 1) * LANES]
            high = (codes * (65536 // LOW + 1)) >> 16
            pair_ref[b, c] = high * 8 + (codes - high * LOW)
    row = iota((16, LANES), 0)
    high_rows = [(row + 16 * k).astype(I16) for k in range(HIGH // 16)]
    low_rows = [((row >> 3) + 2 * k).astype(I16) for k in range(LOW // 2)]
    one = jnp.ones((16, LANES), BF16)
    zero = jnp.zeros((16, LANES), BF16)

    def add_rows(index, totals):
        totals = list(totals)
        for pair in range(unroll // 2):
            left = [[] for _ in range(books)]
            right = [[] for _ in range(books)]
            for member in range(2):
                f = index * unroll + pair * 2 + member
                at = pl.ds(pl.multiple_of(f * size, size), size)
                for c in range(chunks):
                    values = grad_ref[c, at, :]
                    values = jnp.concatenate([values, values], 0).astype(BF16)
                    for b in range(books):
                        pairs = pair_ref[b, c, pl.ds(f, 8, stride=0), :]
                        pairs = jnp.concatenate([pairs, pairs], 0).astype(I16)
                        high = pairs >> I16(3)
                        low = pairs & I16(7)
                        left[b].append(
                            jnp.concatenate([jnp.where(high == r, one, zero) for r in high_rows], 0)
                        )
                        right[b].append(
                            jnp.concatenate([jnp.where(low == r, values, zero) for r in low_rows], 0)
                        )
            for b in range(books):
                totals[b] = totals[b] + dot_nt(
                    jnp.concatenate(left[b], 1), jnp.concatenate(right[b], 1)
                )
        return tuple(totals)

    start = tuple(jnp.zeros(out_ref.shape[1:], F32) for _ in range(books))
    totals = lax.fori_loop(0, block // unroll, add_rows, start)
    for b in range(books):
        out_ref[b] += totals[b]


def whole(shape):
    return pl.BlockSpec(shape, lambda *_: (0,) * len(shape))


def exchange(value):
    return lax.all_to_all(value, "expert", split_axis=0, concat_axis=0, tiled=True)


def swap(value, distance):
    count = lax.axis_size("expert")
    return lax.ppermute(value, "expert", [(i, i ^ distance) for i in range(count)])


def gather_exchange(shares):
    count = lax.axis_size("expert")
    return jnp.stack([shares] + [swap(shares, d) for d in range(2, count, 2)])


def on_device(out_grad, saved_inputs, router, routes, hidden_saved, codes, codebook, scale):
    experts = lax.axis_size("expert")
    layers = lax.axis_size("pipe")
    place = lax.axis_index("expert")
    tokens, width = out_grad.shape
    routed = router.shape[2]
    codes = codes[0, 0]
    codebook = codebook[0, 0]
    hidden = hidden_saved[0, 0]
    inner = hidden.shape[1]
    books, _, groups = codes.shape
    entries, size = codebook.shape[1:]
    rows = experts * SLOT
    later_count = layers - 1
    wide = later_count * WIDE
    grow = max(1, rows // 128)
    router_t = router[0].T
    scale_split = scale[0, 0].reshape(groups, size).T
    hidden = jnp.pad(hidden.reshape(experts, MOST, inner), ((0, 0), (0, SLOT - MOST), (0, 0)))
    hidden = hidden.reshape(rows, inner)

    parts = math.gcd(width // LANES, experts)
    direct = parts == experts
    sharers = experts // parts
    part_width = width // parts
    share_rows = routed // sharers
    own_share = lax.dynamic_slice(
        router_t,
        ((place % sharers) * share_rows, (place // sharers) * part_width),
        (share_rows, part_width),
    )
    shares = jnp.stack(
        [
            lax.ppermute(own_share, "pipe", [(p, p - s) for p in range(s, layers)])
            for s in range(1, layers)
        ]
    )
    twist = jnp.full((1,), place if direct else 0, jnp.int32)

    logits = dot(saved_inputs[0], router[0])
    probs, select, outgoing = pl.pallas_call(
        prepare_kernel,
        out_shape=(
            jax.ShapeDtypeStruct((tokens, routed), F32),
            jax.ShapeDtypeStruct((rows, tokens), BF16),
            jax.ShapeDtypeStruct((rows, width + LANES), BF16),
        ),
        compiler_params=params(12 + 6 * grow),
        name="prepare",
    )(logits, routes[0].T, out_grad)
    slots = exchange(outgoing)
    hidden, outgoing = lax.optimization_barrier((hidden, outgoing))

    halves = entries // LANES
    table = codebook.transpose(0, 2, 1).reshape(books, size, halves, LANES)
    table = jnp.broadcast_to(
        table.transpose(0, 2, 1, 3)[:, :, :, None, :], (books, halves, size, 16, LANES)
    )
    block = 128

    def decode(start, count, before):
        first = before is None
        last = start + count == inner // block
        more = [] if first else [before, scale_split]
        return pl.pallas_call(
            functools.partial(decode_kernel, first, last),
            grid=(count,),
            in_specs=[
                pl.BlockSpec((books, block, groups), lambda s: (0, s + start, 0)),
                whole((books, halves, size, 16, LANES)),
                pl.BlockSpec((rows, block), lambda s: (0, s + start)),
            ]
            + [whole(m.shape) for m in more],
            out_specs=[whole((size, rows, groups))] + [whole((rows, width))] * last,
            out_shape=[jax.ShapeDtypeStruct((size, rows, groups), F32)]
            + [jax.ShapeDtypeStruct((rows, width), BF16)] * last,
            scratch_shapes=[pltpu.VMEM((block, size * LANES), BF16)],
            input_output_aliases={} if first else {3: 0},
            compiler_params=params(60),
            cost_estimate=pl.CostEstimate(
                flops=count * 5_000_000_000, bytes_accessed=2_000_000, transcendentals=0
            ),
            name="decode",
        )(codes, table, hidden, *more)

    blocks = inner // block
    (plain_out,) = decode(0, blocks // 3, None)
    plain_out, shares = lax.optimization_barrier((plain_out, shares))
    near = gather_exchange(shares) if direct else None
    plain_out, expert_out = decode(blocks // 3, blocks - blocks // 3, plain_out)
    if direct:
        plain_out, expert_out, near, slots = lax.optimization_barrier(
            (plain_out, expert_out, near, slots)
        )
        far = swap(near, 1)
    else:
        routers = lax.all_gather(shares, "expert", axis=0, tiled=False)
        routers = routers.reshape(parts, sharers, later_count, share_rows, part_width)
        routers = routers.transpose(0, 2, 1, 3, 4)
        routers = routers.reshape(parts, later_count, routed, part_width)
        near, far = routers[0::2], routers[1::2]

    grid = (parts // 2, 2)

    def columns(height):
        return pl.BlockSpec((height, part_width), lambda i, j, t: (0, t[0] ^ (2 * i + j)))

    router_spec = pl.BlockSpec(
        (1, later_count, routed, part_width), lambda i, j, t: (i, 0, 0, 0)
    )

    def by_columns(kernel, in_specs, out_specs, out_shape, scratch, name):
        return pl.pallas_call(
            kernel,
            grid_spec=pltpu.PrefetchScalarGridSpec(
                num_scalar_prefetch=1,
                grid=grid,
                in_specs=in_specs,
                out_specs=out_specs,
                scratch_shapes=scratch,
            ),
            out_shape=out_shape,
            compiler_params=params(60),
            name=name,
        )

    def score(last, routers, before):
        def half(height):
            return pl.BlockSpec((height, part_width), lambda i, t: (0, t[0] ^ (2 * i + last)))

        sums = [((later_count * routed, rows), F32), ((rows, LANES), F32)]
        return pl.pallas_call(
            functools.partial(score_kernel, last),
            grid_spec=pltpu.PrefetchScalarGridSpec(
                num_scalar_prefetch=1,
                grid=(parts // 2,),
                in_specs=[
                    half(rows),
                    half(rows),
                    pl.BlockSpec(
                        (1, later_count, routed, part_width), lambda i, t: (i, 0, 0, 0)
                    ),
                ]
                + [whole(b.shape) for b in before],
                out_specs=whole((rows, wide + LANES)) if last else [whole(s) for s, _ in sums],
                scratch_shapes=[pltpu.VMEM(s, d) for s, d in sums] if last else [],
            ),
            out_shape=(
                jax.ShapeDtypeStruct((rows, wide + LANES), BF16)
                if last
                else [jax.ShapeDtypeStruct(s, d) for s, d in sums]
            ),
            compiler_params=params(60),
            name="scores",
        )(twist, expert_out, slots, routers, *before)

    scores = exchange(score(True, far, score(False, near, [])))

    chain = pl.pallas_call(
        chain_kernel,
        out_shape=(
            jax.ShapeDtypeStruct((tokens, routed), BF16),
            jax.ShapeDtypeStruct((tokens, wide), BF16),
            jax.ShapeDtypeStruct((rows, wide), BF16),
        ),
        compiler_params=params(8 + 4 * grow),
        name="chain",
    )
    later = jnp.zeros((tokens, wide), BF16)
    for step in range(layers):
        own, send, picked = chain(scores, later, probs, select)
        if step + 1 < layers:
            later = lax.ppermute(send, "pipe", [(p, p - 1) for p in range(1, layers)])

    slot_later = exchange(picked)

    result = by_columns(
        finish_kernel,
        [
            columns(tokens),
            whole((tokens, wide)),
            whole((tokens, routed)),
            columns(routed),
            router_spec,
            router_spec,
        ],
        columns(tokens),
        jax.ShapeDtypeStruct((tokens, width), BF16),
        [],
        "finish",
    )(twist, out_grad, later, own, router_t, near, far)

    slot_split, scale_grad = by_columns(
        slots_kernel,
        [
            columns(rows),
            pl.BlockSpec((rows, LANES), lambda *_: (0, width // LANES)),
            whole((rows, wide)),
            router_spec,
            router_spec,
            whole((size, rows, groups)),
        ],
        [whole((size, rows, groups)), whole((size, groups))],
        [
            jax.ShapeDtypeStruct((size, rows, groups), BF16),
            jax.ShapeDtypeStruct((size, groups), F32),
        ],
        [pltpu.VMEM((rows, width), BF16)],
        "slot_grads",
    )(twist, slots, slots, slot_later, near, far, plain_out)

    block = 128
    unroll = 32
    book_grad = pl.pallas_call(
        functools.partial(book_kernel, unroll),
        grid=(inner // block,),
        in_specs=[
            pl.BlockSpec((rows, block), lambda s: (0, s)),
            whole((size, rows, groups)),
            whole((size, groups)),
            pl.BlockSpec((books, block, groups), lambda s: (0, s, 0)),
        ],
        out_specs=whole((books, HIGH, LOW * size)),
        out_shape=jax.ShapeDtypeStruct((books, HIGH, LOW * size), F32),
        scratch_shapes=[
            pltpu.VMEM((groups // LANES, block * size, LANES), F32),
            pltpu.VMEM((books, groups // LANES, block, LANES), jnp.int32),
        ],
        compiler_params=params(20 + 6 * grow),
        name="book_grads",
    )(hidden, slot_split, scale_split, codes)

    book_grad = book_grad.reshape(books, HIGH * LOW, size)[:, :entries]
    scale_grad = scale_grad.T.reshape(width)
    return (result[None], book_grad[None, None], scale_grad[None, None])


def solution(mesh):
    placed = (
        P("expert", None),
        P("pipe", "expert", None),
        P("pipe", None, None),
        P("pipe", "expert", None),
        P("pipe", "expert", None, None),
        P("pipe", "expert", None, None, None),
        P("pipe", "expert", None, None, None),
        P("pipe", "expert", None),
    )
    return jax.shard_map(
        on_device,
        mesh=mesh,
        in_specs=placed,
        out_specs=(
            P("pipe", "expert", None),
            P("pipe", "expert", None, None, None),
            P("pipe", "expert", None),
        ),
        check_vma=False,
    )
```

```python
import functools
import math

import jax
import jax.numpy as jnp
from jax import lax
from jax.experimental import pallas as pl
from jax.experimental.pallas import tpu as pltpu
from jax.sharding import PartitionSpec as P

MOST = 9
SLOT = 16
ROUTE_SCALE = 16.0
LANES = 128
WIDE = 256
LOW = 6
HIGH = 48
F32 = jnp.float32
BF16 = jnp.bfloat16
I16 = jnp.int16


def params(mib):
    return pltpu.CompilerParams(vmem_limit_bytes=mib << 20)


def dot(a, b):
    return jnp.dot(a, b, preferred_element_type=F32)


def dot_nt(a, b):
    return lax.dot_general(a, b, (((1,), (1,)), ((), ())), preferred_element_type=F32)


def dot_tn(a, b):
    return lax.dot_general(a, b, (((0,), (0,)), ((), ())), preferred_element_type=F32)


def iota(shape, axis):
    return lax.broadcasted_iota(jnp.int32, shape, axis)


def lane_gather(table, index):
    return lax.gather(
        table,
        index[..., None],
        lax.GatherDimensionNumbers(
            offset_dims=(),
            collapsed_slice_dims=(1,),
            start_index_map=(1,),
            operand_batching_dims=(0,),
            start_indices_batching_dims=(0,),
        ),
        slice_sizes=(1, 1),
        mode=lax.GatherScatterMode.PROMISE_IN_BOUNDS,
    )


def slot_expert(rows, columns):
    return iota((rows, columns), 0) // SLOT == iota((rows, columns), 1)


def one_hot(mask):
    return mask.astype(F32).astype(BF16)


def slot_select(state, rows, routed):
    tokens, width = state.shape
    number = jnp.where(iota((tokens, width), 1) >= routed, state, 0.0).astype(BF16)
    owner = iota((width, rows), 0) - routed == iota((width, rows), 1) // SLOT
    place = (iota((tokens, rows), 1) % SLOT + 1).astype(F32)
    return one_hot(jnp.abs(dot(number, one_hot(owner)) - place) < 0.5)


def prepare_kernel(logits_ref, routes_ref, grad_ref, state_ref, rows_ref, order_ref):
    tokens, routed = logits_ref.shape
    top = routes_ref.shape[1]
    width = grad_ref.shape[1]
    rows = rows_ref.shape[0]
    experts = rows // SLOT
    state_width = state_ref.shape[1]
    raised = jnp.exp(logits_ref[...])
    probs = raised / jnp.sum(raised, axis=1, keepdims=True)
    expert = iota((tokens, state_width), 1) - routed
    named = jnp.zeros((tokens, state_width), F32)
    for k in range(top):
        named = named + (routes_ref[:, k : k + 1] == expert).astype(F32)
    named = jnp.where(expert < experts, named, 0.0)
    earlier = one_hot(iota((tokens, tokens), 1) < iota((tokens, tokens), 0))
    state_ref[...] = named * (dot(earlier, named.astype(BF16)) + 1.0)
    state_ref[:, :routed] = probs
    select = slot_select(state_ref[...], rows, routed)
    gate = (ROUTE_SCALE * probs).astype(BF16)
    slot_gate = jnp.sum(
        jnp.where(slot_expert(rows, routed), dot_tn(select, gate), 0.0), axis=1, keepdims=True
    )
    rows_ref[:, :width] = dot_tn(select, grad_ref[...]).astype(BF16)
    rows_ref[:, width:] = jnp.broadcast_to(slot_gate, (rows, LANES)).astype(BF16)
    span = order_ref.shape[0]
    row = iota((span, span), 0)
    source = (span // LANES) * (row & (LANES - 1)) + row // LANES
    order_ref[...] = one_hot(source == iota((span, span), 1))


def decode_kernel(first, last, codes_ref, table_ref, hidden_ref, *rest):
    if not first:
        before_ref, scale_ref, order_ref, *rest = rest
    plain_out_ref, *rest = rest
    weight_ref = rest[-1]
    unroll = 8
    step = pl.program_id(0)
    books, block, groups = codes_ref.shape
    entries = table_ref.shape[1]
    size = table_ref.shape[2]

    @pl.when(step == 0)
    def _():
        plain_out_ref[...] = jnp.zeros_like(plain_out_ref) if first else before_ref[...]

    for chunk in range(groups // LANES):
        lanes = slice(chunk * LANES, (chunk + 1) * LANES)

        def decode_rows(index, carry):
            for member in range(unroll):
                at = pl.ds(pl.multiple_of((index * unroll + member) * 16, 16), 16)
                codes = [codes_ref[b, at, lanes].astype(I16) for b in range(books)]
                low = [c & I16(LANES - 1) for c in codes]
                part = [c >= I16(LANES) for c in codes]
                for i in range(size):
                    values = [
                        jnp.where(
                            part[b],
                            lane_gather(table_ref[b, 1, i], low[b]),
                            lane_gather(table_ref[b, 0, i], low[b]),
                        )
                        for b in range(books)
                    ]
                    weight_ref[at, i * LANES : (i + 1) * LANES] = sum(values[1:], values[0])
            return carry

        lax.fori_loop(0, block // 16 // unroll, decode_rows, 0)
        product = dot(hidden_ref[...], weight_ref[...])
        for i in range(size):
            plain_out_ref[i, :, lanes] += product[:, i * LANES : (i + 1) * LANES]

    if not last:
        return
    out_ref = rest[0]

    @pl.when(step == pl.num_programs(0) - 1)
    def _():
        span = size * LANES
        for chunk in range(groups // LANES):
            lanes = slice(chunk * LANES, (chunk + 1) * LANES)
            split = jnp.concatenate(
                [plain_out_ref[i, :, lanes] * scale_ref[i : i + 1, lanes] for i in range(size)], 1
            ).astype(BF16)
            out_ref[:, chunk * span : (chunk + 1) * span] = dot(
                split, order_ref[...]
            ).astype(BF16)


def score_kernel(last, twist_ref, out_ref, slots_ref, router_ref, *rest):
    i = pl.program_id(0)
    rows = out_ref.shape[0]
    later_count, routed, part_width = router_ref.shape[1:]
    if last:
        total_before_ref, base_before_ref, score_ref, total_ref, base_ref = rest
    else:
        total_ref, base_ref = rest

    @pl.when(i == 0)
    def _():
        total_ref[...] = total_before_ref[...] if last else jnp.zeros_like(total_ref)
        base_ref[...] = base_before_ref[...] if last else jnp.zeros_like(base_ref)

    out = out_ref[...]
    base = jnp.sum(slots_ref[...].astype(F32) * out.astype(F32), axis=1, keepdims=True)
    base_ref[...] += jnp.broadcast_to(base, (rows, LANES))
    total_ref[...] += dot_nt(router_ref[0].reshape(later_count * routed, part_width), out)

    if not last:
        return

    @pl.when(i == pl.num_programs(0) - 1)
    def _():
        wide = later_count * WIDE
        score_ref[:, :wide] = jnp.zeros((rows, wide), BF16)
        for s in range(later_count):
            score_ref[:, s * WIDE : s * WIDE + routed] = total_ref[
                s * routed : (s + 1) * routed, :
            ].T.astype(BF16)
        base = base_ref[...]
        high = base.astype(BF16).astype(F32)
        middle = (base - high).astype(BF16).astype(F32)
        low = base - high - middle
        column = iota((rows, LANES), 1)
        score_ref[:, wide:] = jnp.where(
            column == 0,
            high,
            jnp.where(column == 1, middle, jnp.where(column == 2, low, 0.0)),
        ).astype(BF16)


def response_kernel(routed, scores_ref, state_ref, *rest):
    *later_refs, response_ref = rest
    later_count = len(later_refs)
    rows, width = response_ref.shape
    experts = rows // SLOT
    select = slot_select(state_ref[...], rows, routed)
    column = iota((routed, width), 1)
    entry = iota((routed, width), 0)
    base_row, base_column = iota((LANES, width), 0), iota((LANES, width), 1)
    total = dot(
        scores_ref[:, later_count * WIDE :],
        one_hot((base_column - later_count * experts == base_row) & (base_row < 3)),
    )
    for s in range(later_count):
        probs = later_refs[s][:, :routed]
        high = probs.astype(BF16)
        low = (probs - high.astype(F32)).astype(BF16)
        picked = dot_tn(select, high) + dot_tn(select, low)
        product = scores_ref[:, s * WIDE : s * WIDE + routed].astype(F32)
        mean = jnp.sum(picked * product, axis=1, keepdims=True)
        response = (ROUTE_SCALE * picked * (product - mean)).astype(BF16)
        total = total + dot(
            response, one_hot((column - s * experts == entry) & (entry < experts))
        )
    response_ref[...] = total.astype(BF16)


def chain_kernel(routed, *refs):
    own_ref, later_ref, picked_ref = refs[-3:]
    count = (len(refs) - 3) // 2
    response_refs, state_refs = refs[:count], refs[count : 2 * count]
    rows, width = response_refs[0].shape
    tokens = state_refs[0].shape[0]
    experts = rows // SLOT
    column = iota((rows, width), 1)
    slot = iota((rows, width), 0)
    base = column >= (count - 1) * experts
    stacks = [jnp.zeros((tokens, width), F32) for _ in range(count)]
    own_select = None
    for s in range(count - 1, -1, -1):
        select = slot_select(state_refs[s][...], rows, routed)
        response = response_refs[s][...].astype(F32)
        terms = jnp.where(base, response, 0.0)
        if s < count - 1:
            terms = terms + dot_tn(select, stacks[s].astype(BF16)) * response
        score = jnp.sum(terms, axis=1, keepdims=True).astype(BF16).astype(F32)
        for u in range(s):
            first = (s - u - 1) * experts
            placed = jnp.where(column - first == slot // SLOT, score, 0.0).astype(BF16)
            stacks[u] = stacks[u] + dot(select, placed)
        placed = jnp.where(slot_expert(rows, routed), score, 0.0).astype(BF16)
        spread = dot(select, placed)
        probs = state_refs[s][:, :routed]
        weighted = jnp.sum(probs * spread, axis=1, keepdims=True)
        dlogit = (ROUTE_SCALE * probs * (spread - weighted)).astype(BF16)
        if s == 0:
            own_ref[...] = dlogit
            own_select = select
        else:
            later_ref[:, (s - 1) * WIDE : s * WIDE] = jnp.zeros((tokens, WIDE), BF16)
            later_ref[:, (s - 1) * WIDE : (s - 1) * WIDE + routed] = dlogit
    picked_ref[...] = dot_tn(own_select, later_ref[...]).astype(BF16)


def add_layers(current, later_ref, router_ref):
    later_count, routed = router_ref.shape[1:3]
    for s in range(later_count - 1, -1, -1):
        part = later_ref[:, s * WIDE : s * WIDE + routed]
        current = (current.astype(F32) + dot(part, router_ref[0, s])).astype(BF16)
    return current


def halves_of(twist, part_width):
    return [
        pl.ds(pl.multiple_of(((twist & 1) ^ far) * part_width, LANES), part_width)
        for far in range(2)
    ]


def finish_kernel(
    twist_ref, grad_ref, later_ref, own_ref, router_ref, near_ref, far_ref, result_ref
):
    places = halves_of(twist_ref[0], near_ref.shape[3])
    grads = [grad_ref[:, at] for at in places]
    routers = [router_ref[:, at] for at in places]
    results = []
    for grad, router, routers_ref in zip(grads, routers, (near_ref, far_ref)):
        current = add_layers(grad, later_ref, routers_ref)
        results.append((current.astype(F32) + dot(own_ref[...], router)).astype(BF16))
    for at, result in zip(places, results):
        result_ref[:, at] = result


def slots_kernel(
    twist_ref, slots_ref, gates_ref, later_ref, near_ref, far_ref, plain_out_ref, order_ref,
    split_ref, scale_grad_ref, grad_ref
):
    i = pl.program_id(0)
    part_width = near_ref.shape[3]
    size, _, groups = plain_out_ref.shape
    span = size * LANES
    twist = twist_ref[0]
    pair = ((twist >> 1) ^ i) * 2
    gate = gates_ref[:, :1].astype(F32)
    places = halves_of(twist, part_width)
    slots = [slots_ref[:, at] for at in places]
    grads = [
        (gate * add_layers(part, later_ref, routers_ref).astype(F32)).astype(BF16)
        for part, routers_ref in zip(slots, (near_ref, far_ref))
    ]
    for far in range(2):
        first = (pair + ((twist & 1) ^ far)) * part_width
        grad_ref[:, pl.ds(pl.multiple_of(first, LANES), part_width)] = grads[far]

    @pl.when(i == pl.num_programs(0) - 1)
    def _():
        for chunk in range(groups // LANES):
            lanes = slice(chunk * LANES, (chunk + 1) * LANES)
            split = dot_nt(grad_ref[:, chunk * span : (chunk + 1) * span], order_ref[...])
            for i in range(size):
                part = split[:, i * LANES : (i + 1) * LANES]
                split_ref[i, :, lanes] = part.astype(BF16)
                scale_grad_ref[i : i + 1, lanes] = jnp.sum(
                    part * plain_out_ref[i, :, lanes], axis=0, keepdims=True
                )


def book_kernel(
    unroll, hidden_ref, slots_ref, scale_ref, codes_ref, out_ref, grad_ref, pair_ref
):
    books, block, groups = codes_ref.shape
    size = slots_ref.shape[0]
    chunks = groups // LANES

    @pl.when(pl.program_id(0) == 0)
    def _():
        out_ref[...] = jnp.zeros_like(out_ref)

    hidden = hidden_ref[...]
    for i in range(size):
        grad = dot_tn(hidden, slots_ref[i]) * scale_ref[i : i + 1, :]
        for c in range(chunks):
            grad_ref[c, pl.ds(i, block, stride=size), :] = grad[:, c * LANES : (c + 1) * LANES]
    for b in range(books):
        for c in range(chunks):
            codes = codes_ref[b, :, c * LANES : (c + 1) * LANES]
            high = (codes * (65536 // LOW + 1)) >> 16
            pair_ref[b, c] = high * 8 + (codes - high * LOW)
    row = iota((16, LANES), 0)
    high_rows = [(row + 16 * k).astype(I16) for k in range(HIGH // 16)]
    low_rows = [((row >> 3) + 2 * k).astype(I16) for k in range(LOW // 2)]
    one = jnp.ones((16, LANES), BF16)
    zero = jnp.zeros((16, LANES), BF16)

    def add_rows(index, totals):
        totals = list(totals)
        for pair in range(unroll // 2):
            left = [[] for _ in range(books)]
            right = [[] for _ in range(books)]
            for member in range(2):
                f = index * unroll + pair * 2 + member
                at = pl.ds(pl.multiple_of(f * size, size), size)
                for c in range(chunks):
                    values = grad_ref[c, at, :]
                    values = jnp.concatenate([values, values], 0).astype(BF16)
                    for b in range(books):
                        pairs = pair_ref[b, c, pl.ds(f, 8, stride=0), :]
                        pairs = jnp.concatenate([pairs, pairs], 0).astype(I16)
                        high = pairs >> I16(3)
                        low = pairs & I16(7)
                        left[b].append(
                            jnp.concatenate([jnp.where(high == r, one, zero) for r in high_rows], 0)
                        )
                        right[b].append(
                            jnp.concatenate([jnp.where(low == r, values, zero) for r in low_rows], 0)
                        )
            for b in range(books):
                totals[b] = totals[b] + dot_nt(
                    jnp.concatenate(left[b], 1), jnp.concatenate(right[b], 1)
                )
        return tuple(totals)

    start = tuple(jnp.zeros(out_ref.shape[1:], F32) for _ in range(books))
    totals = lax.fori_loop(0, block // unroll, add_rows, start)
    for b in range(books):
        out_ref[b] += totals[b]


def whole(shape):
    return pl.BlockSpec(shape, lambda *_: (0,) * len(shape))


def exchange(value):
    return lax.all_to_all(value, "expert", split_axis=0, concat_axis=0, tiled=True)


def swap(value, distance):
    count = lax.axis_size("expert")
    return lax.ppermute(value, "expert", [(i, i ^ distance) for i in range(count)])


def pass_down(value, layers):
    return [
        lax.ppermute(value, "pipe", [(p, p - s) for p in range(s, layers)])
        for s in range(1, layers)
    ]


def gather_exchange(shares):
    count = lax.axis_size("expert")
    return jnp.stack([shares] + [swap(shares, d) for d in range(2, count, 2)])


def on_device(out_grad, saved_inputs, router, routes, hidden_saved, codes, codebook, scale):
    experts = lax.axis_size("expert")
    layers = lax.axis_size("pipe")
    place = lax.axis_index("expert")
    tokens, width = out_grad.shape
    routed = router.shape[2]
    codes = codes[0, 0]
    codebook = codebook[0, 0]
    hidden = hidden_saved[0, 0]
    inner = hidden.shape[1]
    books, _, groups = codes.shape
    entries, size = codebook.shape[1:]
    rows = experts * SLOT
    later_count = layers - 1
    wide = later_count * WIDE
    grow = max(1, rows // 128)
    router_t = router[0].T
    scale_split = scale[0, 0].reshape(groups, size).T
    hidden = jnp.pad(hidden.reshape(experts, MOST, inner), ((0, 0), (0, SLOT - MOST), (0, 0)))
    hidden = hidden.reshape(rows, inner)

    parts = math.gcd(width // LANES, experts)
    direct = parts == experts
    sharers = experts // parts
    part_width = width // parts
    share_rows = routed // sharers
    own_share = lax.dynamic_slice(
        router_t,
        ((place % sharers) * share_rows, (place // sharers) * part_width),
        (share_rows, part_width),
    )
    shares = jnp.stack(pass_down(own_share, layers))
    twist = jnp.full((1,), place if direct else 0, jnp.int32)

    logits = dot(saved_inputs[0], router[0])
    state_width = -(-(routed + experts) // LANES) * LANES
    span = size * LANES
    state, outgoing, order = pl.pallas_call(
        prepare_kernel,
        out_shape=(
            jax.ShapeDtypeStruct((tokens, state_width), F32),
            jax.ShapeDtypeStruct((rows, width + LANES), BF16),
            jax.ShapeDtypeStruct((span, span), BF16),
        ),
        compiler_params=params(20 + 6 * grow),
        name="prepare",
    )(logits, routes[0], out_grad)
    slots = exchange(outgoing)
    hidden, outgoing, scale_split = lax.optimization_barrier((hidden, outgoing, scale_split))

    halves = entries // LANES
    table = codebook.transpose(0, 2, 1).reshape(books, size, halves, LANES)
    table = jnp.broadcast_to(
        table.transpose(0, 2, 1, 3)[:, :, :, None, :], (books, halves, size, 16, LANES)
    )
    block = 128

    def decode(start, count, before):
        first = before is None
        last = start + count == inner // block
        more = [] if first else [before, scale_split, order]
        return pl.pallas_call(
            functools.partial(decode_kernel, first, last),
            grid=(count,),
            in_specs=[
                pl.BlockSpec((books, block, groups), lambda s: (0, s + start, 0)),
                whole((books, halves, size, 16, LANES)),
                pl.BlockSpec((rows, block), lambda s: (0, s + start)),
            ]
            + [whole(m.shape) for m in more],
            out_specs=[whole((size, rows, groups))] + [whole((rows, width))] * last,
            out_shape=[jax.ShapeDtypeStruct((size, rows, groups), F32)]
            + [jax.ShapeDtypeStruct((rows, width), BF16)] * last,
            scratch_shapes=[pltpu.VMEM((block, size * LANES), BF16)],
            input_output_aliases={} if first else {3: 0},
            compiler_params=params(60),
            cost_estimate=pl.CostEstimate(
                flops=count * 5_000_000_000, bytes_accessed=2_000_000, transcendentals=0
            ),
            name="decode",
        )(codes, table, hidden, *more)

    blocks = inner // block
    early = max(1, blocks // 6)
    (plain_out,) = decode(0, early, None)
    plain_out, shares, later_state = lax.optimization_barrier((plain_out, shares, state))
    near = gather_exchange(shares) if direct else None
    states = [state] + pass_down(later_state, layers)
    plain_out, expert_out = decode(early, blocks - early, plain_out)
    if direct:
        plain_out, expert_out, near, slots = lax.optimization_barrier(
            (plain_out, expert_out, near, slots)
        )
        far = swap(near, 1)
    else:
        routers = lax.all_gather(shares, "expert", axis=0, tiled=False)
        routers = routers.reshape(parts, sharers, later_count, share_rows, part_width)
        routers = routers.transpose(0, 2, 1, 3, 4)
        routers = routers.reshape(parts, later_count, routed, part_width)
        near, far = routers[0::2], routers[1::2]

    grid = (parts // 2,)

    def columns(height):
        return pl.BlockSpec((height, 2 * part_width), lambda i, t: (0, (t[0] >> 1) ^ i))

    router_spec = pl.BlockSpec((1, later_count, routed, part_width), lambda i, t: (i, 0, 0, 0))

    def by_columns(kernel, in_specs, out_specs, out_shape, scratch, name):
        return pl.pallas_call(
            kernel,
            grid_spec=pltpu.PrefetchScalarGridSpec(
                num_scalar_prefetch=1,
                grid=grid,
                in_specs=in_specs,
                out_specs=out_specs,
                scratch_shapes=scratch,
            ),
            out_shape=out_shape,
            compiler_params=params(60),
            name=name,
        )

    def score(last, routers, before):
        def half(height):
            return pl.BlockSpec((height, part_width), lambda i, t: (0, t[0] ^ (2 * i + last)))

        sums = [((later_count * routed, rows), F32), ((rows, LANES), F32)]
        return pl.pallas_call(
            functools.partial(score_kernel, last),
            grid_spec=pltpu.PrefetchScalarGridSpec(
                num_scalar_prefetch=1,
                grid=(parts // 2,),
                in_specs=[
                    half(rows),
                    half(rows),
                    pl.BlockSpec(
                        (1, later_count, routed, part_width), lambda i, t: (i, 0, 0, 0)
                    ),
                ]
                + [whole(b.shape) for b in before],
                out_specs=whole((rows, wide + LANES)) if last else [whole(s) for s, _ in sums],
                scratch_shapes=[pltpu.VMEM(s, d) for s, d in sums] if last else [],
            ),
            out_shape=(
                jax.ShapeDtypeStruct((rows, wide + LANES), BF16)
                if last
                else [jax.ShapeDtypeStruct(s, d) for s, d in sums]
            ),
            compiler_params=params(60),
            name="scores",
        )(twist, expert_out, slots, routers, *before)

    scores = exchange(score(True, far, score(False, near, [])))

    response_width = -(-(later_count * experts + 3) // LANES) * LANES
    response = pl.pallas_call(
        functools.partial(response_kernel, routed),
        out_shape=jax.ShapeDtypeStruct((rows, response_width), BF16),
        compiler_params=params(12 + 4 * grow),
        name="responses",
    )(scores, *states)
    own, later, picked = pl.pallas_call(
        functools.partial(chain_kernel, routed),
        out_shape=(
            jax.ShapeDtypeStruct((tokens, routed), BF16),
            jax.ShapeDtypeStruct((tokens, wide), BF16),
            jax.ShapeDtypeStruct((rows, wide), BF16),
        ),
        compiler_params=params(12 + 4 * grow),
        name="chain",
    )(response, *pass_down(response, layers), *states)

    slot_later = exchange(picked)

    result = by_columns(
        finish_kernel,
        [
            columns(tokens),
            whole((tokens, wide)),
            whole((tokens, routed)),
            columns(routed),
            router_spec,
            router_spec,
        ],
        columns(tokens),
        jax.ShapeDtypeStruct((tokens, width), BF16),
        [],
        "finish",
    )(twist, out_grad, later, own, router_t, near, far)

    slot_split, scale_grad = by_columns(
        slots_kernel,
        [
            columns(rows),
            pl.BlockSpec((rows, LANES), lambda *_: (0, width // LANES)),
            whole((rows, wide)),
            router_spec,
            router_spec,
            whole((size, rows, groups)),
            whole((span, span)),
        ],
        [whole((size, rows, groups)), whole((size, groups))],
        [
            jax.ShapeDtypeStruct((size, rows, groups), BF16),
            jax.ShapeDtypeStruct((size, groups), F32),
        ],
        [pltpu.VMEM((rows, width), BF16)],
        "slot_grads",
    )(twist, slots, slots, slot_later, near, far, plain_out, order)

    block = 128
    unroll = 64
    book_grad = pl.pallas_call(
        functools.partial(book_kernel, unroll),
        grid=(inner // block,),
        in_specs=[
            pl.BlockSpec((rows, block), lambda s: (0, s)),
            whole((size, rows, groups)),
            whole((size, groups)),
            pl.BlockSpec((books, block, groups), lambda s: (0, s, 0)),
        ],
        out_specs=whole((books, HIGH, LOW * size)),
        out_shape=jax.ShapeDtypeStruct((books, HIGH, LOW * size), F32),
        scratch_shapes=[
            pltpu.VMEM((groups // LANES, block * size, LANES), F32),
            pltpu.VMEM((books, groups // LANES, block, LANES), jnp.int32),
        ],
        compiler_params=params(60),
        name="book_grads",
    )(hidden, slot_split, scale_split, codes)

    book_grad = book_grad.reshape(books, HIGH * LOW, size)[:, :entries]
    scale_grad = scale_grad.T.reshape(width)
    return (result[None], book_grad[None, None], scale_grad[None, None])


def solution(mesh):
    placed = (
        P("expert", None),
        P("pipe", "expert", None),
        P("pipe", None, None),
        P("pipe", "expert", None),
        P("pipe", "expert", None, None),
        P("pipe", "expert", None, None, None),
        P("pipe", "expert", None, None, None),
        P("pipe", "expert", None),
    )
    return jax.shard_map(
        on_device,
        mesh=mesh,
        in_specs=placed,
        out_specs=(
            P("pipe", "expert", None),
            P("pipe", "expert", None, None, None),
            P("pipe", "expert", None),
        ),
        check_vma=False,
    )
```

```python
import functools
import math

import jax
import jax.numpy as jnp
from jax import lax
from jax.experimental import pallas as pl
from jax.experimental.pallas import tpu as pltpu
from jax.sharding import PartitionSpec as P

MOST = 9
SLOT = 16
ROUTE_SCALE = 16.0
LANES = 128
WIDE = 256
LOW = 6
HIGH = 48
F32 = jnp.float32
BF16 = jnp.bfloat16
I16 = jnp.int16


def params(mib):
    return pltpu.CompilerParams(vmem_limit_bytes=mib << 20)


def dot(a, b):
    return jnp.dot(a, b, preferred_element_type=F32)


def dot_nt(a, b):
    return lax.dot_general(a, b, (((1,), (1,)), ((), ())), preferred_element_type=F32)


def dot_tn(a, b):
    return lax.dot_general(a, b, (((0,), (0,)), ((), ())), preferred_element_type=F32)


def iota(shape, axis):
    return lax.broadcasted_iota(jnp.int32, shape, axis)


def lane_gather(table, index):
    return lax.gather(
        table,
        index[..., None],
        lax.GatherDimensionNumbers(
            offset_dims=(),
            collapsed_slice_dims=(1,),
            start_index_map=(1,),
            operand_batching_dims=(0,),
            start_indices_batching_dims=(0,),
        ),
        slice_sizes=(1, 1),
        mode=lax.GatherScatterMode.PROMISE_IN_BOUNDS,
    )


def slot_expert(rows, columns):
    return iota((rows, columns), 0) // SLOT == iota((rows, columns), 1)


def one_hot(mask):
    return mask.astype(F32).astype(BF16)


def slot_select(state, rows, routed):
    tokens, width = state.shape
    number = jnp.where(iota((tokens, width), 1) >= routed, state, 0.0).astype(BF16)
    owner = iota((width, rows), 0) - routed == iota((width, rows), 1) // SLOT
    place = (iota((tokens, rows), 1) % SLOT + 1).astype(F32)
    return one_hot(jnp.abs(dot(number, one_hot(owner)) - place) < 0.5)


def prepare_kernel(logits_ref, routes_ref, grad_ref, state_ref, rows_ref, order_ref):
    tokens, routed = logits_ref.shape
    top = routes_ref.shape[1]
    width = grad_ref.shape[1]
    rows = rows_ref.shape[0]
    experts = rows // SLOT
    state_width = state_ref.shape[1]
    raised = jnp.exp(logits_ref[...])
    probs = raised / jnp.sum(raised, axis=1, keepdims=True)
    expert = iota((tokens, state_width), 1) - routed
    named = jnp.zeros((tokens, state_width), F32)
    for k in range(top):
        named = named + (routes_ref[:, k : k + 1] == expert).astype(F32)
    named = jnp.where(expert < experts, named, 0.0)
    earlier = one_hot(iota((tokens, tokens), 1) < iota((tokens, tokens), 0))
    state_ref[...] = named * (dot(earlier, named.astype(BF16)) + 1.0)
    state_ref[:, :routed] = probs
    select = slot_select(state_ref[...], rows, routed)
    gate = (ROUTE_SCALE * probs).astype(BF16)
    slot_gate = jnp.sum(
        jnp.where(slot_expert(rows, routed), dot_tn(select, gate), 0.0), axis=1, keepdims=True
    )
    rows_ref[:, :width] = dot_tn(select, grad_ref[...]).astype(BF16)
    rows_ref[:, width:] = jnp.broadcast_to(slot_gate, (rows, LANES)).astype(BF16)
    span = order_ref.shape[0]
    row = iota((span, span), 0)
    source = (span // LANES) * (row & (LANES - 1)) + row // LANES
    order_ref[...] = one_hot(source == iota((span, span), 1))


def decode_kernel(first, last, codes_ref, table_ref, hidden_ref, *rest):
    if not first:
        before_ref, scale_ref, order_ref, *rest = rest
    plain_out_ref, *rest = rest
    weight_ref = rest[-1]
    unroll = 8
    step = pl.program_id(0)
    books, block, groups = codes_ref.shape
    entries = table_ref.shape[1]
    size = table_ref.shape[2]

    @pl.when(step == 0)
    def _():
        plain_out_ref[...] = jnp.zeros_like(plain_out_ref) if first else before_ref[...]

    for chunk in range(groups // LANES):
        lanes = slice(chunk * LANES, (chunk + 1) * LANES)

        def decode_rows(index, carry):
            for member in range(unroll):
                at = pl.ds(pl.multiple_of((index * unroll + member) * 16, 16), 16)
                codes = [codes_ref[b, at, lanes].astype(I16) for b in range(books)]
                low = [c & I16(LANES - 1) for c in codes]
                part = [c >= I16(LANES) for c in codes]
                for i in range(size):
                    values = [
                        jnp.where(
                            part[b],
                            lane_gather(table_ref[b, 1, i], low[b]),
                            lane_gather(table_ref[b, 0, i], low[b]),
                        )
                        for b in range(books)
                    ]
                    weight_ref[at, i * LANES : (i + 1) * LANES] = sum(values[1:], values[0])
            return carry

        lax.fori_loop(0, block // 16 // unroll, decode_rows, 0)
        product = dot(hidden_ref[...], weight_ref[...])
        for i in range(size):
            plain_out_ref[i, :, lanes] += product[:, i * LANES : (i + 1) * LANES]

    if not last:
        return
    out_ref = rest[0]

    @pl.when(step == pl.num_programs(0) - 1)
    def _():
        rows = plain_out_ref.shape[1]
        split = [
            jnp.concatenate([plain_out_ref[i, :, at] * scale_ref[i : i + 1, at] for i in range(size)], 1)
            for at in (slice(c * LANES, (c + 1) * LANES) for c in range(groups // LANES))
        ]
        back = dot(jnp.concatenate(split, 0).astype(BF16), order_ref[...]).astype(BF16)
        span = size * LANES
        for chunk in range(groups // LANES):
            out_ref[:, chunk * span : (chunk + 1) * span] = back[chunk * rows : (chunk + 1) * rows]


def score_kernel(last, twist_ref, out_ref, slots_ref, router_ref, *rest):
    i = pl.program_id(0)
    rows = out_ref.shape[0]
    later_count, routed, part_width = router_ref.shape[1:]
    if last:
        total_before_ref, base_before_ref, score_ref, total_ref, base_ref = rest
    else:
        total_ref, base_ref = rest

    @pl.when(i == 0)
    def _():
        total_ref[...] = total_before_ref[...] if last else jnp.zeros_like(total_ref)
        base_ref[...] = base_before_ref[...] if last else jnp.zeros_like(base_ref)

    out = out_ref[...]
    base = jnp.sum(slots_ref[...].astype(F32) * out.astype(F32), axis=1, keepdims=True)
    base_ref[...] += jnp.broadcast_to(base, (rows, LANES))
    total_ref[...] += dot_nt(router_ref[0].reshape(later_count * routed, part_width), out)

    if not last:
        return

    @pl.when(i == pl.num_programs(0) - 1)
    def _():
        wide = later_count * WIDE
        score_ref[:, :wide] = jnp.zeros((rows, wide), BF16)
        for s in range(later_count):
            score_ref[:, s * WIDE : s * WIDE + routed] = total_ref[
                s * routed : (s + 1) * routed, :
            ].T.astype(BF16)
        base = base_ref[...]
        high = base.astype(BF16).astype(F32)
        middle = (base - high).astype(BF16).astype(F32)
        low = base - high - middle
        column = iota((rows, LANES), 1)
        score_ref[:, wide:] = jnp.where(
            column == 0,
            high,
            jnp.where(column == 1, middle, jnp.where(column == 2, low, 0.0)),
        ).astype(BF16)


def response_kernel(routed, scores_ref, state_ref, *rest):
    *later_refs, response_ref = rest
    later_count = len(later_refs)
    rows, width = response_ref.shape
    experts = rows // SLOT
    select = slot_select(state_ref[...], rows, routed)
    column = iota((routed, width), 1)
    entry = iota((routed, width), 0)
    base_row, base_column = iota((LANES, width), 0), iota((LANES, width), 1)
    total = dot(
        scores_ref[:, later_count * WIDE :],
        one_hot((base_column - later_count * experts == base_row) & (base_row < 3)),
    )
    for s in range(later_count):
        probs = later_refs[s][:, :routed]
        high = probs.astype(BF16)
        low = (probs - high.astype(F32)).astype(BF16)
        picked = dot_tn(select, high) + dot_tn(select, low)
        product = scores_ref[:, s * WIDE : s * WIDE + routed].astype(F32)
        mean = jnp.sum(picked * product, axis=1, keepdims=True)
        response = (ROUTE_SCALE * picked * (product - mean)).astype(BF16)
        total = total + dot(
            response, one_hot((column - s * experts == entry) & (entry < experts))
        )
    response_ref[...] = total.astype(BF16)


def chain_kernel(routed, *refs):
    own_ref, later_ref, picked_ref = refs[-3:]
    count = (len(refs) - 3) // 2
    response_refs, state_refs = refs[:count], refs[count : 2 * count]
    rows, width = response_refs[0].shape
    tokens = state_refs[0].shape[0]
    experts = rows // SLOT
    column = iota((rows, width), 1)
    slot = iota((rows, width), 0)
    base = column >= (count - 1) * experts
    stacks = [jnp.zeros((tokens, width), F32) for _ in range(count)]
    own_select = None
    for s in range(count - 1, -1, -1):
        select = slot_select(state_refs[s][...], rows, routed)
        response = response_refs[s][...].astype(F32)
        terms = jnp.where(base, response, 0.0)
        if s < count - 1:
            terms = terms + dot_tn(select, stacks[s].astype(BF16)) * response
        score = jnp.sum(terms, axis=1, keepdims=True).astype(BF16).astype(F32)
        for u in range(s):
            first = (s - u - 1) * experts
            placed = jnp.where(column - first == slot // SLOT, score, 0.0).astype(BF16)
            stacks[u] = stacks[u] + dot(select, placed)
        placed = jnp.where(slot_expert(rows, routed), score, 0.0).astype(BF16)
        spread = dot(select, placed)
        probs = state_refs[s][:, :routed]
        weighted = jnp.sum(probs * spread, axis=1, keepdims=True)
        dlogit = (ROUTE_SCALE * probs * (spread - weighted)).astype(BF16)
        if s == 0:
            own_ref[...] = dlogit
            own_select = select
        else:
            later_ref[:, (s - 1) * WIDE : s * WIDE] = jnp.zeros((tokens, WIDE), BF16)
            later_ref[:, (s - 1) * WIDE : (s - 1) * WIDE + routed] = dlogit
    picked_ref[...] = dot_tn(own_select, later_ref[...]).astype(BF16)


def add_layers(current, later_ref, router_ref):
    later_count, routed = router_ref.shape[1:3]
    for s in range(later_count - 1, -1, -1):
        part = later_ref[:, s * WIDE : s * WIDE + routed]
        current = (current.astype(F32) + dot(part, router_ref[0, s])).astype(BF16)
    return current


def halves_of(twist, part_width):
    return [
        pl.ds(pl.multiple_of(((twist & 1) ^ far) * part_width, LANES), part_width)
        for far in range(2)
    ]


def finish_kernel(
    twist_ref, grad_ref, later_ref, own_ref, router_ref, near_ref, far_ref, result_ref
):
    places = halves_of(twist_ref[0], near_ref.shape[3])
    grads = [grad_ref[:, at] for at in places]
    routers = [router_ref[:, at] for at in places]
    results = []
    for grad, router, routers_ref in zip(grads, routers, (near_ref, far_ref)):
        current = add_layers(grad, later_ref, routers_ref)
        results.append((current.astype(F32) + dot(own_ref[...], router)).astype(BF16))
    for at, result in zip(places, results):
        result_ref[:, at] = result


def slots_kernel(
    twist_ref, slots_ref, gates_ref, later_ref, near_ref, far_ref, plain_out_ref, order_ref,
    split_ref, scale_grad_ref, grad_ref
):
    i = pl.program_id(0)
    part_width = near_ref.shape[3]
    size, _, groups = plain_out_ref.shape
    span = size * LANES
    twist = twist_ref[0]
    pair = ((twist >> 1) ^ i) * 2
    gate = gates_ref[:, :1].astype(F32)
    places = halves_of(twist, part_width)
    slots = [slots_ref[:, at] for at in places]
    grads = [
        (gate * add_layers(part, later_ref, routers_ref).astype(F32)).astype(BF16)
        for part, routers_ref in zip(slots, (near_ref, far_ref))
    ]
    for far in range(2):
        first = (pair + ((twist & 1) ^ far)) * part_width
        grad_ref[:, pl.ds(pl.multiple_of(first, LANES), part_width)] = grads[far]

    @pl.when(i == pl.num_programs(0) - 1)
    def _():
        rows = grad_ref.shape[0]
        chunks = groups // LANES
        grad = [grad_ref[:, c * span : (c + 1) * span] for c in range(chunks)]
        split = dot_nt(jnp.concatenate(grad, 0), order_ref[...])
        for c in range(chunks):
            lanes = slice(c * LANES, (c + 1) * LANES)
            for i in range(size):
                part = split[c * rows : (c + 1) * rows, i * LANES : (i + 1) * LANES]
                split_ref[i, :, lanes] = part.astype(BF16)
                scale_grad_ref[i : i + 1, lanes] = jnp.sum(
                    part * plain_out_ref[i, :, lanes], axis=0, keepdims=True
                )


def book_kernel(
    unroll, hidden_ref, slots_ref, scale_ref, codes_ref, out_ref, grad_ref, pair_ref
):
    books, block, groups = codes_ref.shape
    size = slots_ref.shape[0]
    chunks = groups // LANES

    @pl.when(pl.program_id(0) == 0)
    def _():
        out_ref[...] = jnp.zeros_like(out_ref)

    hidden = hidden_ref[...]
    for i in range(size):
        grad = dot_tn(hidden, slots_ref[i]) * scale_ref[i : i + 1, :]
        for c in range(chunks):
            grad_ref[c, pl.ds(i, block, stride=size), :] = grad[:, c * LANES : (c + 1) * LANES]
    for b in range(books):
        for c in range(chunks):
            codes = codes_ref[b, :, c * LANES : (c + 1) * LANES]
            high = (codes * (65536 // LOW + 1)) >> 16
            pair_ref[b, c] = high * 8 + (codes - high * LOW)
    row = iota((16, LANES), 0)
    high_rows = [(row + 16 * k).astype(I16) for k in range(HIGH // 16)]
    low_rows = [((row >> 3) + 2 * k).astype(I16) for k in range(LOW // 2)]
    one = jnp.ones((16, LANES), BF16)
    zero = jnp.zeros((16, LANES), BF16)

    def add_rows(index, totals):
        totals = list(totals)
        for pair in range(unroll // 2):
            left = [[] for _ in range(books)]
            right = [[] for _ in range(books)]
            for member in range(2):
                f = index * unroll + pair * 2 + member
                at = pl.ds(pl.multiple_of(f * size, size), size)
                for c in range(chunks):
                    values = grad_ref[c, at, :]
                    values = jnp.concatenate([values, values], 0).astype(BF16)
                    for b in range(books):
                        pairs = pair_ref[b, c, pl.ds(f, 8, stride=0), :]
                        pairs = jnp.concatenate([pairs, pairs], 0).astype(I16)
                        high = pairs >> I16(3)
                        low = pairs & I16(7)
                        left[b].append(
                            jnp.concatenate([jnp.where(high == r, one, zero) for r in high_rows], 0)
                        )
                        right[b].append(
                            jnp.concatenate([jnp.where(low == r, values, zero) for r in low_rows], 0)
                        )
            for b in range(books):
                totals[b] = totals[b] + dot_nt(
                    jnp.concatenate(left[b], 1), jnp.concatenate(right[b], 1)
                )
        return tuple(totals)

    start = tuple(jnp.zeros(out_ref.shape[1:], F32) for _ in range(books))
    totals = lax.fori_loop(0, block // unroll, add_rows, start)
    for b in range(books):
        out_ref[b] += totals[b]


def whole(shape):
    return pl.BlockSpec(shape, lambda *_: (0,) * len(shape))


def exchange(value):
    return lax.all_to_all(value, "expert", split_axis=0, concat_axis=0, tiled=True)


def swap(value, distance):
    count = lax.axis_size("expert")
    return lax.ppermute(value, "expert", [(i, i ^ distance) for i in range(count)])


def pass_down(value, layers):
    return [
        lax.ppermute(value, "pipe", [(p, p - s) for p in range(s, layers)])
        for s in range(1, layers)
    ]


def join_kernel(count, *refs):
    *part_refs, out_ref, sems = refs
    copies = [
        pltpu.make_async_copy(ref, out_ref.at[k], sems.at[k])
        for k, ref in enumerate(part_refs[:count])
    ]
    first = 0
    for k in range(count, len(part_refs)):
        last = first + part_refs[k].shape[1]
        copies.append(
            pltpu.make_async_copy(part_refs[k], out_ref.at[count, :, first:last], sems.at[k])
        )
        first = last
    for copy in copies:
        copy.start()
    for copy in copies:
        copy.wait()


def join(wholes, pieces):
    parts = wholes + pieces
    anywhere = pl.BlockSpec(memory_space=pl.ANY)
    return pl.pallas_call(
        functools.partial(join_kernel, len(wholes)),
        in_specs=[anywhere] * len(parts),
        out_specs=anywhere,
        out_shape=jax.ShapeDtypeStruct((len(wholes) + 1,) + wholes[0].shape, wholes[0].dtype),
        scratch_shapes=[pltpu.SemaphoreType.DMA((len(parts),))],
        compiler_params=params(60),
        name="join",
    )(*parts)


def gather_exchange(shares):
    count = lax.axis_size("expert")
    return jnp.stack([shares] + [swap(shares, d) for d in range(2, count, 2)])


def on_device(out_grad, saved_inputs, router, routes, hidden_saved, codes, codebook, scale):
    experts = lax.axis_size("expert")
    layers = lax.axis_size("pipe")
    place = lax.axis_index("expert")
    tokens, width = out_grad.shape
    routed = router.shape[2]
    codes = codes[0, 0]
    codebook = codebook[0, 0]
    hidden = hidden_saved[0, 0]
    inner = hidden.shape[1]
    books, _, groups = codes.shape
    entries, size = codebook.shape[1:]
    rows = experts * SLOT
    later_count = layers - 1
    wide = later_count * WIDE
    grow = max(1, rows // 128)
    router_t = router[0].T
    scale_split = scale[0, 0].reshape(groups, size).T
    hidden = jnp.pad(hidden.reshape(experts, MOST, inner), ((0, 0), (0, SLOT - MOST), (0, 0)))
    hidden = hidden.reshape(rows, inner)

    parts = math.gcd(width // LANES, experts)
    direct = parts == experts
    sharers = experts // parts
    part_width = width // parts
    share_rows = routed // sharers
    own_share = lax.dynamic_slice(
        router_t,
        ((place % sharers) * share_rows, (place // sharers) * part_width),
        (share_rows, part_width),
    )
    shares = jnp.stack(pass_down(own_share, layers))
    twist = jnp.full((1,), place if direct else 0, jnp.int32)

    logits = dot(saved_inputs[0], router[0])
    state_width = -(-(routed + experts) // LANES) * LANES
    span = size * LANES
    state, outgoing, order = pl.pallas_call(
        prepare_kernel,
        out_shape=(
            jax.ShapeDtypeStruct((tokens, state_width), F32),
            jax.ShapeDtypeStruct((rows, width + LANES), BF16),
            jax.ShapeDtypeStruct((span, span), BF16),
        ),
        compiler_params=params(60),
        name="prepare",
    )(logits, routes[0], out_grad)
    slots = exchange(outgoing)
    hidden, outgoing, scale_split = lax.optimization_barrier((hidden, outgoing, scale_split))

    halves = entries // LANES
    table = codebook.transpose(0, 2, 1).reshape(books, size, halves, LANES)
    table = jnp.broadcast_to(
        table.transpose(0, 2, 1, 3)[:, :, :, None, :], (books, halves, size, 16, LANES)
    )
    block = 128

    def decode(start, count, before):
        first = before is None
        last = start + count == inner // block
        more = [] if first else [before, scale_split, order]
        return pl.pallas_call(
            functools.partial(decode_kernel, first, last),
            grid=(count,),
            in_specs=[
                pl.BlockSpec((books, block, groups), lambda s: (0, s + start, 0)),
                whole((books, halves, size, 16, LANES)),
                pl.BlockSpec((rows, block), lambda s: (0, s + start)),
            ]
            + [whole(m.shape) for m in more],
            out_specs=[whole((size, rows, groups))] + [whole((rows, width))] * last,
            out_shape=[jax.ShapeDtypeStruct((size, rows, groups), F32)]
            + [jax.ShapeDtypeStruct((rows, width), BF16)] * last,
            scratch_shapes=[pltpu.VMEM((block, size * LANES), BF16)],
            input_output_aliases={} if first else {3: 0},
            compiler_params=params(60),
            cost_estimate=pl.CostEstimate(
                flops=count * 5_000_000_000, bytes_accessed=2_000_000, transcendentals=0
            ),
            name="decode",
        )(codes, table, hidden, *more)

    blocks = inner // block
    early = max(1, blocks // 6)
    (plain_out,) = decode(0, early, None)
    plain_out, shares, later_state = lax.optimization_barrier((plain_out, shares, state))
    middle = early
    near = None
    if direct and experts == 8:
        half = routed // 2
        beside, above = swap(shares, 2), swap(shares, 4)
        middle = blocks // 2
        (plain_out,) = decode(early, middle - early, plain_out)
        plain_out, beside, above, later_state = lax.optimization_barrier(
            (plain_out, beside, above, later_state)
        )
        upper, lower = swap(beside[:, :half], 4), swap(above[:, half:], 2)
    elif direct:
        near = gather_exchange(shares)
    states = [state] + pass_down(later_state, layers)
    plain_out, expert_out = decode(middle, blocks - middle, plain_out)
    if direct:
        if near is None:
            near = join([shares, beside, above], [upper, lower])
        plain_out, expert_out, near, slots, states = lax.optimization_barrier(
            (plain_out, expert_out, near, slots, states)
        )
        far = swap(near, 1)
    else:
        routers = lax.all_gather(shares, "expert", axis=0, tiled=False)
        routers = routers.reshape(parts, sharers, later_count, share_rows, part_width)
        routers = routers.transpose(0, 2, 1, 3, 4)
        routers = routers.reshape(parts, later_count, routed, part_width)
        near, far = routers[0::2], routers[1::2]

    grid = (parts // 2,)

    def columns(height):
        return pl.BlockSpec((height, 2 * part_width), lambda i, t: (0, (t[0] >> 1) ^ i))

    router_spec = pl.BlockSpec((1, later_count, routed, part_width), lambda i, t: (i, 0, 0, 0))

    def by_columns(kernel, in_specs, out_specs, out_shape, scratch, name):
        return pl.pallas_call(
            kernel,
            grid_spec=pltpu.PrefetchScalarGridSpec(
                num_scalar_prefetch=1,
                grid=grid,
                in_specs=in_specs,
                out_specs=out_specs,
                scratch_shapes=scratch,
            ),
            out_shape=out_shape,
            compiler_params=params(60),
            name=name,
        )

    def score(last, routers, before):
        def half(height):
            return pl.BlockSpec((height, part_width), lambda i, t: (0, t[0] ^ (2 * i + last)))

        sums = [((later_count * routed, rows), F32), ((rows, LANES), F32)]
        return pl.pallas_call(
            functools.partial(score_kernel, last),
            grid_spec=pltpu.PrefetchScalarGridSpec(
                num_scalar_prefetch=1,
                grid=(parts // 2,),
                in_specs=[
                    half(rows),
                    half(rows),
                    pl.BlockSpec(
                        (1, later_count, routed, part_width), lambda i, t: (i, 0, 0, 0)
                    ),
                ]
                + [whole(b.shape) for b in before],
                out_specs=whole((rows, wide + LANES)) if last else [whole(s) for s, _ in sums],
                scratch_shapes=[pltpu.VMEM(s, d) for s, d in sums] if last else [],
            ),
            out_shape=(
                jax.ShapeDtypeStruct((rows, wide + LANES), BF16)
                if last
                else [jax.ShapeDtypeStruct(s, d) for s, d in sums]
            ),
            compiler_params=params(60),
            name="scores",
        )(twist, expert_out, slots, routers, *before)

    scores = exchange(score(True, far, score(False, near, [])))

    response_width = -(-(later_count * experts + 3) // LANES) * LANES
    response = pl.pallas_call(
        functools.partial(response_kernel, routed),
        out_shape=jax.ShapeDtypeStruct((rows, response_width), BF16),
        compiler_params=params(12 + 4 * grow),
        name="responses",
    )(scores, *states)
    own, later, picked = pl.pallas_call(
        functools.partial(chain_kernel, routed),
        out_shape=(
            jax.ShapeDtypeStruct((tokens, routed), BF16),
            jax.ShapeDtypeStruct((tokens, wide), BF16),
            jax.ShapeDtypeStruct((rows, wide), BF16),
        ),
        compiler_params=params(12 + 4 * grow),
        name="chain",
    )(response, *pass_down(response, layers), *states)

    slot_later = exchange(picked)

    result = by_columns(
        finish_kernel,
        [
            columns(tokens),
            whole((tokens, wide)),
            whole((tokens, routed)),
            columns(routed),
            router_spec,
            router_spec,
        ],
        columns(tokens),
        jax.ShapeDtypeStruct((tokens, width), BF16),
        [],
        "finish",
    )(twist, out_grad, later, own, router_t, near, far)

    slot_split, scale_grad = by_columns(
        slots_kernel,
        [
            columns(rows),
            pl.BlockSpec((rows, LANES), lambda *_: (0, width // LANES)),
            whole((rows, wide)),
            router_spec,
            router_spec,
            whole((size, rows, groups)),
            whole((span, span)),
        ],
        [whole((size, rows, groups)), whole((size, groups))],
        [
            jax.ShapeDtypeStruct((size, rows, groups), BF16),
            jax.ShapeDtypeStruct((size, groups), F32),
        ],
        [pltpu.VMEM((rows, width), BF16)],
        "slot_grads",
    )(twist, slots, slots, slot_later, near, far, plain_out, order)

    block = 128
    unroll = 64
    book_grad = pl.pallas_call(
        functools.partial(book_kernel, unroll),
        grid=(inner // block,),
        in_specs=[
            pl.BlockSpec((rows, block), lambda s: (0, s)),
            whole((size, rows, groups)),
            whole((size, groups)),
            pl.BlockSpec((books, block, groups), lambda s: (0, s, 0)),
        ],
        out_specs=whole((books, HIGH, LOW * size)),
        out_shape=jax.ShapeDtypeStruct((books, HIGH, LOW * size), F32),
        scratch_shapes=[
            pltpu.VMEM((groups // LANES, block * size, LANES), F32),
            pltpu.VMEM((books, groups // LANES, block, LANES), jnp.int32),
        ],
        compiler_params=params(60),
        name="book_grads",
    )(hidden, slot_split, scale_split, codes)

    book_grad = book_grad.reshape(books, HIGH * LOW, size)[:, :entries]
    scale_grad = scale_grad.T.reshape(width)
    return (result[None], book_grad[None, None], scale_grad[None, None])


def solution(mesh):
    placed = (
        P("expert", None),
        P("pipe", "expert", None),
        P("pipe", None, None),
        P("pipe", "expert", None),
        P("pipe", "expert", None, None),
        P("pipe", "expert", None, None, None),
        P("pipe", "expert", None, None, None),
        P("pipe", "expert", None),
    )
    return jax.shard_map(
        on_device,
        mesh=mesh,
        in_specs=placed,
        out_specs=(
            P("pipe", "expert", None),
            P("pipe", "expert", None, None, None),
            P("pipe", "expert", None),
        ),
        check_vma=False,
    )
```

```python
import functools
import math

import jax
import jax.numpy as jnp
from jax import lax
from jax.experimental import pallas as pl
from jax.experimental.pallas import tpu as pltpu
from jax.sharding import PartitionSpec as P

MOST = 9
SLOT = 16
ROUTE_SCALE = 16.0
LANES = 128
WIDE = 256
LOW = 6
HIGH = 48
F32 = jnp.float32
BF16 = jnp.bfloat16
I16 = jnp.int16


def params(mib):
    return pltpu.CompilerParams(vmem_limit_bytes=mib << 20)


def dot(a, b):
    return jnp.dot(a, b, preferred_element_type=F32)


def dot_nt(a, b):
    return lax.dot_general(a, b, (((1,), (1,)), ((), ())), preferred_element_type=F32)


def dot_tn(a, b):
    return lax.dot_general(a, b, (((0,), (0,)), ((), ())), preferred_element_type=F32)


def iota(shape, axis):
    return lax.broadcasted_iota(jnp.int32, shape, axis)


def lane_gather(table, index):
    return lax.gather(
        table,
        index[..., None],
        lax.GatherDimensionNumbers(
            offset_dims=(),
            collapsed_slice_dims=(1,),
            start_index_map=(1,),
            operand_batching_dims=(0,),
            start_indices_batching_dims=(0,),
        ),
        slice_sizes=(1, 1),
        mode=lax.GatherScatterMode.PROMISE_IN_BOUNDS,
    )


def slot_expert(rows, columns):
    return iota((rows, columns), 0) // SLOT == iota((rows, columns), 1)


def one_hot(mask):
    return mask.astype(F32).astype(BF16)


def slot_select(state, rows, routed):
    tokens, width = state.shape
    number = jnp.where(iota((tokens, width), 1) >= routed, state, 0.0).astype(BF16)
    owner = iota((width, rows), 0) - routed == iota((width, rows), 1) // SLOT
    place = (iota((tokens, rows), 1) % SLOT + 1).astype(F32)
    return one_hot(jnp.abs(dot(number, one_hot(owner)) - place) < 0.5)


def prepare_kernel(logits_ref, routes_ref, grad_ref, state_ref, rows_ref, order_ref):
    tokens, routed = logits_ref.shape
    top = routes_ref.shape[1]
    width = grad_ref.shape[1]
    rows = rows_ref.shape[0]
    experts = rows // SLOT
    state_width = state_ref.shape[1]
    raised = jnp.exp(logits_ref[...])
    probs = raised / jnp.sum(raised, axis=1, keepdims=True)
    expert = iota((tokens, state_width), 1) - routed
    named = jnp.zeros((tokens, state_width), F32)
    for k in range(top):
        named = named + (routes_ref[:, k : k + 1] == expert).astype(F32)
    named = jnp.where(expert < experts, named, 0.0)
    earlier = one_hot(iota((tokens, tokens), 1) < iota((tokens, tokens), 0))
    state_ref[...] = named * (dot(earlier, named.astype(BF16)) + 1.0)
    state_ref[:, :routed] = probs
    select = slot_select(state_ref[...], rows, routed)
    gate = (ROUTE_SCALE * probs).astype(BF16)
    slot_gate = jnp.sum(
        jnp.where(slot_expert(rows, routed), dot_tn(select, gate), 0.0), axis=1, keepdims=True
    )
    rows_ref[:, :width] = dot_tn(select, grad_ref[...]).astype(BF16)
    rows_ref[:, width:] = jnp.broadcast_to(slot_gate, (rows, LANES)).astype(BF16)
    span = order_ref.shape[0]
    row = iota((span, span), 0)
    source = (span // LANES) * (row & (LANES - 1)) + row // LANES
    order_ref[...] = one_hot(source == iota((span, span), 1))


def decode_kernel(first, last, codes_ref, table_ref, hidden_ref, *rest):
    if not first:
        before_ref, scale_ref, order_ref, *rest = rest
    plain_out_ref, *rest = rest
    weight_ref = rest[-1]
    unroll = 8
    step = pl.program_id(0)
    books, block, groups = codes_ref.shape
    entries = table_ref.shape[1]
    size = table_ref.shape[2]

    @pl.when(step == 0)
    def _():
        plain_out_ref[...] = jnp.zeros_like(plain_out_ref) if first else before_ref[...]

    for chunk in range(groups // LANES):
        lanes = slice(chunk * LANES, (chunk + 1) * LANES)

        def decode_rows(index, carry):
            for member in range(unroll):
                at = pl.ds(pl.multiple_of((index * unroll + member) * 16, 16), 16)
                codes = [codes_ref[b, at, lanes].astype(I16) for b in range(books)]
                low = [c & I16(LANES - 1) for c in codes]
                part = [c >= I16(LANES) for c in codes]
                for i in range(size):
                    values = [
                        jnp.where(
                            part[b],
                            lane_gather(table_ref[b, 1, i], low[b]),
                            lane_gather(table_ref[b, 0, i], low[b]),
                        )
                        for b in range(books)
                    ]
                    weight_ref[at, i * LANES : (i + 1) * LANES] = sum(values[1:], values[0])
            return carry

        lax.fori_loop(0, block // 16 // unroll, decode_rows, 0)
        product = dot(hidden_ref[...], weight_ref[...])
        for i in range(size):
            plain_out_ref[i, :, lanes] += product[:, i * LANES : (i + 1) * LANES]

    if not last:
        return
    out_ref = rest[0]

    @pl.when(step == pl.num_programs(0) - 1)
    def _():
        rows = plain_out_ref.shape[1]
        split = [
            jnp.concatenate([plain_out_ref[i, :, at] * scale_ref[i : i + 1, at] for i in range(size)], 1)
            for at in (slice(c * LANES, (c + 1) * LANES) for c in range(groups // LANES))
        ]
        back = dot(jnp.concatenate(split, 0).astype(BF16), order_ref[...]).astype(BF16)
        span = size * LANES
        for chunk in range(groups // LANES):
            out_ref[:, chunk * span : (chunk + 1) * span] = back[chunk * rows : (chunk + 1) * rows]


def score_kernel(last, twist_ref, out_ref, slots_ref, router_ref, *rest):
    i = pl.program_id(0)
    rows = out_ref.shape[0]
    later_count, routed, part_width = router_ref.shape[1:]
    if last:
        total_before_ref, base_before_ref, score_ref, total_ref, base_ref = rest
    else:
        total_ref, base_ref = rest

    @pl.when(i == 0)
    def _():
        total_ref[...] = total_before_ref[...] if last else jnp.zeros_like(total_ref)
        base_ref[...] = base_before_ref[...] if last else jnp.zeros_like(base_ref)

    out = out_ref[...]
    base = jnp.sum(slots_ref[...].astype(F32) * out.astype(F32), axis=1, keepdims=True)
    base_ref[...] += jnp.broadcast_to(base, (rows, LANES))
    total_ref[...] += dot_nt(router_ref[0].reshape(later_count * routed, part_width), out)

    if not last:
        return

    @pl.when(i == pl.num_programs(0) - 1)
    def _():
        wide = later_count * WIDE
        score_ref[:, :wide] = jnp.zeros((rows, wide), BF16)
        for s in range(later_count):
            score_ref[:, s * WIDE : s * WIDE + routed] = total_ref[
                s * routed : (s + 1) * routed, :
            ].T.astype(BF16)
        base = base_ref[...]
        high = base.astype(BF16).astype(F32)
        middle = (base - high).astype(BF16).astype(F32)
        low = base - high - middle
        column = iota((rows, LANES), 1)
        score_ref[:, wide:] = jnp.where(
            column == 0,
            high,
            jnp.where(column == 1, middle, jnp.where(column == 2, low, 0.0)),
        ).astype(BF16)


def response_kernel(routed, scores_ref, state_ref, *rest):
    *later_refs, response_ref = rest
    later_count = len(later_refs)
    rows, width = response_ref.shape
    experts = rows // SLOT
    select = slot_select(state_ref[...], rows, routed)
    column = iota((routed, width), 1)
    entry = iota((routed, width), 0)
    base_row, base_column = iota((LANES, width), 0), iota((LANES, width), 1)
    total = dot(
        scores_ref[:, later_count * WIDE :],
        one_hot((base_column - later_count * experts == base_row) & (base_row < 3)),
    )
    for s in range(later_count):
        probs = later_refs[s][:, :routed]
        high = probs.astype(BF16)
        low = (probs - high.astype(F32)).astype(BF16)
        picked = dot_tn(select, high) + dot_tn(select, low)
        product = scores_ref[:, s * WIDE : s * WIDE + routed].astype(F32)
        mean = jnp.sum(picked * product, axis=1, keepdims=True)
        response = (ROUTE_SCALE * picked * (product - mean)).astype(BF16)
        total = total + dot(
            response, one_hot((column - s * experts == entry) & (entry < experts))
        )
    response_ref[...] = total.astype(BF16)


def chain_kernel(routed, *refs):
    own_ref, later_ref, picked_ref = refs[-3:]
    count = (len(refs) - 3) // 2
    response_refs, state_refs = refs[:count], refs[count : 2 * count]
    rows, width = response_refs[0].shape
    tokens = state_refs[0].shape[0]
    experts = rows // SLOT
    column = iota((rows, width), 1)
    slot = iota((rows, width), 0)
    base = column >= (count - 1) * experts
    stacks = [jnp.zeros((tokens, width), F32) for _ in range(count)]
    own_select = None
    for s in range(count - 1, -1, -1):
        select = slot_select(state_refs[s][...], rows, routed)
        response = response_refs[s][...].astype(F32)
        terms = jnp.where(base, response, 0.0)
        if s < count - 1:
            terms = terms + dot_tn(select, stacks[s].astype(BF16)) * response
        score = jnp.sum(terms, axis=1, keepdims=True).astype(BF16).astype(F32)
        for u in range(s):
            first = (s - u - 1) * experts
            placed = jnp.where(column - first == slot // SLOT, score, 0.0).astype(BF16)
            stacks[u] = stacks[u] + dot(select, placed)
        placed = jnp.where(slot_expert(rows, routed), score, 0.0).astype(BF16)
        spread = dot(select, placed)
        probs = state_refs[s][:, :routed]
        weighted = jnp.sum(probs * spread, axis=1, keepdims=True)
        dlogit = (ROUTE_SCALE * probs * (spread - weighted)).astype(BF16)
        if s == 0:
            own_ref[...] = dlogit
            own_select = select
        else:
            later_ref[:, (s - 1) * WIDE : s * WIDE] = jnp.zeros((tokens, WIDE), BF16)
            later_ref[:, (s - 1) * WIDE : (s - 1) * WIDE + routed] = dlogit
    picked_ref[...] = dot_tn(own_select, later_ref[...]).astype(BF16)


def add_layers(current, later_ref, router_ref):
    later_count, routed = router_ref.shape[1:3]
    for s in range(later_count - 1, -1, -1):
        part = later_ref[:, s * WIDE : s * WIDE + routed]
        current = (current.astype(F32) + dot(part, router_ref[0, s])).astype(BF16)
    return current


def halves_of(twist, part_width):
    return [
        pl.ds(pl.multiple_of(((twist & 1) ^ far) * part_width, LANES), part_width)
        for far in range(2)
    ]


def finish_kernel(
    twist_ref, grad_ref, later_ref, own_ref, router_ref, near_ref, far_ref, result_ref
):
    places = halves_of(twist_ref[0], near_ref.shape[3])
    grads = [grad_ref[:, at] for at in places]
    routers = [router_ref[:, at] for at in places]
    results = []
    for grad, router, routers_ref in zip(grads, routers, (near_ref, far_ref)):
        current = add_layers(grad, later_ref, routers_ref)
        results.append((current.astype(F32) + dot(own_ref[...], router)).astype(BF16))
    for at, result in zip(places, results):
        result_ref[:, at] = result


def slots_kernel(
    twist_ref, slots_ref, gates_ref, later_ref, near_ref, far_ref, plain_out_ref, order_ref,
    split_ref, scale_grad_ref, grad_ref
):
    i = pl.program_id(0)
    part_width = near_ref.shape[3]
    size, _, groups = plain_out_ref.shape
    span = size * LANES
    twist = twist_ref[0]
    pair = ((twist >> 1) ^ i) * 2
    gate = gates_ref[:, :1].astype(F32)
    places = halves_of(twist, part_width)
    slots = [slots_ref[:, at] for at in places]
    grads = [
        (gate * add_layers(part, later_ref, routers_ref).astype(F32)).astype(BF16)
        for part, routers_ref in zip(slots, (near_ref, far_ref))
    ]
    for far in range(2):
        first = (pair + ((twist & 1) ^ far)) * part_width
        grad_ref[:, pl.ds(pl.multiple_of(first, LANES), part_width)] = grads[far]

    @pl.when(i == pl.num_programs(0) - 1)
    def _():
        rows = grad_ref.shape[0]
        chunks = groups // LANES
        grad = [grad_ref[:, c * span : (c + 1) * span] for c in range(chunks)]
        split = dot_nt(jnp.concatenate(grad, 0), order_ref[...])
        for c in range(chunks):
            lanes = slice(c * LANES, (c + 1) * LANES)
            for i in range(size):
                part = split[c * rows : (c + 1) * rows, i * LANES : (i + 1) * LANES]
                split_ref[i, :, lanes] = part.astype(BF16)
                scale_grad_ref[i : i + 1, lanes] = jnp.sum(
                    part * plain_out_ref[i, :, lanes], axis=0, keepdims=True
                )


def book_kernel(
    unroll, hidden_ref, slots_ref, scale_ref, codes_ref, out_ref, grad_ref, pair_ref
):
    books, block, groups = codes_ref.shape
    size = slots_ref.shape[0]
    chunks = groups // LANES

    @pl.when(pl.program_id(0) == 0)
    def _():
        out_ref[...] = jnp.zeros_like(out_ref)

    hidden = hidden_ref[...]
    for i in range(size):
        grad = dot_tn(hidden, slots_ref[i]) * scale_ref[i : i + 1, :]
        for c in range(chunks):
            grad_ref[c, pl.ds(i, block, stride=size), :] = grad[:, c * LANES : (c + 1) * LANES]
    for b in range(books):
        for c in range(chunks):
            codes = codes_ref[b, :, c * LANES : (c + 1) * LANES]
            high = (codes * (65536 // LOW + 1)) >> 16
            pair_ref[b, c] = high * 8 + (codes - high * LOW)
    row = iota((16, LANES), 0)
    high_rows = [(row + 16 * k).astype(I16) for k in range(HIGH // 16)]
    low_rows = [((row >> 3) + 2 * k).astype(I16) for k in range(LOW // 2)]
    one = jnp.ones((16, LANES), BF16)
    zero = jnp.zeros((16, LANES), BF16)

    def add_rows(index, totals):
        totals = list(totals)
        for pair in range(unroll // 2):
            left = [[] for _ in range(books)]
            right = [[] for _ in range(books)]
            for member in range(2):
                f = index * unroll + pair * 2 + member
                at = pl.ds(pl.multiple_of(f * size, size), size)
                for c in range(chunks):
                    values = grad_ref[c, at, :]
                    values = jnp.concatenate([values, values], 0).astype(BF16)
                    for b in range(books):
                        pairs = pair_ref[b, c, pl.ds(f, 8, stride=0), :]
                        pairs = jnp.concatenate([pairs, pairs], 0).astype(I16)
                        high = pairs >> I16(3)
                        low = pairs & I16(7)
                        left[b].append(
                            jnp.concatenate([jnp.where(high == r, one, zero) for r in high_rows], 0)
                        )
                        right[b].append(
                            jnp.concatenate([jnp.where(low == r, values, zero) for r in low_rows], 0)
                        )
            for b in range(books):
                totals[b] = totals[b] + dot_nt(
                    jnp.concatenate(left[b], 1), jnp.concatenate(right[b], 1)
                )
        return tuple(totals)

    start = tuple(jnp.zeros(out_ref.shape[1:], F32) for _ in range(books))
    totals = lax.fori_loop(0, block // unroll, add_rows, start)
    for b in range(books):
        out_ref[b] += totals[b]


def whole(shape):
    return pl.BlockSpec(shape, lambda *_: (0,) * len(shape))


def exchange(value):
    return lax.all_to_all(value, "expert", split_axis=0, concat_axis=0, tiled=True)


def swap(value, distance):
    count = lax.axis_size("expert")
    return lax.ppermute(value, "expert", [(i, i ^ distance) for i in range(count)])


def pass_down(value, layers):
    return [
        lax.ppermute(value, "pipe", [(p, p - s) for p in range(s, layers)])
        for s in range(1, layers)
    ]


def join_kernel(*refs):
    *part_refs, out_ref = refs
    for k, ref in enumerate(part_refs):
        out_ref[k] = ref[...]


def join(parts):
    return pl.pallas_call(
        join_kernel,
        out_shape=jax.ShapeDtypeStruct((len(parts),) + parts[0].shape, parts[0].dtype),
        compiler_params=params(60),
        name="join",
    )(*parts)


def exchange_near(shares):
    count = lax.axis_size("expert")
    return [shares] + [swap(shares, d) for d in range(2, count, 2)]


def on_device(out_grad, saved_inputs, router, routes, hidden_saved, codes, codebook, scale):
    experts = lax.axis_size("expert")
    layers = lax.axis_size("pipe")
    place = lax.axis_index("expert")
    tokens, width = out_grad.shape
    routed = router.shape[2]
    codes = codes[0, 0]
    codebook = codebook[0, 0]
    hidden = hidden_saved[0, 0]
    inner = hidden.shape[1]
    books, _, groups = codes.shape
    entries, size = codebook.shape[1:]
    rows = experts * SLOT
    later_count = layers - 1
    wide = later_count * WIDE
    grow = max(1, rows // 128)
    router_t = router[0].T
    scale_split = scale[0, 0].reshape(groups, size).T
    hidden = jnp.pad(hidden.reshape(experts, MOST, inner), ((0, 0), (0, SLOT - MOST), (0, 0)))
    hidden = hidden.reshape(rows, inner)

    parts = math.gcd(width // LANES, experts)
    direct = parts == experts
    sharers = experts // parts
    part_width = width // parts
    share_rows = routed // sharers
    own_share = lax.dynamic_slice(
        router_t,
        ((place % sharers) * share_rows, (place // sharers) * part_width),
        (share_rows, part_width),
    )
    shares = jnp.stack(pass_down(own_share, layers))
    twist = jnp.full((1,), place if direct else 0, jnp.int32)

    logits = dot(saved_inputs[0], router[0])
    state_width = -(-(routed + experts) // LANES) * LANES
    span = size * LANES
    state, outgoing, order = pl.pallas_call(
        prepare_kernel,
        out_shape=(
            jax.ShapeDtypeStruct((tokens, state_width), F32),
            jax.ShapeDtypeStruct((rows, width + LANES), BF16),
            jax.ShapeDtypeStruct((span, span), BF16),
        ),
        compiler_params=params(20 + 6 * grow),
        name="prepare",
    )(logits, routes[0], out_grad)
    slots = exchange(outgoing)
    hidden, outgoing, scale_split = lax.optimization_barrier((hidden, outgoing, scale_split))

    halves = entries // LANES
    table = codebook.transpose(0, 2, 1).reshape(books, size, halves, LANES)
    table = jnp.broadcast_to(
        table.transpose(0, 2, 1, 3)[:, :, :, None, :], (books, halves, size, 16, LANES)
    )
    block = 128

    def decode(start, count, before):
        first = before is None
        last = start + count == inner // block
        more = [] if first else [before, scale_split, order]
        return pl.pallas_call(
            functools.partial(decode_kernel, first, last),
            grid=(count,),
            in_specs=[
                pl.BlockSpec((books, block, groups), lambda s: (0, s + start, 0)),
                whole((books, halves, size, 16, LANES)),
                pl.BlockSpec((rows, block), lambda s: (0, s + start)),
            ]
            + [whole(m.shape) for m in more],
            out_specs=[whole((size, rows, groups))] + [whole((rows, width))] * last,
            out_shape=[jax.ShapeDtypeStruct((size, rows, groups), F32)]
            + [jax.ShapeDtypeStruct((rows, width), BF16)] * last,
            scratch_shapes=[pltpu.VMEM((block, size * LANES), BF16)],
            input_output_aliases={} if first else {3: 0},
            compiler_params=params(60),
            cost_estimate=pl.CostEstimate(
                flops=count * 5_000_000_000, bytes_accessed=2_000_000, transcendentals=0
            ),
            name="decode",
        )(codes, table, hidden, *more)

    blocks = inner // block
    early = max(1, blocks // 6)
    (plain_out,) = decode(0, early, None)
    later_states = pass_down(state, layers)
    plain_out, shares, farthest = lax.optimization_barrier((plain_out, shares, later_states[-1]))
    near = exchange_near(shares) if direct else None
    states = [state] + later_states[:-1] + [farthest]
    plain_out, expert_out = decode(early, blocks - early, plain_out)
    if direct:
        near = join(near)
        plain_out, expert_out, near, slots, states = lax.optimization_barrier(
            (plain_out, expert_out, near, slots, states)
        )
        far = swap(near, 1)
    else:
        routers = lax.all_gather(shares, "expert", axis=0, tiled=False)
        routers = routers.reshape(parts, sharers, later_count, share_rows, part_width)
        routers = routers.transpose(0, 2, 1, 3, 4)
        routers = routers.reshape(parts, later_count, routed, part_width)
        near, far = routers[0::2], routers[1::2]

    grid = (parts // 2,)

    def columns(height):
        return pl.BlockSpec((height, 2 * part_width), lambda i, t: (0, (t[0] >> 1) ^ i))

    router_spec = pl.BlockSpec((1, later_count, routed, part_width), lambda i, t: (i, 0, 0, 0))

    def by_columns(kernel, in_specs, out_specs, out_shape, scratch, name):
        return pl.pallas_call(
            kernel,
            grid_spec=pltpu.PrefetchScalarGridSpec(
                num_scalar_prefetch=1,
                grid=grid,
                in_specs=in_specs,
                out_specs=out_specs,
                scratch_shapes=scratch,
            ),
            out_shape=out_shape,
            compiler_params=params(60),
            name=name,
        )

    def score(last, routers, before):
        def half(height):
            return pl.BlockSpec((height, part_width), lambda i, t: (0, t[0] ^ (2 * i + last)))

        sums = [((later_count * routed, rows), F32), ((rows, LANES), F32)]
        return pl.pallas_call(
            functools.partial(score_kernel, last),
            grid_spec=pltpu.PrefetchScalarGridSpec(
                num_scalar_prefetch=1,
                grid=(parts // 2,),
                in_specs=[
                    half(rows),
                    half(rows),
                    pl.BlockSpec(
                        (1, later_count, routed, part_width), lambda i, t: (i, 0, 0, 0)
                    ),
                ]
                + [whole(b.shape) for b in before],
                out_specs=whole((rows, wide + LANES)) if last else [whole(s) for s, _ in sums],
                scratch_shapes=[pltpu.VMEM(s, d) for s, d in sums] if last else [],
            ),
            out_shape=(
                jax.ShapeDtypeStruct((rows, wide + LANES), BF16)
                if last
                else [jax.ShapeDtypeStruct(s, d) for s, d in sums]
            ),
            compiler_params=params(60),
            name="scores",
        )(twist, expert_out, slots, routers, *before)

    scores = exchange(score(True, far, score(False, near, [])))

    response_width = -(-(later_count * experts + 3) // LANES) * LANES
    response = pl.pallas_call(
        functools.partial(response_kernel, routed),
        out_shape=jax.ShapeDtypeStruct((rows, response_width), BF16),
        compiler_params=params(12 + 4 * grow),
        name="responses",
    )(scores, *states)
    own, later, picked = pl.pallas_call(
        functools.partial(chain_kernel, routed),
        out_shape=(
            jax.ShapeDtypeStruct((tokens, routed), BF16),
            jax.ShapeDtypeStruct((tokens, wide), BF16),
            jax.ShapeDtypeStruct((rows, wide), BF16),
        ),
        compiler_params=params(12 + 4 * grow),
        name="chain",
    )(response, *pass_down(response, layers), *states)

    slot_later = exchange(picked)

    result = by_columns(
        finish_kernel,
        [
            columns(tokens),
            whole((tokens, wide)),
            whole((tokens, routed)),
            columns(routed),
            router_spec,
            router_spec,
        ],
        columns(tokens),
        jax.ShapeDtypeStruct((tokens, width), BF16),
        [],
        "finish",
    )(twist, out_grad, later, own, router_t, near, far)

    slot_split, scale_grad = by_columns(
        slots_kernel,
        [
            columns(rows),
            pl.BlockSpec((rows, LANES), lambda *_: (0, width // LANES)),
            whole((rows, wide)),
            router_spec,
            router_spec,
            whole((size, rows, groups)),
            whole((span, span)),
        ],
        [whole((size, rows, groups)), whole((size, groups))],
        [
            jax.ShapeDtypeStruct((size, rows, groups), BF16),
            jax.ShapeDtypeStruct((size, groups), F32),
        ],
        [pltpu.VMEM((rows, width), BF16)],
        "slot_grads",
    )(twist, slots, slots, slot_later, near, far, plain_out, order)

    block = 128
    unroll = 64
    book_grad = pl.pallas_call(
        functools.partial(book_kernel, unroll),
        grid=(inner // block,),
        in_specs=[
            pl.BlockSpec((rows, block), lambda s: (0, s)),
            whole((size, rows, groups)),
            whole((size, groups)),
            pl.BlockSpec((books, block, groups), lambda s: (0, s, 0)),
        ],
        out_specs=whole((books, HIGH, LOW * size)),
        out_shape=jax.ShapeDtypeStruct((books, HIGH, LOW * size), F32),
        scratch_shapes=[
            pltpu.VMEM((groups // LANES, block * size, LANES), F32),
            pltpu.VMEM((books, groups // LANES, block, LANES), jnp.int32),
        ],
        compiler_params=params(60),
        name="book_grads",
    )(hidden, slot_split, scale_split, codes)

    book_grad = book_grad.reshape(books, HIGH * LOW, size)[:, :entries]
    scale_grad = scale_grad.T.reshape(width)
    return (result[None], book_grad[None, None], scale_grad[None, None])


def solution(mesh):
    placed = (
        P("expert", None),
        P("pipe", "expert", None),
        P("pipe", None, None),
        P("pipe", "expert", None),
        P("pipe", "expert", None, None),
        P("pipe", "expert", None, None, None),
        P("pipe", "expert", None, None, None),
        P("pipe", "expert", None),
    )
    return jax.shard_map(
        on_device,
        mesh=mesh,
        in_specs=placed,
        out_specs=(
            P("pipe", "expert", None),
            P("pipe", "expert", None, None, None),
            P("pipe", "expert", None),
        ),
        check_vma=False,
    )
```

```python
import functools
import math

import jax
import jax.numpy as jnp
from jax import lax
from jax.experimental import pallas as pl
from jax.experimental.pallas import tpu as pltpu
from jax.sharding import PartitionSpec as P

MOST = 9
SLOT = 16
ROUTE_SCALE = 16.0
LANES = 128
WIDE = 256
LOW = 6
HIGH = 48
F32 = jnp.float32
BF16 = jnp.bfloat16
I16 = jnp.int16


def params(mib):
    return pltpu.CompilerParams(vmem_limit_bytes=mib << 20)


def dot(a, b):
    return jnp.dot(a, b, preferred_element_type=F32)


def dot_nt(a, b):
    return lax.dot_general(a, b, (((1,), (1,)), ((), ())), preferred_element_type=F32)


def dot_tn(a, b):
    return lax.dot_general(a, b, (((0,), (0,)), ((), ())), preferred_element_type=F32)


def iota(shape, axis):
    return lax.broadcasted_iota(jnp.int32, shape, axis)


def lane_gather(table, index):
    return lax.gather(
        table,
        index[..., None],
        lax.GatherDimensionNumbers(
            offset_dims=(),
            collapsed_slice_dims=(1,),
            start_index_map=(1,),
            operand_batching_dims=(0,),
            start_indices_batching_dims=(0,),
        ),
        slice_sizes=(1, 1),
        mode=lax.GatherScatterMode.PROMISE_IN_BOUNDS,
    )


def slot_expert(rows, columns):
    return iota((rows, columns), 0) // SLOT == iota((rows, columns), 1)


def one_hot(mask):
    return mask.astype(F32).astype(BF16)


def spread_slots(hidden, rows):
    row = iota((rows, hidden.shape[0]), 0)
    place = row % SLOT
    source = iota((rows, hidden.shape[0]), 1)
    spread = one_hot((row // SLOT * MOST + place == source) & (place < MOST))
    return dot(spread, hidden).astype(BF16)


def slot_select(state, rows, routed):
    tokens, width = state.shape
    number = jnp.where(iota((tokens, width), 1) >= routed, state, 0.0).astype(BF16)
    owner = iota((width, rows), 0) - routed == iota((width, rows), 1) // SLOT
    place = (iota((tokens, rows), 1) % SLOT + 1).astype(F32)
    return one_hot(jnp.abs(dot(number, one_hot(owner)) - place) < 0.5)


def prepare_kernel(logits_ref, routes_ref, grad_ref, state_ref, rows_ref, order_ref):
    tokens, routed = logits_ref.shape
    top = routes_ref.shape[1]
    width = grad_ref.shape[1]
    rows = rows_ref.shape[0]
    experts = rows // SLOT
    state_width = state_ref.shape[1]
    raised = jnp.exp(logits_ref[...])
    probs = raised / jnp.sum(raised, axis=1, keepdims=True)
    expert = iota((tokens, state_width), 1) - routed
    named = jnp.zeros((tokens, state_width), F32)
    for k in range(top):
        named = named + (routes_ref[:, k : k + 1] == expert).astype(F32)
    named = jnp.where(expert < experts, named, 0.0)
    earlier = one_hot(iota((tokens, tokens), 1) < iota((tokens, tokens), 0))
    state_ref[...] = named * (dot(earlier, named.astype(BF16)) + 1.0)
    state_ref[:, :routed] = probs
    select = slot_select(state_ref[...], rows, routed)
    gate = (ROUTE_SCALE * probs).astype(BF16)
    slot_gate = jnp.sum(
        jnp.where(slot_expert(rows, routed), dot_tn(select, gate), 0.0), axis=1, keepdims=True
    )
    rows_ref[:, :width] = dot_tn(select, grad_ref[...]).astype(BF16)
    rows_ref[:, width:] = jnp.broadcast_to(slot_gate, (rows, LANES)).astype(BF16)
    span = order_ref.shape[0]
    row = iota((span, span), 0)
    source = (span // LANES) * (row & (LANES - 1)) + row // LANES
    order_ref[...] = one_hot(source == iota((span, span), 1))


def decode_kernel(
    codes_ref, table_ref, hidden_ref, scale_ref, order_ref, plain_out_ref, out_ref, weight_ref
):
    unroll = 8
    step = pl.program_id(0)
    books, block, groups = codes_ref.shape
    entries = table_ref.shape[1]
    size = table_ref.shape[2]

    @pl.when(step == 0)
    def _():
        plain_out_ref[...] = jnp.zeros_like(plain_out_ref)

    hidden = spread_slots(hidden_ref[...], out_ref.shape[0])
    for chunk in range(groups // LANES):
        lanes = slice(chunk * LANES, (chunk + 1) * LANES)

        def decode_rows(index, carry):
            for member in range(unroll):
                at = pl.ds(pl.multiple_of((index * unroll + member) * 16, 16), 16)
                codes = [codes_ref[b, at, lanes].astype(I16) for b in range(books)]
                low = [c & I16(LANES - 1) for c in codes]
                part = [c >= I16(LANES) for c in codes]
                for i in range(size):
                    values = [
                        jnp.where(
                            part[b],
                            lane_gather(table_ref[b, 1, i], low[b]),
                            lane_gather(table_ref[b, 0, i], low[b]),
                        )
                        for b in range(books)
                    ]
                    weight_ref[at, i * LANES : (i + 1) * LANES] = sum(values[1:], values[0])
            return carry

        lax.fori_loop(0, block // 16 // unroll, decode_rows, 0)
        product = dot(hidden, weight_ref[...])
        for i in range(size):
            plain_out_ref[i, :, lanes] += product[:, i * LANES : (i + 1) * LANES]

    @pl.when(step == pl.num_programs(0) - 1)
    def _():
        rows = plain_out_ref.shape[1]
        split = [
            jnp.concatenate([plain_out_ref[i, :, at] * scale_ref[i : i + 1, at] for i in range(size)], 1)
            for at in (slice(c * LANES, (c + 1) * LANES) for c in range(groups // LANES))
        ]
        back = dot(jnp.concatenate(split, 0).astype(BF16), order_ref[...]).astype(BF16)
        span = size * LANES
        for chunk in range(groups // LANES):
            out_ref[:, chunk * span : (chunk + 1) * span] = back[chunk * rows : (chunk + 1) * rows]


def score_near_kernel(twist_ref, out_ref, slots_ref, router_ref, total_ref, base_ref):
    rows, width = out_ref.shape
    total_ref[...] = add_products(0, twist_ref[0], out_ref, router_ref, None)
    base = jnp.zeros((rows, LANES), F32)
    for c in range(width // LANES):
        at = slice(c * LANES, (c + 1) * LANES)
        base = base + slots_ref[:, at].astype(F32) * out_ref[:, at].astype(F32)
    base_ref[...] = jnp.broadcast_to(jnp.sum(base, axis=1, keepdims=True), (rows, LANES))


def add_products(far, twist, out_ref, router_ref, total):
    parts, later_count, routed, part_width = router_ref.shape
    for i in range(parts):
        first = (twist ^ (2 * i + far)) * part_width
        out = out_ref[:, pl.ds(pl.multiple_of(first, LANES), part_width)]
        product = dot_nt(router_ref[i].reshape(later_count * routed, part_width), out)
        total = product if total is None else total + product
    return total


def score_far_kernel(twist_ref, out_ref, router_ref, total_ref, base_ref, score_ref):
    rows = out_ref.shape[0]
    later_count, routed = router_ref.shape[1:3]
    wide = later_count * WIDE
    total = add_products(1, twist_ref[0], out_ref, router_ref, total_ref[...])
    score_ref[:, :wide] = jnp.zeros((rows, wide), BF16)
    for s in range(later_count):
        part = total[s * routed : (s + 1) * routed, :].T
        score_ref[:, s * WIDE : s * WIDE + routed] = part.astype(BF16)
    base = base_ref[...]
    high = base.astype(BF16).astype(F32)
    middle = (base - high).astype(BF16).astype(F32)
    low = base - high - middle
    column = iota((rows, LANES), 1)
    score_ref[:, wide:] = jnp.where(
        column == 0,
        high,
        jnp.where(column == 1, middle, jnp.where(column == 2, low, 0.0)),
    ).astype(BF16)


def response_kernel(routed, scores_ref, state_ref, *rest):
    *later_refs, response_ref = rest
    later_count = len(later_refs)
    rows, width = response_ref.shape
    experts = rows // SLOT
    select = slot_select(state_ref[...], rows, routed)
    column = iota((routed, width), 1)
    entry = iota((routed, width), 0)
    base_row, base_column = iota((LANES, width), 0), iota((LANES, width), 1)
    total = dot(
        scores_ref[:, later_count * WIDE :],
        one_hot((base_column - later_count * experts == base_row) & (base_row < 3)),
    )
    for s in range(later_count):
        probs = later_refs[s][:, :routed]
        high = probs.astype(BF16)
        low = (probs - high.astype(F32)).astype(BF16)
        picked = dot_tn(select, high) + dot_tn(select, low)
        product = scores_ref[:, s * WIDE : s * WIDE + routed].astype(F32)
        mean = jnp.sum(picked * product, axis=1, keepdims=True)
        response = (ROUTE_SCALE * picked * (product - mean)).astype(BF16)
        total = total + dot(
            response, one_hot((column - s * experts == entry) & (entry < experts))
        )
    response_ref[...] = total.astype(BF16)


def chain_kernel(routed, *refs):
    own_ref, later_ref, picked_ref = refs[-3:]
    count = (len(refs) - 3) // 2
    response_refs, state_refs = refs[:count], refs[count : 2 * count]
    rows, width = response_refs[0].shape
    tokens = state_refs[0].shape[0]
    experts = rows // SLOT
    column = iota((rows, width), 1)
    slot = iota((rows, width), 0)
    base = column >= (count - 1) * experts
    stacks = [jnp.zeros((tokens, width), F32) for _ in range(count)]
    own_select = None
    for s in range(count - 1, -1, -1):
        select = slot_select(state_refs[s][...], rows, routed)
        response = response_refs[s][...].astype(F32)
        terms = jnp.where(base, response, 0.0)
        if s < count - 1:
            terms = terms + dot_tn(select, stacks[s].astype(BF16)) * response
        score = jnp.sum(terms, axis=1, keepdims=True).astype(BF16).astype(F32)
        for u in range(s):
            first = (s - u - 1) * experts
            placed = jnp.where(column - first == slot // SLOT, score, 0.0).astype(BF16)
            stacks[u] = stacks[u] + dot(select, placed)
        placed = jnp.where(slot_expert(rows, routed), score, 0.0).astype(BF16)
        spread = dot(select, placed)
        probs = state_refs[s][:, :routed]
        weighted = jnp.sum(probs * spread, axis=1, keepdims=True)
        dlogit = (ROUTE_SCALE * probs * (spread - weighted)).astype(BF16)
        if s == 0:
            own_ref[...] = dlogit
            own_select = select
        else:
            later_ref[:, (s - 1) * WIDE : s * WIDE] = jnp.zeros((tokens, WIDE), BF16)
            later_ref[:, (s - 1) * WIDE : (s - 1) * WIDE + routed] = dlogit
    picked_ref[...] = dot_tn(own_select, later_ref[...]).astype(BF16)


def add_layers(current, later_ref, router_ref):
    later_count, routed = router_ref.shape[1:3]
    for s in range(later_count - 1, -1, -1):
        part = later_ref[:, s * WIDE : s * WIDE + routed]
        current = (current.astype(F32) + dot(part, router_ref[0, s])).astype(BF16)
    return current


def halves_of(twist, part_width):
    return [
        pl.ds(pl.multiple_of(((twist & 1) ^ far) * part_width, LANES), part_width)
        for far in range(2)
    ]


def finish_kernel(
    twist_ref, grad_ref, later_ref, own_ref, router_ref, near_ref, far_ref, result_ref
):
    places = halves_of(twist_ref[0], near_ref.shape[3])
    grads = [grad_ref[:, at] for at in places]
    routers = [router_ref[:, at] for at in places]
    results = []
    for grad, router, routers_ref in zip(grads, routers, (near_ref, far_ref)):
        current = add_layers(grad, later_ref, routers_ref)
        results.append((current.astype(F32) + dot(own_ref[...], router)).astype(BF16))
    for at, result in zip(places, results):
        result_ref[:, at] = result


def slots_kernel(
    twist_ref, slots_ref, gates_ref, later_ref, near_ref, far_ref, plain_out_ref, order_ref,
    split_ref, scale_grad_ref, grad_ref
):
    i = pl.program_id(0)
    part_width = near_ref.shape[3]
    size, _, groups = plain_out_ref.shape
    span = size * LANES
    twist = twist_ref[0]
    pair = ((twist >> 1) ^ i) * 2
    gate = gates_ref[:, :1].astype(F32)
    places = halves_of(twist, part_width)
    slots = [slots_ref[:, at] for at in places]
    grads = [
        (gate * add_layers(part, later_ref, routers_ref).astype(F32)).astype(BF16)
        for part, routers_ref in zip(slots, (near_ref, far_ref))
    ]
    for far in range(2):
        first = (pair + ((twist & 1) ^ far)) * part_width
        grad_ref[:, pl.ds(pl.multiple_of(first, LANES), part_width)] = grads[far]

    @pl.when(i == pl.num_programs(0) - 1)
    def _():
        rows = grad_ref.shape[0]
        chunks = groups // LANES
        grad = [grad_ref[:, c * span : (c + 1) * span] for c in range(chunks)]
        split = dot_nt(jnp.concatenate(grad, 0), order_ref[...])
        for c in range(chunks):
            lanes = slice(c * LANES, (c + 1) * LANES)
            for i in range(size):
                part = split[c * rows : (c + 1) * rows, i * LANES : (i + 1) * LANES]
                split_ref[i, :, lanes] = part.astype(BF16)
                scale_grad_ref[i : i + 1, lanes] = jnp.sum(
                    part * plain_out_ref[i, :, lanes], axis=0, keepdims=True
                )


def book_kernel(
    unroll, hidden_ref, slots_ref, scale_ref, codes_ref, out_ref, grad_ref, pair_ref
):
    books, block, groups = codes_ref.shape
    size = slots_ref.shape[0]
    chunks = groups // LANES

    @pl.when(pl.program_id(0) == 0)
    def _():
        out_ref[...] = jnp.zeros_like(out_ref)

    hidden = spread_slots(hidden_ref[...], slots_ref.shape[1])
    for i in range(size):
        grad = dot_tn(hidden, slots_ref[i]) * scale_ref[i : i + 1, :]
        for c in range(chunks):
            grad_ref[c, pl.ds(i, block, stride=size), :] = grad[:, c * LANES : (c + 1) * LANES]
    for b in range(books):
        for c in range(chunks):
            codes = codes_ref[b, :, c * LANES : (c + 1) * LANES]
            high = (codes * (65536 // LOW + 1)) >> 16
            pair_ref[b, c] = high * 8 + (codes - high * LOW)
    row = iota((16, LANES), 0)
    high_rows = [(row + 16 * k).astype(I16) for k in range(HIGH // 16)]
    low_rows = [((row >> 3) + 2 * k).astype(I16) for k in range(LOW // 2)]
    one = jnp.ones((16, LANES), BF16)
    zero = jnp.zeros((16, LANES), BF16)

    def add_rows(index, totals):
        totals = list(totals)
        for pair in range(unroll // 2):
            left = [[] for _ in range(books)]
            right = [[] for _ in range(books)]
            for member in range(2):
                f = index * unroll + pair * 2 + member
                at = pl.ds(pl.multiple_of(f * size, size), size)
                for c in range(chunks):
                    values = grad_ref[c, at, :]
                    values = jnp.concatenate([values, values], 0).astype(BF16)
                    for b in range(books):
                        pairs = pair_ref[b, c, pl.ds(f, 8, stride=0), :]
                        pairs = jnp.concatenate([pairs, pairs], 0).astype(I16)
                        high = pairs >> I16(3)
                        low = pairs & I16(7)
                        left[b].append(
                            jnp.concatenate([jnp.where(high == r, one, zero) for r in high_rows], 0)
                        )
                        right[b].append(
                            jnp.concatenate([jnp.where(low == r, values, zero) for r in low_rows], 0)
                        )
            for b in range(books):
                totals[b] = totals[b] + dot_nt(
                    jnp.concatenate(left[b], 1), jnp.concatenate(right[b], 1)
                )
        return tuple(totals)

    start = tuple(jnp.zeros(out_ref.shape[1:], F32) for _ in range(books))
    totals = lax.fori_loop(0, block // unroll, add_rows, start)
    for b in range(books):
        out_ref[b] += totals[b]


def whole(shape):
    return pl.BlockSpec(shape, lambda *_: (0,) * len(shape))


def exchange(value):
    return lax.all_to_all(value, "expert", split_axis=0, concat_axis=0, tiled=True)


def swap(value, distance):
    count = lax.axis_size("expert")
    return lax.ppermute(value, "expert", [(i, i ^ distance) for i in range(count)])


def pass_down(value, layers):
    return [
        lax.ppermute(value, "pipe", [(p, p - s) for p in range(s, layers)])
        for s in range(1, layers)
    ]


def join_kernel(*refs):
    *part_refs, out_ref = refs
    for k, ref in enumerate(part_refs):
        out_ref[k] = ref[...]


def join(parts):
    return pl.pallas_call(
        join_kernel,
        out_shape=jax.ShapeDtypeStruct((len(parts),) + parts[0].shape, parts[0].dtype),
        compiler_params=params(60),
        name="join",
    )(*parts)


def exchange_near(shares):
    count = lax.axis_size("expert")
    return [shares] + [swap(shares, d) for d in range(2, count, 2)]


def on_device(out_grad, saved_inputs, router, routes, hidden_saved, codes, codebook, scale):
    experts = lax.axis_size("expert")
    layers = lax.axis_size("pipe")
    place = lax.axis_index("expert")
    tokens, width = out_grad.shape
    routed = router.shape[2]
    codes = codes[0, 0]
    codebook = codebook[0, 0]
    hidden = hidden_saved[0, 0]
    inner = hidden.shape[1]
    books, _, groups = codes.shape
    entries, size = codebook.shape[1:]
    rows = experts * SLOT
    later_count = layers - 1
    wide = later_count * WIDE
    grow = max(1, rows // 128)
    router_t = router[0].T
    scale_split = scale[0, 0].reshape(groups, size).T

    parts = math.gcd(width // LANES, experts)
    direct = parts == experts
    sharers = experts // parts
    part_width = width // parts
    share_rows = routed // sharers
    own_share = lax.dynamic_slice(
        router_t,
        ((place % sharers) * share_rows, (place // sharers) * part_width),
        (share_rows, part_width),
    )
    shares = join(pass_down(own_share, layers))
    twist = jnp.full((1,), place if direct else 0, jnp.int32)

    logits = dot(saved_inputs[0], router[0])
    state_width = -(-(routed + experts) // LANES) * LANES
    span = size * LANES
    state, outgoing, order = pl.pallas_call(
        prepare_kernel,
        out_shape=(
            jax.ShapeDtypeStruct((tokens, state_width), F32),
            jax.ShapeDtypeStruct((rows, width + LANES), BF16),
            jax.ShapeDtypeStruct((span, span), BF16),
        ),
        compiler_params=params(20 + 6 * grow),
        name="prepare",
    )(logits, routes[0], out_grad)
    slots = exchange(outgoing)
    hidden, outgoing, scale_split = lax.optimization_barrier((hidden, outgoing, scale_split))

    halves = entries // LANES
    table = codebook.transpose(0, 2, 1).reshape(books, size, halves, LANES)
    table = jnp.broadcast_to(
        table.transpose(0, 2, 1, 3)[:, :, :, None, :], (books, halves, size, 16, LANES)
    )
    block = 128

    blocks = inner // block

    def decode():
        return pl.pallas_call(
            decode_kernel,
            grid=(blocks,),
            in_specs=[
                pl.BlockSpec((books, block, groups), lambda s: (0, s, 0)),
                whole((books, halves, size, 16, LANES)),
                pl.BlockSpec((experts * MOST, block), lambda s: (0, s)),
                whole((size, groups)),
                whole((span, span)),
            ],
            out_specs=[whole((size, rows, groups)), whole((rows, width))],
            out_shape=[
                jax.ShapeDtypeStruct((size, rows, groups), F32),
                jax.ShapeDtypeStruct((rows, width), BF16),
            ],
            scratch_shapes=[pltpu.VMEM((block, size * LANES), BF16)],
            compiler_params=params(60),
            cost_estimate=pl.CostEstimate(
                flops=blocks * 5_000_000_000, bytes_accessed=10_000_000, transcendentals=0
            ),
            name="decode",
        )(codes, table, hidden, scale_split, order)

    later_states = pass_down(state, layers)
    hidden, shares, farthest = lax.optimization_barrier((hidden, shares, later_states[-1]))
    near = exchange_near(shares) if direct else None
    states = [state] + later_states[:-1] + [farthest]
    plain_out, expert_out = decode()
    if direct:
        near = join(near)
        plain_out, expert_out, near, slots, states = lax.optimization_barrier(
            (plain_out, expert_out, near, slots, states)
        )
        far = swap(near, 1)
    else:
        routers = lax.all_gather(shares, "expert", axis=0, tiled=False)
        routers = routers.reshape(parts, sharers, later_count, share_rows, part_width)
        routers = routers.transpose(0, 2, 1, 3, 4)
        routers = routers.reshape(parts, later_count, routed, part_width)
        near, far = routers[0::2], routers[1::2]

    grid = (parts // 2,)

    def columns(height):
        return pl.BlockSpec((height, 2 * part_width), lambda i, t: (0, (t[0] >> 1) ^ i))

    router_spec = pl.BlockSpec((1, later_count, routed, part_width), lambda i, t: (i, 0, 0, 0))

    def by_columns(kernel, in_specs, out_specs, out_shape, scratch, name):
        return pl.pallas_call(
            kernel,
            grid_spec=pltpu.PrefetchScalarGridSpec(
                num_scalar_prefetch=1,
                grid=grid,
                in_specs=in_specs,
                out_specs=out_specs,
                scratch_shapes=scratch,
            ),
            out_shape=out_shape,
            compiler_params=params(60),
            name=name,
        )

    def score(kernel, operands, out_shape):
        return pl.pallas_call(
            kernel,
            grid_spec=pltpu.PrefetchScalarGridSpec(
                num_scalar_prefetch=1,
                grid=(1,),
                in_specs=[whole(a.shape) for a in operands],
                out_specs=jax.tree.map(lambda a: whole(a.shape), out_shape),
            ),
            out_shape=out_shape,
            compiler_params=params(60),
            name="scores",
        )(twist, *operands)

    sums = [
        jax.ShapeDtypeStruct((later_count * routed, rows), F32),
        jax.ShapeDtypeStruct((rows, LANES), F32),
    ]
    sums = score(score_near_kernel, [expert_out, slots, near], sums)
    scores = exchange(
        score(
            score_far_kernel,
            [expert_out, far, *sums],
            jax.ShapeDtypeStruct((rows, wide + LANES), BF16),
        )
    )

    response_width = -(-(later_count * experts + 3) // LANES) * LANES
    response = pl.pallas_call(
        functools.partial(response_kernel, routed),
        out_shape=jax.ShapeDtypeStruct((rows, response_width), BF16),
        compiler_params=params(12 + 4 * grow),
        name="responses",
    )(scores, *states)
    own, later, picked = pl.pallas_call(
        functools.partial(chain_kernel, routed),
        out_shape=(
            jax.ShapeDtypeStruct((tokens, routed), BF16),
            jax.ShapeDtypeStruct((tokens, wide), BF16),
            jax.ShapeDtypeStruct((rows, wide), BF16),
        ),
        compiler_params=params(12 + 4 * grow),
        name="chain",
    )(response, *pass_down(response, layers), *states)

    slot_later = exchange(picked)

    result = by_columns(
        finish_kernel,
        [
            columns(tokens),
            whole((tokens, wide)),
            whole((tokens, routed)),
            columns(routed),
            router_spec,
            router_spec,
        ],
        columns(tokens),
        jax.ShapeDtypeStruct((tokens, width), BF16),
        [],
        "finish",
    )(twist, out_grad, later, own, router_t, near, far)

    slot_split, scale_grad = by_columns(
        slots_kernel,
        [
            columns(rows),
            pl.BlockSpec((rows, LANES), lambda *_: (0, width // LANES)),
            whole((rows, wide)),
            router_spec,
            router_spec,
            whole((size, rows, groups)),
            whole((span, span)),
        ],
        [whole((size, rows, groups)), whole((size, groups))],
        [
            jax.ShapeDtypeStruct((size, rows, groups), BF16),
            jax.ShapeDtypeStruct((size, groups), F32),
        ],
        [pltpu.VMEM((rows, width), BF16)],
        "slot_grads",
    )(twist, slots, slots, slot_later, near, far, plain_out, order)

    block = 128
    unroll = 64
    book_grad = pl.pallas_call(
        functools.partial(book_kernel, unroll),
        grid=(inner // block,),
        in_specs=[
            pl.BlockSpec((experts * MOST, block), lambda s: (0, s)),
            whole((size, rows, groups)),
            whole((size, groups)),
            pl.BlockSpec((books, block, groups), lambda s: (0, s, 0)),
        ],
        out_specs=whole((books, HIGH, LOW * size)),
        out_shape=jax.ShapeDtypeStruct((books, HIGH, LOW * size), F32),
        scratch_shapes=[
            pltpu.VMEM((groups // LANES, block * size, LANES), F32),
            pltpu.VMEM((books, groups // LANES, block, LANES), jnp.int32),
        ],
        compiler_params=params(60),
        name="book_grads",
    )(hidden, slot_split, scale_split, codes)

    book_grad = book_grad.reshape(books, HIGH * LOW, size)[:, :entries]
    scale_grad = scale_grad.T.reshape(width)
    return (result[None], book_grad[None, None], scale_grad[None, None])


def solution(mesh):
    placed = (
        P("expert", None),
        P("pipe", "expert", None),
        P("pipe", None, None),
        P("pipe", "expert", None),
        P("pipe", "expert", None, None),
        P("pipe", "expert", None, None, None),
        P("pipe", "expert", None, None, None),
        P("pipe", "expert", None),
    )
    return jax.shard_map(
        on_device,
        mesh=mesh,
        in_specs=placed,
        out_specs=(
            P("pipe", "expert", None),
            P("pipe", "expert", None, None, None),
            P("pipe", "expert", None),
        ),
        check_vma=False,
    )
```

```python
import functools
import math

import jax
import jax.numpy as jnp
from jax import lax
from jax.experimental import pallas as pl
from jax.experimental.pallas import tpu as pltpu
from jax.sharding import PartitionSpec as P

MOST = 9
SLOT = 16
ROUTE_SCALE = 16.0
LANES = 128
WIDE = 256
LOW = 6
HIGH = 48
F32 = jnp.float32
BF16 = jnp.bfloat16
I16 = jnp.int16


def params(mib):
    return pltpu.CompilerParams(vmem_limit_bytes=mib << 20)


def dot(a, b):
    return jnp.dot(a, b, preferred_element_type=F32)


def dot_nt(a, b):
    return lax.dot_general(a, b, (((1,), (1,)), ((), ())), preferred_element_type=F32)


def dot_tn(a, b):
    return lax.dot_general(a, b, (((0,), (0,)), ((), ())), preferred_element_type=F32)


def iota(shape, axis):
    return lax.broadcasted_iota(jnp.int32, shape, axis)


def lane_gather(table, index):
    return lax.gather(
        table,
        index[..., None],
        lax.GatherDimensionNumbers(
            offset_dims=(),
            collapsed_slice_dims=(1,),
            start_index_map=(1,),
            operand_batching_dims=(0,),
            start_indices_batching_dims=(0,),
        ),
        slice_sizes=(1, 1),
        mode=lax.GatherScatterMode.PROMISE_IN_BOUNDS,
    )


def slot_expert(rows, columns):
    return iota((rows, columns), 0) // SLOT == iota((rows, columns), 1)


def one_hot(mask):
    return mask.astype(F32).astype(BF16)


def spread_slots(hidden, rows):
    row = iota((rows, hidden.shape[0]), 0)
    place = row % SLOT
    source = iota((rows, hidden.shape[0]), 1)
    spread = one_hot((row // SLOT * MOST + place == source) & (place < MOST))
    return dot(spread, hidden).astype(BF16)


def slot_select(state, rows, routed):
    tokens, width = state.shape
    number = jnp.where(iota((tokens, width), 1) >= routed, state, 0.0).astype(BF16)
    owner = iota((width, rows), 0) - routed == iota((width, rows), 1) // SLOT
    place = (iota((tokens, rows), 1) % SLOT + 1).astype(F32)
    return one_hot(jnp.abs(dot(number, one_hot(owner)) - place) < 0.5)


def prepare_kernel(logits_ref, routes_ref, grad_ref, state_ref, rows_ref):
    tokens, routed = logits_ref.shape
    top = routes_ref.shape[1]
    width = grad_ref.shape[1]
    rows = rows_ref.shape[0]
    experts = rows // SLOT
    state_width = state_ref.shape[1]
    raised = jnp.exp(logits_ref[...])
    probs = raised / jnp.sum(raised, axis=1, keepdims=True)
    expert = iota((tokens, state_width), 1) - routed
    named = jnp.zeros((tokens, state_width), F32)
    for k in range(top):
        named = named + (routes_ref[:, k : k + 1] == expert).astype(F32)
    named = jnp.where(expert < experts, named, 0.0)
    earlier = one_hot(iota((tokens, tokens), 1) < iota((tokens, tokens), 0))
    state_ref[...] = named * (dot(earlier, named.astype(BF16)) + 1.0)
    state_ref[:, :routed] = probs
    select = slot_select(state_ref[...], rows, routed)
    gate = (ROUTE_SCALE * probs).astype(BF16)
    slot_gate = jnp.sum(
        jnp.where(slot_expert(rows, routed), dot_tn(select, gate), 0.0), axis=1, keepdims=True
    )
    rows_ref[:, :width] = dot_tn(select, grad_ref[...]).astype(BF16)
    rows_ref[:, width:] = jnp.broadcast_to(slot_gate, (rows, LANES)).astype(BF16)


def order_kernel(after_ref, order_ref):
    span = order_ref.shape[0]
    row = iota((span, span), 0)
    source = (span // LANES) * (row & (LANES - 1)) + row // LANES
    order_ref[...] = one_hot(source == iota((span, span), 1))


def decode_kernel(
    codes_ref, table_ref, hidden_ref, scale_ref, order_ref, plain_out_ref, out_ref, weight_ref
):
    unroll = 8
    step = pl.program_id(0)
    books, block, groups = codes_ref.shape
    entries = table_ref.shape[1]
    size = table_ref.shape[2]

    @pl.when(step == 0)
    def _():
        plain_out_ref[...] = jnp.zeros_like(plain_out_ref)

    hidden = spread_slots(hidden_ref[...], out_ref.shape[0])
    for chunk in range(groups // LANES):
        lanes = slice(chunk * LANES, (chunk + 1) * LANES)

        def decode_rows(index, carry):
            for member in range(unroll):
                at = pl.ds(pl.multiple_of((index * unroll + member) * 16, 16), 16)
                codes = [codes_ref[b, at, lanes].astype(I16) for b in range(books)]
                low = [c & I16(LANES - 1) for c in codes]
                part = [c >= I16(LANES) for c in codes]
                for i in range(size):
                    values = [
                        jnp.where(
                            part[b],
                            lane_gather(table_ref[b, 1, i], low[b]),
                            lane_gather(table_ref[b, 0, i], low[b]),
                        )
                        for b in range(books)
                    ]
                    weight_ref[at, i * LANES : (i + 1) * LANES] = sum(values[1:], values[0])
            return carry

        lax.fori_loop(0, block // 16 // unroll, decode_rows, 0)
        product = dot(hidden, weight_ref[...])
        for i in range(size):
            plain_out_ref[i, :, lanes] += product[:, i * LANES : (i + 1) * LANES]

    @pl.when(step == pl.num_programs(0) - 1)
    def _():
        rows = plain_out_ref.shape[1]
        split = [
            jnp.concatenate([plain_out_ref[i, :, at] * scale_ref[i : i + 1, at] for i in range(size)], 1)
            for at in (slice(c * LANES, (c + 1) * LANES) for c in range(groups // LANES))
        ]
        back = dot(jnp.concatenate(split, 0).astype(BF16), order_ref[...]).astype(BF16)
        span = size * LANES
        for chunk in range(groups // LANES):
            out_ref[:, chunk * span : (chunk + 1) * span] = back[chunk * rows : (chunk + 1) * rows]


def score_near_kernel(twist_ref, out_ref, slots_ref, router_ref, total_ref, base_ref):
    rows, width = out_ref.shape
    total_ref[...] = add_products(0, twist_ref[0], out_ref, router_ref, None)
    base = jnp.zeros((rows, LANES), F32)
    for c in range(width // LANES):
        at = slice(c * LANES, (c + 1) * LANES)
        base = base + slots_ref[:, at].astype(F32) * out_ref[:, at].astype(F32)
    base_ref[...] = jnp.broadcast_to(jnp.sum(base, axis=1, keepdims=True), (rows, LANES))


def add_products(far, twist, out_ref, router_ref, total):
    parts, later_count, routed, part_width = router_ref.shape
    for i in range(parts):
        first = (twist ^ (2 * i + far)) * part_width
        out = out_ref[:, pl.ds(pl.multiple_of(first, LANES), part_width)]
        product = dot_nt(router_ref[i].reshape(later_count * routed, part_width), out)
        total = product if total is None else total + product
    return total


def score_far_kernel(twist_ref, out_ref, router_ref, total_ref, base_ref, score_ref):
    rows = out_ref.shape[0]
    later_count, routed = router_ref.shape[1:3]
    wide = later_count * routed
    total = add_products(1, twist_ref[0], out_ref, router_ref, total_ref[...])
    tail = jnp.zeros((score_ref.shape[1] - wide, rows), F32)
    total = jnp.concatenate([total, tail], 0).T
    base = base_ref[:, :1]
    high = base.astype(BF16).astype(F32)
    middle = (base - high).astype(BF16).astype(F32)
    low = base - high - middle
    column = iota(total.shape, 1) - wide
    for place, part in enumerate((high, middle, low)):
        total = jnp.where(column == place, part, total)
    score_ref[...] = total.astype(BF16)


def response_kernel(routed, scores_ref, state_ref, *rest):
    *later_refs, response_ref = rest
    later_count = len(later_refs)
    rows, width = response_ref.shape
    experts = rows // SLOT
    select = slot_select(state_ref[...], rows, routed)
    column = iota((routed, width), 1)
    entry = iota((routed, width), 0)
    base_row, base_column = iota((LANES, width), 0), iota((LANES, width), 1)
    last = scores_ref.shape[1] - LANES
    base_row = base_row + last - later_count * routed
    total = dot(
        scores_ref[:, last:],
        one_hot(
            (base_column - later_count * experts == base_row) & (base_row >= 0) & (base_row < 3)
        ),
    )
    for s in range(later_count):
        probs = later_refs[s][:, :routed]
        high = probs.astype(BF16)
        low = (probs - high.astype(F32)).astype(BF16)
        picked = dot_tn(select, high) + dot_tn(select, low)
        product = scores_ref[:, s * routed : (s + 1) * routed].astype(F32)
        mean = jnp.sum(picked * product, axis=1, keepdims=True)
        response = (ROUTE_SCALE * picked * (product - mean)).astype(BF16)
        total = total + dot(
            response, one_hot((column - s * experts == entry) & (entry < experts))
        )
    response_ref[...] = total.astype(BF16)


def chain_kernel(routed, *refs):
    own_ref, later_ref, picked_ref = refs[-3:]
    count = (len(refs) - 3) // 2
    response_refs, state_refs = refs[:count], refs[count : 2 * count]
    rows, width = response_refs[0].shape
    tokens = state_refs[0].shape[0]
    experts = rows // SLOT
    column = iota((rows, width), 1)
    slot = iota((rows, width), 0)
    base = column >= (count - 1) * experts
    stacks = [jnp.zeros((tokens, width), F32) for _ in range(count)]
    own_select = None
    for s in range(count - 1, -1, -1):
        select = slot_select(state_refs[s][...], rows, routed)
        response = response_refs[s][...].astype(F32)
        terms = jnp.where(base, response, 0.0)
        if s < count - 1:
            terms = terms + dot_tn(select, stacks[s].astype(BF16)) * response
        score = jnp.sum(terms, axis=1, keepdims=True).astype(BF16).astype(F32)
        for u in range(s):
            first = (s - u - 1) * experts
            placed = jnp.where(column - first == slot // SLOT, score, 0.0).astype(BF16)
            stacks[u] = stacks[u] + dot(select, placed)
        placed = jnp.where(slot_expert(rows, routed), score, 0.0).astype(BF16)
        spread = dot(select, placed)
        probs = state_refs[s][:, :routed]
        weighted = jnp.sum(probs * spread, axis=1, keepdims=True)
        dlogit = (ROUTE_SCALE * probs * (spread - weighted)).astype(BF16)
        if s == 0:
            own_ref[...] = dlogit
            own_select = select
        else:
            later_ref[:, (s - 1) * WIDE : s * WIDE] = jnp.zeros((tokens, WIDE), BF16)
            later_ref[:, (s - 1) * WIDE : (s - 1) * WIDE + routed] = dlogit
    picked_ref[...] = dot_tn(own_select, later_ref[...]).astype(BF16)


def add_layers(current, later_ref, router_ref):
    later_count, routed = router_ref.shape[1:3]
    for s in range(later_count - 1, -1, -1):
        part = later_ref[:, s * WIDE : s * WIDE + routed]
        current = (current.astype(F32) + dot(part, router_ref[0, s])).astype(BF16)
    return current


def halves_of(twist, part_width):
    return [
        pl.ds(pl.multiple_of(((twist & 1) ^ far) * part_width, LANES), part_width)
        for far in range(2)
    ]


def finish_kernel(
    twist_ref, grad_ref, later_ref, own_ref, router_ref, near_ref, far_ref, result_ref
):
    places = halves_of(twist_ref[0], near_ref.shape[3])
    grads = [grad_ref[:, at] for at in places]
    routers = [router_ref[:, at] for at in places]
    results = []
    for grad, router, routers_ref in zip(grads, routers, (near_ref, far_ref)):
        current = add_layers(grad, later_ref, routers_ref)
        results.append((current.astype(F32) + dot(own_ref[...], router)).astype(BF16))
    for at, result in zip(places, results):
        result_ref[:, at] = result


def slots_kernel(
    twist_ref, slots_ref, gates_ref, later_ref, near_ref, far_ref, plain_out_ref, order_ref,
    split_ref, scale_grad_ref, grad_ref
):
    i = pl.program_id(0)
    part_width = near_ref.shape[3]
    size, _, groups = plain_out_ref.shape
    span = size * LANES
    twist = twist_ref[0]
    pair = ((twist >> 1) ^ i) * 2
    gate = gates_ref[:, :1].astype(F32)
    places = halves_of(twist, part_width)
    slots = [slots_ref[:, at] for at in places]
    grads = [
        (gate * add_layers(part, later_ref, routers_ref).astype(F32)).astype(BF16)
        for part, routers_ref in zip(slots, (near_ref, far_ref))
    ]
    for far in range(2):
        first = (pair + ((twist & 1) ^ far)) * part_width
        grad_ref[:, pl.ds(pl.multiple_of(first, LANES), part_width)] = grads[far]

    @pl.when(i == pl.num_programs(0) - 1)
    def _():
        rows = grad_ref.shape[0]
        chunks = groups // LANES
        grad = [grad_ref[:, c * span : (c + 1) * span] for c in range(chunks)]
        split = dot_nt(jnp.concatenate(grad, 0), order_ref[...])
        for c in range(chunks):
            lanes = slice(c * LANES, (c + 1) * LANES)
            for i in range(size):
                part = split[c * rows : (c + 1) * rows, i * LANES : (i + 1) * LANES]
                split_ref[i, :, lanes] = part.astype(BF16)
                scale_grad_ref[i : i + 1, lanes] = jnp.sum(
                    part * plain_out_ref[i, :, lanes], axis=0, keepdims=True
                )


def book_kernel(
    unroll, hidden_ref, slots_ref, scale_ref, codes_ref, out_ref, grad_ref, pair_ref
):
    books, block, groups = codes_ref.shape
    size = slots_ref.shape[0]
    chunks = groups // LANES

    @pl.when(pl.program_id(0) == 0)
    def _():
        out_ref[...] = jnp.zeros_like(out_ref)

    hidden = spread_slots(hidden_ref[...], slots_ref.shape[1])
    for i in range(size):
        grad = dot_tn(hidden, slots_ref[i]) * scale_ref[i : i + 1, :]
        for c in range(chunks):
            grad_ref[c, pl.ds(i, block, stride=size), :] = grad[:, c * LANES : (c + 1) * LANES]
    for b in range(books):
        for c in range(chunks):
            codes = codes_ref[b, :, c * LANES : (c + 1) * LANES]
            high = (codes * (65536 // LOW + 1)) >> 16
            pair_ref[b, c] = high * 8 + (codes - high * LOW)
    row = iota((16, LANES), 0)
    high_rows = [(row + 16 * k).astype(I16) for k in range(HIGH // 16)]
    low_rows = [((row >> 3) + 2 * k).astype(I16) for k in range(LOW // 2)]
    one = jnp.ones((16, LANES), BF16)
    zero = jnp.zeros((16, LANES), BF16)

    def add_rows(index, totals):
        totals = list(totals)
        for pair in range(unroll // 2):
            left = [[] for _ in range(books)]
            right = [[] for _ in range(books)]
            for member in range(2):
                f = index * unroll + pair * 2 + member
                at = pl.ds(pl.multiple_of(f * size, size), size)
                for c in range(chunks):
                    values = grad_ref[c, at, :]
                    values = jnp.concatenate([values, values], 0).astype(BF16)
                    for b in range(books):
                        pairs = pair_ref[b, c, pl.ds(f, 8, stride=0), :]
                        pairs = jnp.concatenate([pairs, pairs], 0).astype(I16)
                        high = pairs >> I16(3)
                        low = pairs & I16(7)
                        left[b].append(
                            jnp.concatenate([jnp.where(high == r, one, zero) for r in high_rows], 0)
                        )
                        right[b].append(
                            jnp.concatenate([jnp.where(low == r, values, zero) for r in low_rows], 0)
                        )
            for b in range(books):
                totals[b] = totals[b] + dot_nt(
                    jnp.concatenate(left[b], 1), jnp.concatenate(right[b], 1)
                )
        return tuple(totals)

    start = tuple(jnp.zeros(out_ref.shape[1:], F32) for _ in range(books))
    totals = lax.fori_loop(0, block // unroll, add_rows, start)
    for b in range(books):
        out_ref[b] += totals[b]


def whole(shape):
    return pl.BlockSpec(shape, lambda *_: (0,) * len(shape))


def exchange(value):
    return lax.all_to_all(value, "expert", split_axis=0, concat_axis=0, tiled=True)


def swap(value, distance):
    count = lax.axis_size("expert")
    return lax.ppermute(value, "expert", [(i, i ^ distance) for i in range(count)])


def pass_down(value, layers):
    return [
        lax.ppermute(value, "pipe", [(p, p - s) for p in range(s, layers)])
        for s in range(1, layers)
    ]


def join_kernel(*refs):
    *part_refs, out_ref = refs
    for k, ref in enumerate(part_refs):
        out_ref[k] = ref[...]


def join(parts):
    return pl.pallas_call(
        join_kernel,
        out_shape=jax.ShapeDtypeStruct((len(parts),) + parts[0].shape, parts[0].dtype),
        compiler_params=params(60),
        name="join",
    )(*parts)


def exchange_near(shares):
    count = lax.axis_size("expert")
    return [shares] + [swap(shares, d) for d in range(2, count, 2)]


def on_device(out_grad, saved_inputs, router, routes, hidden_saved, codes, codebook, scale):
    experts = lax.axis_size("expert")
    layers = lax.axis_size("pipe")
    place = lax.axis_index("expert")
    tokens, width = out_grad.shape
    routed = router.shape[2]
    codes = codes[0, 0]
    codebook = codebook[0, 0]
    hidden = hidden_saved[0, 0]
    inner = hidden.shape[1]
    books, _, groups = codes.shape
    entries, size = codebook.shape[1:]
    rows = experts * SLOT
    later_count = layers - 1
    wide = later_count * WIDE
    grow = max(1, rows // 128)
    router_t = router[0].T
    scale_split = scale[0, 0].reshape(groups, size).T

    parts = math.gcd(width // LANES, experts)
    direct = parts == experts
    sharers = experts // parts
    part_width = width // parts
    share_rows = routed // sharers
    own_share = lax.dynamic_slice(
        router_t,
        ((place % sharers) * share_rows, (place // sharers) * part_width),
        (share_rows, part_width),
    )
    shares = join(pass_down(own_share, layers))
    twist = jnp.full((1,), place if direct else 0, jnp.int32)

    logits = dot(saved_inputs[0], router[0])
    state_width = -(-(routed + experts) // LANES) * LANES
    span = size * LANES
    state, outgoing = pl.pallas_call(
        prepare_kernel,
        out_shape=(
            jax.ShapeDtypeStruct((tokens, state_width), F32),
            jax.ShapeDtypeStruct((rows, width + LANES), BF16),
        ),
        compiler_params=params(20 + 6 * grow),
        name="prepare",
    )(logits, routes[0], out_grad)
    slots = exchange(outgoing)
    hidden, outgoing = lax.optimization_barrier((hidden, outgoing))

    halves = entries // LANES
    table = codebook.transpose(0, 2, 1).reshape(books, size, halves, LANES)
    table = jnp.broadcast_to(
        table.transpose(0, 2, 1, 3)[:, :, :, None, :], (books, halves, size, 16, LANES)
    )
    block = 128

    blocks = inner // block

    later_states = pass_down(state, layers)
    hidden, shares, farthest = lax.optimization_barrier((hidden, shares, later_states[-1]))
    near = exchange_near(shares) if direct else None
    states = [state] + later_states[:-1] + [farthest]
    order = pl.pallas_call(
        order_kernel,
        in_specs=[pl.BlockSpec(memory_space=pl.ANY)],
        out_shape=jax.ShapeDtypeStruct((span, span), BF16),
        compiler_params=params(60),
        name="order",
    )(hidden)
    def decode():
        return pl.pallas_call(
            decode_kernel,
            grid=(blocks,),
            in_specs=[
                pl.BlockSpec((books, block, groups), lambda s: (0, s, 0)),
                whole((books, halves, size, 16, LANES)),
                pl.BlockSpec((experts * MOST, block), lambda s: (0, s)),
                whole((size, groups)),
                whole((span, span)),
            ],
            out_specs=[whole((size, rows, groups)), whole((rows, width))],
            out_shape=[
                jax.ShapeDtypeStruct((size, rows, groups), F32),
                jax.ShapeDtypeStruct((rows, width), BF16),
            ],
            scratch_shapes=[pltpu.VMEM((block, size * LANES), BF16)],
            compiler_params=params(60),
            cost_estimate=pl.CostEstimate(
                flops=blocks * 5_000_000_000, bytes_accessed=10_000_000, transcendentals=0
            ),
            name="decode",
        )(codes, table, hidden, scale_split, order)

    plain_out, expert_out = decode()
    if direct:
        near = join(near)
        plain_out, expert_out, near, slots, states = lax.optimization_barrier(
            (plain_out, expert_out, near, slots, states)
        )
        far = swap(near, 1)
    else:
        routers = lax.all_gather(shares, "expert", axis=0, tiled=False)
        routers = routers.reshape(parts, sharers, later_count, share_rows, part_width)
        routers = routers.transpose(0, 2, 1, 3, 4)
        routers = routers.reshape(parts, later_count, routed, part_width)
        near, far = routers[0::2], routers[1::2]

    grid = (parts // 2,)

    def columns(height):
        return pl.BlockSpec((height, 2 * part_width), lambda i, t: (0, (t[0] >> 1) ^ i))

    router_spec = pl.BlockSpec((1, later_count, routed, part_width), lambda i, t: (i, 0, 0, 0))

    def by_columns(kernel, in_specs, out_specs, out_shape, scratch, name):
        return pl.pallas_call(
            kernel,
            grid_spec=pltpu.PrefetchScalarGridSpec(
                num_scalar_prefetch=1,
                grid=grid,
                in_specs=in_specs,
                out_specs=out_specs,
                scratch_shapes=scratch,
            ),
            out_shape=out_shape,
            compiler_params=params(60),
            name=name,
        )

    def score(kernel, operands, out_shape):
        return pl.pallas_call(
            kernel,
            grid_spec=pltpu.PrefetchScalarGridSpec(
                num_scalar_prefetch=1,
                grid=(1,),
                in_specs=[whole(a.shape) for a in operands],
                out_specs=jax.tree.map(lambda a: whole(a.shape), out_shape),
            ),
            out_shape=out_shape,
            compiler_params=params(60),
            name="scores",
        )(twist, *operands)

    score_width = -(-(later_count * routed + 3) // LANES) * LANES
    sums = [
        jax.ShapeDtypeStruct((later_count * routed, rows), F32),
        jax.ShapeDtypeStruct((rows, LANES), F32),
    ]
    sums = score(score_near_kernel, [expert_out, slots, near], sums)
    scores = exchange(
        score(
            score_far_kernel,
            [expert_out, far, *sums],
            jax.ShapeDtypeStruct((rows, score_width), BF16),
        )
    )

    response_width = -(-(later_count * experts + 3) // LANES) * LANES
    response = pl.pallas_call(
        functools.partial(response_kernel, routed),
        out_shape=jax.ShapeDtypeStruct((rows, response_width), BF16),
        compiler_params=params(12 + 4 * grow),
        name="responses",
    )(scores, *states)
    own, later, picked = pl.pallas_call(
        functools.partial(chain_kernel, routed),
        out_shape=(
            jax.ShapeDtypeStruct((tokens, routed), BF16),
            jax.ShapeDtypeStruct((tokens, wide), BF16),
            jax.ShapeDtypeStruct((rows, wide), BF16),
        ),
        compiler_params=params(60),
        name="chain",
    )(response, *pass_down(response, layers), *states)

    slot_later = exchange(picked)

    result = by_columns(
        finish_kernel,
        [
            columns(tokens),
            whole((tokens, wide)),
            whole((tokens, routed)),
            columns(routed),
            router_spec,
            router_spec,
        ],
        columns(tokens),
        jax.ShapeDtypeStruct((tokens, width), BF16),
        [],
        "finish",
    )(twist, out_grad, later, own, router_t, near, far)

    slot_split, scale_grad = by_columns(
        slots_kernel,
        [
            columns(rows),
            pl.BlockSpec((rows, LANES), lambda *_: (0, width // LANES)),
            whole((rows, wide)),
            router_spec,
            router_spec,
            whole((size, rows, groups)),
            whole((span, span)),
        ],
        [whole((size, rows, groups)), whole((size, groups))],
        [
            jax.ShapeDtypeStruct((size, rows, groups), BF16),
            jax.ShapeDtypeStruct((size, groups), F32),
        ],
        [pltpu.VMEM((rows, width), BF16)],
        "slot_grads",
    )(twist, slots, slots, slot_later, near, far, plain_out, order)

    block = 128
    unroll = 64
    book_grad = pl.pallas_call(
        functools.partial(book_kernel, unroll),
        grid=(inner // block,),
        in_specs=[
            pl.BlockSpec((experts * MOST, block), lambda s: (0, s)),
            whole((size, rows, groups)),
            whole((size, groups)),
            pl.BlockSpec((books, block, groups), lambda s: (0, s, 0)),
        ],
        out_specs=whole((books, HIGH, LOW * size)),
        out_shape=jax.ShapeDtypeStruct((books, HIGH, LOW * size), F32),
        scratch_shapes=[
            pltpu.VMEM((groups // LANES, block * size, LANES), F32),
            pltpu.VMEM((books, groups // LANES, block, LANES), jnp.int32),
        ],
        compiler_params=params(60),
        name="book_grads",
    )(hidden, slot_split, scale_split, codes)

    book_grad = book_grad.reshape(books, HIGH * LOW, size)[:, :entries]
    scale_grad = scale_grad.T.reshape(width)
    return (result[None], book_grad[None, None], scale_grad[None, None])


def solution(mesh):
    placed = (
        P("expert", None),
        P("pipe", "expert", None),
        P("pipe", None, None),
        P("pipe", "expert", None),
        P("pipe", "expert", None, None),
        P("pipe", "expert", None, None, None),
        P("pipe", "expert", None, None, None),
        P("pipe", "expert", None),
    )
    return jax.shard_map(
        on_device,
        mesh=mesh,
        in_specs=placed,
        out_specs=(
            P("pipe", "expert", None),
            P("pipe", "expert", None, None, None),
            P("pipe", "expert", None),
        ),
        check_vma=False,
    )
```

```python
import functools
import math

import jax
import jax.numpy as jnp
from jax import lax
from jax.experimental import pallas as pl
from jax.experimental.pallas import tpu as pltpu
from jax.sharding import PartitionSpec as P

MOST = 9
SLOT = 16
ROUTE_SCALE = 16.0
LANES = 128
WIDE = 256
LOW = 6
HIGH = 48
F32 = jnp.float32
BF16 = jnp.bfloat16
I16 = jnp.int16


def params(mib):
    return pltpu.CompilerParams(vmem_limit_bytes=mib << 20)


def dot(a, b):
    return jnp.dot(a, b, preferred_element_type=F32)


def dot_nt(a, b):
    return lax.dot_general(a, b, (((1,), (1,)), ((), ())), preferred_element_type=F32)


def dot_tn(a, b):
    return lax.dot_general(a, b, (((0,), (0,)), ((), ())), preferred_element_type=F32)


def iota(shape, axis):
    return lax.broadcasted_iota(jnp.int32, shape, axis)


def lane_gather(table, index):
    return lax.gather(
        table,
        index[..., None],
        lax.GatherDimensionNumbers(
            offset_dims=(),
            collapsed_slice_dims=(1,),
            start_index_map=(1,),
            operand_batching_dims=(0,),
            start_indices_batching_dims=(0,),
        ),
        slice_sizes=(1, 1),
        mode=lax.GatherScatterMode.PROMISE_IN_BOUNDS,
    )


def slot_expert(rows, columns):
    return iota((rows, columns), 0) // SLOT == iota((rows, columns), 1)


def one_hot(mask):
    return mask.astype(F32).astype(BF16)


def spread_slots(hidden, rows):
    row = iota((rows, hidden.shape[0]), 0)
    place = row % SLOT
    source = iota((rows, hidden.shape[0]), 1)
    spread = one_hot((row // SLOT * MOST + place == source) & (place < MOST))
    return dot(spread, hidden).astype(BF16)


def slot_select(state, rows, routed):
    tokens, width = state.shape
    number = jnp.where(iota((tokens, width), 1) >= routed, state, 0.0).astype(BF16)
    owner = iota((width, rows), 0) - routed == iota((width, rows), 1) // SLOT
    place = (iota((tokens, rows), 1) % SLOT + 1).astype(F32)
    return one_hot(jnp.abs(dot(number, one_hot(owner)) - place) < 0.5)


def prepare_kernel(logits_ref, routes_ref, grad_ref, state_ref, rows_ref):
    tokens, routed = logits_ref.shape
    top = routes_ref.shape[1]
    width = grad_ref.shape[1]
    rows = rows_ref.shape[0]
    experts = rows // SLOT
    state_width = state_ref.shape[1]
    raised = jnp.exp(logits_ref[...])
    probs = raised / jnp.sum(raised, axis=1, keepdims=True)
    expert = iota((tokens, state_width), 1) - routed
    named = jnp.zeros((tokens, state_width), F32)
    for k in range(top):
        named = named + (routes_ref[:, k : k + 1] == expert).astype(F32)
    named = jnp.where(expert < experts, named, 0.0)
    earlier = one_hot(iota((tokens, tokens), 1) < iota((tokens, tokens), 0))
    state_ref[...] = named * (dot(earlier, named.astype(BF16)) + 1.0)
    state_ref[:, :routed] = probs
    select = slot_select(state_ref[...], rows, routed)
    gate = (ROUTE_SCALE * probs).astype(BF16)
    slot_gate = jnp.sum(
        jnp.where(slot_expert(rows, routed), dot_tn(select, gate), 0.0), axis=1, keepdims=True
    )
    rows_ref[:, :width] = dot_tn(select, grad_ref[...]).astype(BF16)
    rows_ref[:, width:] = jnp.broadcast_to(slot_gate, (rows, LANES)).astype(BF16)


def order_kernel(after_ref, order_ref):
    span = order_ref.shape[0]
    row = iota((span, span), 0)
    source = (span // LANES) * (row & (LANES - 1)) + row // LANES
    order_ref[...] = one_hot(source == iota((span, span), 1))


def decode_kernel(
    codes_ref, table_ref, hidden_ref, scale_ref, order_ref, plain_out_ref, out_ref, weight_ref
):
    unroll = 8
    step = pl.program_id(0)
    books, block, groups = codes_ref.shape
    entries = table_ref.shape[1]
    size = table_ref.shape[2]

    @pl.when(step == 0)
    def _():
        plain_out_ref[...] = jnp.zeros_like(plain_out_ref)

    hidden = spread_slots(hidden_ref[...], out_ref.shape[0])
    for chunk in range(groups // LANES):
        lanes = slice(chunk * LANES, (chunk + 1) * LANES)

        def decode_rows(index, carry):
            for member in range(unroll):
                at = pl.ds(pl.multiple_of((index * unroll + member) * 16, 16), 16)
                codes = [codes_ref[b, at, lanes].astype(I16) for b in range(books)]
                low = [c & I16(LANES - 1) for c in codes]
                part = [c >= I16(LANES) for c in codes]
                for i in range(size):
                    values = [
                        jnp.where(
                            part[b],
                            lane_gather(table_ref[b, 1, i], low[b]),
                            lane_gather(table_ref[b, 0, i], low[b]),
                        )
                        for b in range(books)
                    ]
                    weight_ref[at, i * LANES : (i + 1) * LANES] = sum(values[1:], values[0])
            return carry

        lax.fori_loop(0, block // 16 // unroll, decode_rows, 0)
        product = dot(hidden, weight_ref[...])
        for i in range(size):
            plain_out_ref[i, :, lanes] += product[:, i * LANES : (i + 1) * LANES]

    @pl.when(step == pl.num_programs(0) - 1)
    def _():
        rows = plain_out_ref.shape[1]
        split = [
            jnp.concatenate([plain_out_ref[i, :, at] * scale_ref[i : i + 1, at] for i in range(size)], 1)
            for at in (slice(c * LANES, (c + 1) * LANES) for c in range(groups // LANES))
        ]
        back = dot(jnp.concatenate(split, 0).astype(BF16), order_ref[...]).astype(BF16)
        span = size * LANES
        for chunk in range(groups // LANES):
            out_ref[:, chunk * span : (chunk + 1) * span] = back[chunk * rows : (chunk + 1) * rows]


def score_near_kernel(twist_ref, out_ref, slots_ref, router_ref, total_ref, base_ref):
    rows, width = out_ref.shape
    total_ref[...] = add_products(0, twist_ref[0], out_ref, router_ref, None)
    base = jnp.zeros((rows, LANES), F32)
    for c in range(width // LANES):
        at = slice(c * LANES, (c + 1) * LANES)
        base = base + slots_ref[:, at].astype(F32) * out_ref[:, at].astype(F32)
    base_ref[...] = jnp.broadcast_to(jnp.sum(base, axis=1, keepdims=True), (rows, LANES))


def add_products(far, twist, out_ref, router_ref, total):
    parts, later_count, routed, part_width = router_ref.shape
    for i in range(parts):
        first = (twist ^ (2 * i + far)) * part_width
        out = out_ref[:, pl.ds(pl.multiple_of(first, LANES), part_width)]
        product = dot_nt(router_ref[i].reshape(later_count * routed, part_width), out)
        total = product if total is None else total + product
    return total


def score_far_kernel(twist_ref, out_ref, router_ref, total_ref, base_ref, score_ref):
    rows = out_ref.shape[0]
    later_count, routed = router_ref.shape[1:3]
    wide = later_count * routed
    total = add_products(1, twist_ref[0], out_ref, router_ref, total_ref[...])
    tail = jnp.zeros((score_ref.shape[1] - wide, rows), F32)
    total = jnp.concatenate([total, tail], 0).T
    base = base_ref[:, :1]
    high = base.astype(BF16).astype(F32)
    middle = (base - high).astype(BF16).astype(F32)
    low = base - high - middle
    column = iota(total.shape, 1) - wide
    for place, part in enumerate((high, middle, low)):
        total = jnp.where(column == place, part, total)
    score_ref[...] = total.astype(BF16)


def response_kernel(routed, scores_ref, state_ref, *rest):
    *later_refs, response_ref = rest
    later_count = len(later_refs)
    rows, width = response_ref.shape
    experts = rows // SLOT
    select = slot_select(state_ref[...], rows, routed)
    column = iota((routed, width), 1)
    entry = iota((routed, width), 0)
    base_row, base_column = iota((LANES, width), 0), iota((LANES, width), 1)
    last = scores_ref.shape[1] - LANES
    base_row = base_row + last - later_count * routed
    total = dot(
        scores_ref[:, last:],
        one_hot(
            (base_column - later_count * experts == base_row) & (base_row >= 0) & (base_row < 3)
        ),
    )
    for s in range(later_count):
        probs = later_refs[s][:, :routed]
        high = probs.astype(BF16)
        low = (probs - high.astype(F32)).astype(BF16)
        picked = dot_tn(select, high) + dot_tn(select, low)
        product = scores_ref[:, s * routed : (s + 1) * routed].astype(F32)
        mean = jnp.sum(picked * product, axis=1, keepdims=True)
        response = (ROUTE_SCALE * picked * (product - mean)).astype(BF16)
        total = total + dot(
            response, one_hot((column - s * experts == entry) & (entry < experts))
        )
    response_ref[...] = total.astype(BF16)


def chain_kernel(routed, *refs):
    own_ref, later_ref, picked_ref = refs[-3:]
    count = (len(refs) - 3) // 2
    response_refs, state_refs = refs[:count], refs[count : 2 * count]
    rows, width = response_refs[0].shape
    tokens = state_refs[0].shape[0]
    experts = rows // SLOT
    column = iota((rows, width), 1)
    slot = iota((rows, width), 0)
    base = column >= (count - 1) * experts
    stacks = [jnp.zeros((tokens, width), F32) for _ in range(count)]
    own_select = None
    for s in range(count - 1, -1, -1):
        select = slot_select(state_refs[s][...], rows, routed)
        response = response_refs[s][...].astype(F32)
        terms = jnp.where(base, response, 0.0)
        if s < count - 1:
            terms = terms + dot_tn(select, stacks[s].astype(BF16)) * response
        score = jnp.sum(terms, axis=1, keepdims=True).astype(BF16).astype(F32)
        for u in range(s):
            first = (s - u - 1) * experts
            placed = jnp.where(column - first == slot // SLOT, score, 0.0).astype(BF16)
            stacks[u] = stacks[u] + dot(select, placed)
        placed = jnp.where(slot_expert(rows, routed), score, 0.0).astype(BF16)
        spread = dot(select, placed)
        probs = state_refs[s][:, :routed]
        weighted = jnp.sum(probs * spread, axis=1, keepdims=True)
        dlogit = (ROUTE_SCALE * probs * (spread - weighted)).astype(BF16)
        if s == 0:
            own_ref[...] = dlogit
            own_select = select
        else:
            later_ref[:, (s - 1) * WIDE : s * WIDE] = jnp.zeros((tokens, WIDE), BF16)
            later_ref[:, (s - 1) * WIDE : (s - 1) * WIDE + routed] = dlogit
    picked_ref[...] = dot_tn(own_select, later_ref[...]).astype(BF16)


def add_layers(current, later_ref, router_ref):
    later_count, routed = router_ref.shape[1:3]
    for s in range(later_count - 1, -1, -1):
        part = later_ref[:, s * WIDE : s * WIDE + routed]
        current = (current.astype(F32) + dot(part, router_ref[0, s])).astype(BF16)
    return current


def halves_of(twist, part_width):
    return [
        pl.ds(pl.multiple_of(((twist & 1) ^ far) * part_width, LANES), part_width)
        for far in range(2)
    ]


def finish_kernel(
    twist_ref, grad_ref, later_ref, own_ref, router_ref, near_ref, far_ref, result_ref
):
    places = halves_of(twist_ref[0], near_ref.shape[3])
    grads = [grad_ref[:, at] for at in places]
    routers = [router_ref[:, at] for at in places]
    results = []
    for grad, router, routers_ref in zip(grads, routers, (near_ref, far_ref)):
        current = add_layers(grad, later_ref, routers_ref)
        results.append((current.astype(F32) + dot(own_ref[...], router)).astype(BF16))
    for at, result in zip(places, results):
        result_ref[:, at] = result


def slots_kernel(
    twist_ref, slots_ref, gates_ref, later_ref, near_ref, far_ref, plain_out_ref, order_ref,
    split_ref, scale_grad_ref, grad_ref
):
    i = pl.program_id(0)
    part_width = near_ref.shape[3]
    size, _, groups = plain_out_ref.shape
    span = size * LANES
    twist = twist_ref[0]
    pair = ((twist >> 1) ^ i) * 2
    gate = gates_ref[:, :1].astype(F32)
    places = halves_of(twist, part_width)
    slots = [slots_ref[:, at] for at in places]
    grads = [
        (gate * add_layers(part, later_ref, routers_ref).astype(F32)).astype(BF16)
        for part, routers_ref in zip(slots, (near_ref, far_ref))
    ]
    for far in range(2):
        first = (pair + ((twist & 1) ^ far)) * part_width
        grad_ref[:, pl.ds(pl.multiple_of(first, LANES), part_width)] = grads[far]

    @pl.when(i == pl.num_programs(0) - 1)
    def _():
        rows = grad_ref.shape[0]
        chunks = groups // LANES
        grad = [grad_ref[:, c * span : (c + 1) * span] for c in range(chunks)]
        split = dot_nt(jnp.concatenate(grad, 0), order_ref[...])
        for c in range(chunks):
            lanes = slice(c * LANES, (c + 1) * LANES)
            for i in range(size):
                part = split[c * rows : (c + 1) * rows, i * LANES : (i + 1) * LANES]
                split_ref[i, :, lanes] = part.astype(BF16)
                scale_grad_ref[i : i + 1, lanes] = jnp.sum(
                    part * plain_out_ref[i, :, lanes], axis=0, keepdims=True
                )


def book_kernel(
    unroll, hidden_ref, slots_ref, scale_ref, codes_ref, out_ref, grad_ref, pair_ref
):
    books, block, groups = codes_ref.shape
    size = slots_ref.shape[0]
    chunks = groups // LANES

    @pl.when(pl.program_id(0) == 0)
    def _():
        out_ref[...] = jnp.zeros_like(out_ref)

    hidden = spread_slots(hidden_ref[...], slots_ref.shape[1])
    for i in range(size):
        grad = dot_tn(hidden, slots_ref[i]) * scale_ref[i : i + 1, :]
        for c in range(chunks):
            grad_ref[c, pl.ds(i, block, stride=size), :] = grad[:, c * LANES : (c + 1) * LANES]
    for b in range(books):
        for c in range(chunks):
            codes = codes_ref[b, :, c * LANES : (c + 1) * LANES]
            high = (codes * (65536 // LOW + 1)) >> 16
            pair_ref[b, c] = high * 8 + (codes - high * LOW)
    row = iota((16, LANES), 0)
    high_rows = [(row + 16 * k).astype(I16) for k in range(HIGH // 16)]
    low_rows = [((row >> 3) + 2 * k).astype(I16) for k in range(LOW // 2)]
    one = jnp.ones((16, LANES), BF16)
    zero = jnp.zeros((16, LANES), BF16)

    def add_rows(index, totals):
        totals = list(totals)
        for pair in range(unroll // 2):
            left = [[] for _ in range(books)]
            right = [[] for _ in range(books)]
            for member in range(2):
                f = index * unroll + pair * 2 + member
                at = pl.ds(pl.multiple_of(f * size, size), size)
                for c in range(chunks):
                    values = grad_ref[c, at, :]
                    values = jnp.concatenate([values, values], 0).astype(BF16)
                    for b in range(books):
                        pairs = pair_ref[b, c, pl.ds(f, 8, stride=0), :]
                        pairs = jnp.concatenate([pairs, pairs], 0).astype(I16)
                        high = pairs >> I16(3)
                        low = pairs & I16(7)
                        left[b].append(
                            jnp.concatenate([jnp.where(high == r, one, zero) for r in high_rows], 0)
                        )
                        right[b].append(
                            jnp.concatenate([jnp.where(low == r, values, zero) for r in low_rows], 0)
                        )
            for b in range(books):
                totals[b] = totals[b] + dot_nt(
                    jnp.concatenate(left[b], 1), jnp.concatenate(right[b], 1)
                )
        return tuple(totals)

    start = tuple(jnp.zeros(out_ref.shape[1:], F32) for _ in range(books))
    totals = lax.fori_loop(0, block // unroll, add_rows, start)
    for b in range(books):
        out_ref[b] += totals[b]


def whole(shape):
    return pl.BlockSpec(shape, lambda *_: (0,) * len(shape))


def exchange(value):
    return lax.all_to_all(value, "expert", split_axis=0, concat_axis=0, tiled=True)


def swap(value, distance):
    count = lax.axis_size("expert")
    return lax.ppermute(value, "expert", [(i, i ^ distance) for i in range(count)])


def pass_down(value, layers):
    return [
        lax.ppermute(value, "pipe", [(p, p - s) for p in range(s, layers)])
        for s in range(1, layers)
    ]


def join_kernel(*refs):
    *part_refs, out_ref, held_ref, in_sems, out_sems = refs
    count = len(part_refs)
    into = [
        pltpu.make_async_copy(part_refs[k], held_ref.at[k], in_sems.at[k]) for k in range(count)
    ]
    out = [
        pltpu.make_async_copy(held_ref.at[k], out_ref.at[k], out_sems.at[k]) for k in range(count)
    ]
    for copy in into:
        copy.start()
    for k in range(count):
        into[k].wait()
        out[k].start()
    for copy in out:
        copy.wait()


def join(parts):
    count = len(parts)
    joined = (count,) + parts[0].shape
    anywhere = pl.BlockSpec(memory_space=pl.ANY)
    return pl.pallas_call(
        join_kernel,
        in_specs=[anywhere] * count,
        out_specs=anywhere,
        out_shape=jax.ShapeDtypeStruct(joined, parts[0].dtype),
        scratch_shapes=[
            pltpu.VMEM(joined, parts[0].dtype),
            pltpu.SemaphoreType.DMA((count,)),
            pltpu.SemaphoreType.DMA((count,)),
        ],
        compiler_params=params(60),
        name="join",
    )(*parts)


def take_kernel(place_ref, value_ref, out_ref):
    out_ref[...] = value_ref[...]


def take(value, row, column, shape):
    return pl.pallas_call(
        take_kernel,
        grid_spec=pltpu.PrefetchScalarGridSpec(
            num_scalar_prefetch=1,
            grid=(1,),
            in_specs=[pl.BlockSpec(shape, lambda i, t: (t[0], t[1]))],
            out_specs=pl.BlockSpec(shape, lambda i, t: (0, 0)),
        ),
        out_shape=jax.ShapeDtypeStruct(shape, value.dtype),
        compiler_params=params(60),
        name="take",
    )(jnp.stack([row, column]).astype(jnp.int32), value)


def exchange_near(shares):
    count = lax.axis_size("expert")
    return [shares] + [swap(shares, d) for d in range(2, count, 2)]


def on_device(out_grad, saved_inputs, router, routes, hidden_saved, codes, codebook, scale):
    experts = lax.axis_size("expert")
    layers = lax.axis_size("pipe")
    place = lax.axis_index("expert")
    tokens, width = out_grad.shape
    routed = router.shape[2]
    codes = codes[0, 0]
    codebook = codebook[0, 0]
    hidden = hidden_saved[0, 0]
    inner = hidden.shape[1]
    books, _, groups = codes.shape
    entries, size = codebook.shape[1:]
    rows = experts * SLOT
    later_count = layers - 1
    wide = later_count * WIDE
    grow = max(1, rows // 128)
    router_t = router[0].T
    scale_split = scale[0, 0].reshape(groups, size).T

    parts = math.gcd(width // LANES, experts)
    direct = parts == experts
    sharers = experts // parts
    part_width = width // parts
    share_rows = routed // sharers
    own_share = take(router_t, place % sharers, place // sharers, (share_rows, part_width))
    shares = join(pass_down(own_share, layers))
    twist = jnp.full((1,), place if direct else 0, jnp.int32)

    logits = dot(saved_inputs[0], router[0])
    state_width = -(-(routed + experts) // LANES) * LANES
    span = size * LANES
    state, outgoing = pl.pallas_call(
        prepare_kernel,
        out_shape=(
            jax.ShapeDtypeStruct((tokens, state_width), F32),
            jax.ShapeDtypeStruct((rows, width + LANES), BF16),
        ),
        compiler_params=params(20 + 6 * grow),
        name="prepare",
    )(logits, routes[0], out_grad)
    slots = exchange(outgoing)
    hidden, outgoing = lax.optimization_barrier((hidden, outgoing))

    halves = entries // LANES
    table = codebook.transpose(0, 2, 1).reshape(books, size, halves, LANES)
    table = jnp.broadcast_to(
        table.transpose(0, 2, 1, 3)[:, :, :, None, :], (books, halves, size, 16, LANES)
    )
    block = 128

    blocks = inner // block

    later_states = pass_down(state, layers)
    hidden, shares, farthest = lax.optimization_barrier((hidden, shares, later_states[-1]))
    near = exchange_near(shares) if direct else None
    states = [state] + later_states[:-1] + [farthest]
    order = pl.pallas_call(
        order_kernel,
        in_specs=[pl.BlockSpec(memory_space=pl.ANY)],
        out_shape=jax.ShapeDtypeStruct((span, span), BF16),
        compiler_params=params(60),
        name="order",
    )(hidden)
    def decode():
        return pl.pallas_call(
            decode_kernel,
            grid=(blocks,),
            in_specs=[
                pl.BlockSpec((books, block, groups), lambda s: (0, s, 0)),
                whole((books, halves, size, 16, LANES)),
                pl.BlockSpec((experts * MOST, block), lambda s: (0, s)),
                whole((size, groups)),
                whole((span, span)),
            ],
            out_specs=[whole((size, rows, groups)), whole((rows, width))],
            out_shape=[
                jax.ShapeDtypeStruct((size, rows, groups), F32),
                jax.ShapeDtypeStruct((rows, width), BF16),
            ],
            scratch_shapes=[pltpu.VMEM((block, size * LANES), BF16)],
            compiler_params=params(60),
            cost_estimate=pl.CostEstimate(
                flops=blocks * 5_000_000_000, bytes_accessed=10_000_000, transcendentals=0
            ),
            name="decode",
        )(codes, table, hidden, scale_split, order)

    plain_out, expert_out = decode()
    if direct:
        near = join(near)
        plain_out, expert_out, near, slots, states = lax.optimization_barrier(
            (plain_out, expert_out, near, slots, states)
        )
        far = swap(near, 1)
    else:
        routers = lax.all_gather(shares, "expert", axis=0, tiled=False)
        routers = routers.reshape(parts, sharers, later_count, share_rows, part_width)
        routers = routers.transpose(0, 2, 1, 3, 4)
        routers = routers.reshape(parts, later_count, routed, part_width)
        near, far = routers[0::2], routers[1::2]

    grid = (parts // 2,)

    def columns(height):
        return pl.BlockSpec((height, 2 * part_width), lambda i, t: (0, (t[0] >> 1) ^ i))

    router_spec = pl.BlockSpec((1, later_count, routed, part_width), lambda i, t: (i, 0, 0, 0))

    def by_columns(kernel, in_specs, out_specs, out_shape, scratch, name):
        return pl.pallas_call(
            kernel,
            grid_spec=pltpu.PrefetchScalarGridSpec(
                num_scalar_prefetch=1,
                grid=grid,
                in_specs=in_specs,
                out_specs=out_specs,
                scratch_shapes=scratch,
            ),
            out_shape=out_shape,
            compiler_params=params(60),
            name=name,
        )

    def score(kernel, operands, out_shape):
        return pl.pallas_call(
            kernel,
            grid_spec=pltpu.PrefetchScalarGridSpec(
                num_scalar_prefetch=1,
                grid=(1,),
                in_specs=[whole(a.shape) for a in operands],
                out_specs=jax.tree.map(lambda a: whole(a.shape), out_shape),
            ),
            out_shape=out_shape,
            compiler_params=params(60),
            name="scores",
        )(twist, *operands)

    score_width = -(-(later_count * routed + 3) // LANES) * LANES
    sums = [
        jax.ShapeDtypeStruct((later_count * routed, rows), F32),
        jax.ShapeDtypeStruct((rows, LANES), F32),
    ]
    sums = score(score_near_kernel, [expert_out, slots, near], sums)
    scores = exchange(
        score(
            score_far_kernel,
            [expert_out, far, *sums],
            jax.ShapeDtypeStruct((rows, score_width), BF16),
        )
    )

    response_width = -(-(later_count * experts + 3) // LANES) * LANES
    response = pl.pallas_call(
        functools.partial(response_kernel, routed),
        out_shape=jax.ShapeDtypeStruct((rows, response_width), BF16),
        compiler_params=params(12 + 4 * grow),
        name="responses",
    )(scores, *states)
    own, later, picked = pl.pallas_call(
        functools.partial(chain_kernel, routed),
        out_shape=(
            jax.ShapeDtypeStruct((tokens, routed), BF16),
            jax.ShapeDtypeStruct((tokens, wide), BF16),
            jax.ShapeDtypeStruct((rows, wide), BF16),
        ),
        compiler_params=params(60),
        name="chain",
    )(response, *pass_down(response, layers), *states)

    slot_later = exchange(picked)

    result = by_columns(
        finish_kernel,
        [
            columns(tokens),
            whole((tokens, wide)),
            whole((tokens, routed)),
            columns(routed),
            router_spec,
            router_spec,
        ],
        columns(tokens),
        jax.ShapeDtypeStruct((tokens, width), BF16),
        [],
        "finish",
    )(twist, out_grad, later, own, router_t, near, far)

    slot_split, scale_grad = by_columns(
        slots_kernel,
        [
            columns(rows),
            pl.BlockSpec((rows, LANES), lambda *_: (0, width // LANES)),
            whole((rows, wide)),
            router_spec,
            router_spec,
            whole((size, rows, groups)),
            whole((span, span)),
        ],
        [whole((size, rows, groups)), whole((size, groups))],
        [
            jax.ShapeDtypeStruct((size, rows, groups), BF16),
            jax.ShapeDtypeStruct((size, groups), F32),
        ],
        [pltpu.VMEM((rows, width), BF16)],
        "slot_grads",
    )(twist, slots, slots, slot_later, near, far, plain_out, order)

    block = 128
    unroll = 64
    book_grad = pl.pallas_call(
        functools.partial(book_kernel, unroll),
        grid=(inner // block,),
        in_specs=[
            pl.BlockSpec((experts * MOST, block), lambda s: (0, s)),
            whole((size, rows, groups)),
            whole((size, groups)),
            pl.BlockSpec((books, block, groups), lambda s: (0, s, 0)),
        ],
        out_specs=whole((books, HIGH, LOW * size)),
        out_shape=jax.ShapeDtypeStruct((books, HIGH, LOW * size), F32),
        scratch_shapes=[
            pltpu.VMEM((groups // LANES, block * size, LANES), F32),
            pltpu.VMEM((books, groups // LANES, block, LANES), jnp.int32),
        ],
        compiler_params=params(60),
        name="book_grads",
    )(hidden, slot_split, scale_split, codes)

    book_grad = book_grad.reshape(books, HIGH * LOW, size)[:, :entries]
    scale_grad = scale_grad.T.reshape(width)
    return (result[None], book_grad[None, None], scale_grad[None, None])


def solution(mesh):
    placed = (
        P("expert", None),
        P("pipe", "expert", None),
        P("pipe", None, None),
        P("pipe", "expert", None),
        P("pipe", "expert", None, None),
        P("pipe", "expert", None, None, None),
        P("pipe", "expert", None, None, None),
        P("pipe", "expert", None),
    )
    return jax.shard_map(
        on_device,
        mesh=mesh,
        in_specs=placed,
        out_specs=(
            P("pipe", "expert", None),
            P("pipe", "expert", None, None, None),
            P("pipe", "expert", None),
        ),
        check_vma=False,
    )
```

```python
import functools
import math

import jax
import jax.numpy as jnp
from jax import lax
from jax.experimental import pallas as pl
from jax.experimental.pallas import tpu as pltpu
from jax.sharding import PartitionSpec as P

MOST = 9
SLOT = 16
ROUTE_SCALE = 16.0
LANES = 128
WIDE = 256
LOW = 6
HIGH = 48
F32 = jnp.float32
BF16 = jnp.bfloat16
I16 = jnp.int16


def params(mib):
    return pltpu.CompilerParams(vmem_limit_bytes=mib << 20)


def dot(a, b):
    return jnp.dot(a, b, preferred_element_type=F32)


def dot_nt(a, b):
    return lax.dot_general(a, b, (((1,), (1,)), ((), ())), preferred_element_type=F32)


def dot_tn(a, b):
    return lax.dot_general(a, b, (((0,), (0,)), ((), ())), preferred_element_type=F32)


def iota(shape, axis):
    return lax.broadcasted_iota(jnp.int32, shape, axis)


def lane_gather(table, index):
    return lax.gather(
        table,
        index[..., None],
        lax.GatherDimensionNumbers(
            offset_dims=(),
            collapsed_slice_dims=(1,),
            start_index_map=(1,),
            operand_batching_dims=(0,),
            start_indices_batching_dims=(0,),
        ),
        slice_sizes=(1, 1),
        mode=lax.GatherScatterMode.PROMISE_IN_BOUNDS,
    )


def slot_expert(rows, columns):
    return iota((rows, columns), 0) // SLOT == iota((rows, columns), 1)


def one_hot(mask):
    return mask.astype(F32).astype(BF16)


def spread_slots(hidden, rows):
    row = iota((rows, hidden.shape[0]), 0)
    place = row % SLOT
    source = iota((rows, hidden.shape[0]), 1)
    spread = one_hot((row // SLOT * MOST + place == source) & (place < MOST))
    return dot(spread, hidden).astype(BF16)


def slot_select(state, rows, routed):
    tokens, width = state.shape
    number = jnp.where(iota((tokens, width), 1) >= routed, state, 0.0).astype(BF16)
    owner = iota((width, rows), 0) - routed == iota((width, rows), 1) // SLOT
    place = (iota((tokens, rows), 1) % SLOT + 1).astype(F32)
    return one_hot(jnp.abs(dot(number, one_hot(owner)) - place) < 0.5)


def prepare_kernel(logits_ref, routes_ref, grad_ref, state_ref, rows_ref):
    tokens, routed = logits_ref.shape
    top = routes_ref.shape[1]
    width = grad_ref.shape[1]
    rows = rows_ref.shape[0]
    experts = rows // SLOT
    state_width = state_ref.shape[1]
    raised = jnp.exp(logits_ref[...])
    probs = raised / jnp.sum(raised, axis=1, keepdims=True)
    expert = iota((tokens, state_width), 1) - routed
    named = jnp.zeros((tokens, state_width), F32)
    for k in range(top):
        named = named + (routes_ref[:, k : k + 1] == expert).astype(F32)
    named = jnp.where(expert < experts, named, 0.0)
    earlier = one_hot(iota((tokens, tokens), 1) < iota((tokens, tokens), 0))
    state_ref[...] = named * (dot(earlier, named.astype(BF16)) + 1.0)
    state_ref[:, :routed] = probs
    select = slot_select(state_ref[...], rows, routed)
    gate = (ROUTE_SCALE * probs).astype(BF16)
    slot_gate = jnp.sum(
        jnp.where(slot_expert(rows, routed), dot_tn(select, gate), 0.0), axis=1, keepdims=True
    )
    rows_ref[:, :width] = dot_tn(select, grad_ref[...]).astype(BF16)
    rows_ref[:, width:] = jnp.broadcast_to(slot_gate, (rows, LANES)).astype(BF16)


def order_kernel(after_ref, order_ref):
    span = order_ref.shape[0]
    row = iota((span, span), 0)
    source = (span // LANES) * (row & (LANES - 1)) + row // LANES
    order_ref[...] = one_hot(source == iota((span, span), 1))


def decode_kernel(
    codes_ref, table_ref, hidden_ref, scale_ref, order_ref, plain_out_ref, out_ref, weight_ref
):
    unroll = 8
    step = pl.program_id(0)
    books, block, groups = codes_ref.shape
    entries = table_ref.shape[1]
    size = table_ref.shape[2]

    @pl.when(step == 0)
    def _():
        plain_out_ref[...] = jnp.zeros_like(plain_out_ref)

    hidden = spread_slots(hidden_ref[...], out_ref.shape[0])
    for chunk in range(groups // LANES):
        lanes = slice(chunk * LANES, (chunk + 1) * LANES)

        def decode_rows(index, carry):
            for member in range(unroll):
                at = pl.ds(pl.multiple_of((index * unroll + member) * 16, 16), 16)
                codes = [codes_ref[b, at, lanes].astype(I16) for b in range(books)]
                low = [c & I16(LANES - 1) for c in codes]
                part = [c >= I16(LANES) for c in codes]
                for i in range(size):
                    values = [
                        jnp.where(
                            part[b],
                            lane_gather(table_ref[b, 1, i], low[b]),
                            lane_gather(table_ref[b, 0, i], low[b]),
                        )
                        for b in range(books)
                    ]
                    weight_ref[at, i * LANES : (i + 1) * LANES] = sum(values[1:], values[0])
            return carry

        lax.fori_loop(0, block // 16 // unroll, decode_rows, 0)
        product = dot(hidden, weight_ref[...])
        for i in range(size):
            plain_out_ref[i, :, lanes] += product[:, i * LANES : (i + 1) * LANES]

    @pl.when(step == pl.num_programs(0) - 1)
    def _():
        rows = plain_out_ref.shape[1]
        split = [
            jnp.concatenate([plain_out_ref[i, :, at] * scale_ref[i : i + 1, at] for i in range(size)], 1)
            for at in (slice(c * LANES, (c + 1) * LANES) for c in range(groups // LANES))
        ]
        back = dot(jnp.concatenate(split, 0).astype(BF16), order_ref[...]).astype(BF16)
        span = size * LANES
        for chunk in range(groups // LANES):
            out_ref[:, chunk * span : (chunk + 1) * span] = back[chunk * rows : (chunk + 1) * rows]


def score_near_kernel(twist_ref, out_ref, slots_ref, router_ref, total_ref, base_ref):
    rows, width = out_ref.shape
    total_ref[...] = add_products(0, twist_ref[0], out_ref, router_ref, None)
    base = jnp.zeros((rows, LANES), F32)
    for c in range(width // LANES):
        at = slice(c * LANES, (c + 1) * LANES)
        base = base + slots_ref[:, at].astype(F32) * out_ref[:, at].astype(F32)
    base_ref[...] = jnp.broadcast_to(jnp.sum(base, axis=1, keepdims=True), (rows, LANES))


def add_products(far, twist, out_ref, router_ref, total):
    parts, later_count, routed, part_width = router_ref.shape
    for i in range(parts):
        first = (twist ^ (2 * i + far)) * part_width
        out = out_ref[:, pl.ds(pl.multiple_of(first, LANES), part_width)]
        product = dot_nt(router_ref[i].reshape(later_count * routed, part_width), out)
        total = product if total is None else total + product
    return total


def score_far_kernel(twist_ref, out_ref, router_ref, total_ref, base_ref, score_ref):
    rows = out_ref.shape[0]
    later_count, routed = router_ref.shape[1:3]
    wide = later_count * routed
    total = add_products(1, twist_ref[0], out_ref, router_ref, total_ref[...])
    tail = jnp.zeros((score_ref.shape[1] - wide, rows), F32)
    total = jnp.concatenate([total, tail], 0).T
    base = base_ref[:, :1]
    high = base.astype(BF16).astype(F32)
    middle = (base - high).astype(BF16).astype(F32)
    low = base - high - middle
    column = iota(total.shape, 1) - wide
    for place, part in enumerate((high, middle, low)):
        total = jnp.where(column == place, part, total)
    score_ref[...] = total.astype(BF16)


def response_kernel(routed, scores_ref, state_ref, *rest):
    *later_refs, response_ref = rest
    later_count = len(later_refs)
    rows, width = response_ref.shape
    experts = rows // SLOT
    select = slot_select(state_ref[...], rows, routed)
    column = iota((routed, width), 1)
    entry = iota((routed, width), 0)
    base_row, base_column = iota((LANES, width), 0), iota((LANES, width), 1)
    last = scores_ref.shape[1] - LANES
    base_row = base_row + last - later_count * routed
    total = dot(
        scores_ref[:, last:],
        one_hot(
            (base_column - later_count * experts == base_row) & (base_row >= 0) & (base_row < 3)
        ),
    )
    for s in range(later_count):
        probs = later_refs[s][:, :routed]
        high = probs.astype(BF16)
        low = (probs - high.astype(F32)).astype(BF16)
        picked = dot_tn(select, high) + dot_tn(select, low)
        product = scores_ref[:, s * routed : (s + 1) * routed].astype(F32)
        mean = jnp.sum(picked * product, axis=1, keepdims=True)
        response = (ROUTE_SCALE * picked * (product - mean)).astype(BF16)
        total = total + dot(
            response, one_hot((column - s * experts == entry) & (entry < experts))
        )
    response_ref[...] = total.astype(BF16)


def chain_kernel(routed, *refs):
    own_ref, later_ref, picked_ref = refs[-3:]
    count = (len(refs) - 3) // 2
    response_refs, state_refs = refs[:count], refs[count : 2 * count]
    rows, width = response_refs[0].shape
    tokens = state_refs[0].shape[0]
    experts = rows // SLOT
    column = iota((rows, width), 1)
    slot = iota((rows, width), 0)
    base = column >= (count - 1) * experts
    stacks = [jnp.zeros((tokens, width), F32) for _ in range(count)]
    own_select = None
    for s in range(count - 1, -1, -1):
        select = slot_select(state_refs[s][...], rows, routed)
        response = response_refs[s][...].astype(F32)
        terms = jnp.where(base, response, 0.0)
        if s < count - 1:
            terms = terms + dot_tn(select, stacks[s].astype(BF16)) * response
        score = jnp.sum(terms, axis=1, keepdims=True).astype(BF16).astype(F32)
        for u in range(s):
            first = (s - u - 1) * experts
            placed = jnp.where(column - first == slot // SLOT, score, 0.0).astype(BF16)
            stacks[u] = stacks[u] + dot(select, placed)
        placed = jnp.where(slot_expert(rows, routed), score, 0.0).astype(BF16)
        spread = dot(select, placed)
        probs = state_refs[s][:, :routed]
        weighted = jnp.sum(probs * spread, axis=1, keepdims=True)
        dlogit = (ROUTE_SCALE * probs * (spread - weighted)).astype(BF16)
        if s == 0:
            own_ref[...] = dlogit
            own_select = select
        else:
            later_ref[:, (s - 1) * WIDE : s * WIDE] = jnp.zeros((tokens, WIDE), BF16)
            later_ref[:, (s - 1) * WIDE : (s - 1) * WIDE + routed] = dlogit
    picked_ref[...] = dot_tn(own_select, later_ref[...]).astype(BF16)


def add_layers(current, later_ref, router_ref):
    later_count, routed = router_ref.shape[1:3]
    for s in range(later_count - 1, -1, -1):
        part = later_ref[:, s * WIDE : s * WIDE + routed]
        current = (current.astype(F32) + dot(part, router_ref[0, s])).astype(BF16)
    return current


def halves_of(twist, part_width):
    return [
        pl.ds(pl.multiple_of(((twist & 1) ^ far) * part_width, LANES), part_width)
        for far in range(2)
    ]


def finish_kernel(
    twist_ref, grad_ref, later_ref, own_ref, router_ref, near_ref, far_ref, result_ref
):
    places = halves_of(twist_ref[0], near_ref.shape[3])
    grads = [grad_ref[:, at] for at in places]
    routers = [router_ref[:, at] for at in places]
    results = []
    for grad, router, routers_ref in zip(grads, routers, (near_ref, far_ref)):
        current = add_layers(grad, later_ref, routers_ref)
        results.append((current.astype(F32) + dot(own_ref[...], router)).astype(BF16))
    for at, result in zip(places, results):
        result_ref[:, at] = result


def slots_kernel(
    twist_ref, slots_ref, gates_ref, later_ref, near_ref, far_ref, plain_out_ref, order_ref,
    split_ref, scale_grad_ref, grad_ref
):
    i = pl.program_id(0)
    part_width = near_ref.shape[3]
    size, _, groups = plain_out_ref.shape
    span = size * LANES
    twist = twist_ref[0]
    pair = ((twist >> 1) ^ i) * 2
    gate = gates_ref[:, :1].astype(F32)
    places = halves_of(twist, part_width)
    slots = [slots_ref[:, at] for at in places]
    grads = [
        (gate * add_layers(part, later_ref, routers_ref).astype(F32)).astype(BF16)
        for part, routers_ref in zip(slots, (near_ref, far_ref))
    ]
    for far in range(2):
        first = (pair + ((twist & 1) ^ far)) * part_width
        grad_ref[:, pl.ds(pl.multiple_of(first, LANES), part_width)] = grads[far]

    @pl.when(i == pl.num_programs(0) - 1)
    def _():
        rows = grad_ref.shape[0]
        chunks = groups // LANES
        grad = [grad_ref[:, c * span : (c + 1) * span] for c in range(chunks)]
        split = dot_nt(jnp.concatenate(grad, 0), order_ref[...])
        for c in range(chunks):
            lanes = slice(c * LANES, (c + 1) * LANES)
            for i in range(size):
                part = split[c * rows : (c + 1) * rows, i * LANES : (i + 1) * LANES]
                split_ref[i, :, lanes] = part.astype(BF16)
                scale_grad_ref[i : i + 1, lanes] = jnp.sum(
                    part * plain_out_ref[i, :, lanes], axis=0, keepdims=True
                )


def book_kernel(
    unroll, hidden_ref, slots_ref, scale_ref, codes_ref, out_ref, grad_ref, pair_ref
):
    books, block, groups = codes_ref.shape
    size = slots_ref.shape[0]
    chunks = groups // LANES

    @pl.when(pl.program_id(0) == 0)
    def _():
        out_ref[...] = jnp.zeros_like(out_ref)

    hidden = spread_slots(hidden_ref[...], slots_ref.shape[1])
    for i in range(size):
        grad = dot_tn(hidden, slots_ref[i]) * scale_ref[i : i + 1, :]
        for c in range(chunks):
            grad_ref[c, pl.ds(i, block, stride=size), :] = grad[:, c * LANES : (c + 1) * LANES]
    for b in range(books):
        for c in range(chunks):
            codes = codes_ref[b, :, c * LANES : (c + 1) * LANES]
            high = (codes * (65536 // LOW + 1)) >> 16
            pair_ref[b, c] = high * 8 + (codes - high * LOW)
    row = iota((16, LANES), 0)
    high_rows = [(row + 16 * k).astype(I16) for k in range(HIGH // 16)]
    low_rows = [((row >> 3) + 2 * k).astype(I16) for k in range(LOW // 2)]
    one = jnp.ones((16, LANES), BF16)
    zero = jnp.zeros((16, LANES), BF16)

    def add_rows(index, totals):
        totals = list(totals)
        for pair in range(unroll // 2):
            left = [[] for _ in range(books)]
            right = [[] for _ in range(books)]
            for member in range(2):
                f = index * unroll + pair * 2 + member
                at = pl.ds(pl.multiple_of(f * size, size), size)
                for c in range(chunks):
                    values = grad_ref[c, at, :]
                    values = jnp.concatenate([values, values], 0).astype(BF16)
                    for b in range(books):
                        pairs = pair_ref[b, c, pl.ds(f, 8, stride=0), :]
                        pairs = jnp.concatenate([pairs, pairs], 0).astype(I16)
                        high = pairs >> I16(3)
                        low = pairs & I16(7)
                        left[b].append(
                            jnp.concatenate([jnp.where(high == r, one, zero) for r in high_rows], 0)
                        )
                        right[b].append(
                            jnp.concatenate([jnp.where(low == r, values, zero) for r in low_rows], 0)
                        )
            for b in range(books):
                totals[b] = totals[b] + dot_nt(
                    jnp.concatenate(left[b], 1), jnp.concatenate(right[b], 1)
                )
        return tuple(totals)

    start = tuple(jnp.zeros(out_ref.shape[1:], F32) for _ in range(books))
    totals = lax.fori_loop(0, block // unroll, add_rows, start)
    for b in range(books):
        out_ref[b] += totals[b]


def whole(shape):
    return pl.BlockSpec(shape, lambda *_: (0,) * len(shape))


def exchange(value):
    return lax.all_to_all(value, "expert", split_axis=0, concat_axis=0, tiled=True)


def swap(value, distance):
    count = lax.axis_size("expert")
    return lax.ppermute(value, "expert", [(i, i ^ distance) for i in range(count)])


def pass_down(value, layers):
    return [
        lax.ppermute(value, "pipe", [(p, p - s) for p in range(s, layers)])
        for s in range(1, layers)
    ]


def join_kernel(*refs):
    *part_refs, out_ref, held_ref, in_sems, out_sems = refs
    count = len(part_refs)
    into = [
        pltpu.make_async_copy(part_refs[k], held_ref.at[k], in_sems.at[k]) for k in range(count)
    ]
    out = [
        pltpu.make_async_copy(held_ref.at[k], out_ref.at[k], out_sems.at[k]) for k in range(count)
    ]
    for copy in into:
        copy.start()
    for k in range(count):
        into[k].wait()
        out[k].start()
    for copy in out:
        copy.wait()


def join(parts):
    count = len(parts)
    joined = (count,) + parts[0].shape
    anywhere = pl.BlockSpec(memory_space=pl.ANY)
    return pl.pallas_call(
        join_kernel,
        in_specs=[anywhere] * count,
        out_specs=anywhere,
        out_shape=jax.ShapeDtypeStruct(joined, parts[0].dtype),
        scratch_shapes=[
            pltpu.VMEM(joined, parts[0].dtype),
            pltpu.SemaphoreType.DMA((count,)),
            pltpu.SemaphoreType.DMA((count,)),
        ],
        compiler_params=params(60),
        name="join",
    )(*parts)


def exchange_near(shares):
    count = lax.axis_size("expert")
    return [shares] + [swap(shares, d) for d in range(2, count, 2)]


def on_device(out_grad, saved_inputs, router, routes, hidden_saved, codes, codebook, scale):
    experts = lax.axis_size("expert")
    layers = lax.axis_size("pipe")
    place = lax.axis_index("expert")
    tokens, width = out_grad.shape
    routed = router.shape[2]
    codes = codes[0, 0]
    codebook = codebook[0, 0]
    hidden = hidden_saved[0, 0]
    inner = hidden.shape[1]
    books, _, groups = codes.shape
    entries, size = codebook.shape[1:]
    rows = experts * SLOT
    later_count = layers - 1
    wide = later_count * WIDE
    grow = max(1, rows // 128)
    router_t = router[0].T
    scale_split = scale[0, 0].reshape(groups, size).T

    parts = math.gcd(width // LANES, experts)
    direct = parts == experts
    sharers = experts // parts
    part_width = width // parts
    share_rows = routed // sharers
    own_share = lax.dynamic_slice(
        router_t,
        ((place % sharers) * share_rows, (place // sharers) * part_width),
        (share_rows, part_width),
    )
    shares = join(pass_down(own_share, layers))
    twist = jnp.full((1,), place if direct else 0, jnp.int32)

    logits = dot(saved_inputs[0], router[0])
    state_width = -(-(routed + experts) // LANES) * LANES
    span = size * LANES
    state, outgoing = pl.pallas_call(
        prepare_kernel,
        out_shape=(
            jax.ShapeDtypeStruct((tokens, state_width), F32),
            jax.ShapeDtypeStruct((rows, width + LANES), BF16),
        ),
        compiler_params=params(20 + 6 * grow),
        name="prepare",
    )(logits, routes[0], out_grad)
    slots = exchange(outgoing)
    hidden, outgoing = lax.optimization_barrier((hidden, outgoing))

    halves = entries // LANES
    table = codebook.transpose(0, 2, 1).reshape(books, size, halves, LANES)
    table = jnp.broadcast_to(
        table.transpose(0, 2, 1, 3)[:, :, :, None, :], (books, halves, size, 16, LANES)
    )
    block = 128

    blocks = inner // block

    later_states = pass_down(state, layers)
    hidden, shares, farthest = lax.optimization_barrier((hidden, shares, later_states[-1]))
    near = exchange_near(shares) if direct else None
    states = [state] + later_states[:-1] + [farthest]
    order = pl.pallas_call(
        order_kernel,
        in_specs=[pl.BlockSpec(memory_space=pl.ANY)],
        out_shape=jax.ShapeDtypeStruct((span, span), BF16),
        compiler_params=params(60),
        name="order",
    )(hidden)
    def decode():
        return pl.pallas_call(
            decode_kernel,
            grid=(blocks,),
            in_specs=[
                pl.BlockSpec((books, block, groups), lambda s: (0, s, 0)),
                whole((books, halves, size, 16, LANES)),
                pl.BlockSpec((experts * MOST, block), lambda s: (0, s)),
                whole((size, groups)),
                whole((span, span)),
            ],
            out_specs=[whole((size, rows, groups)), whole((rows, width))],
            out_shape=[
                jax.ShapeDtypeStruct((size, rows, groups), F32),
                jax.ShapeDtypeStruct((rows, width), BF16),
            ],
            scratch_shapes=[pltpu.VMEM((block, size * LANES), BF16)],
            compiler_params=params(60),
            cost_estimate=pl.CostEstimate(
                flops=blocks * 5_000_000_000, bytes_accessed=10_000_000, transcendentals=0
            ),
            name="decode",
        )(codes, table, hidden, scale_split, order)

    plain_out, expert_out = decode()
    if direct:
        near = join(near)
        plain_out, expert_out, near, slots, states = lax.optimization_barrier(
            (plain_out, expert_out, near, slots, states)
        )
        far = swap(near, 1)
    else:
        routers = lax.all_gather(shares, "expert", axis=0, tiled=False)
        routers = routers.reshape(parts, sharers, later_count, share_rows, part_width)
        routers = routers.transpose(0, 2, 1, 3, 4)
        routers = routers.reshape(parts, later_count, routed, part_width)
        near, far = routers[0::2], routers[1::2]

    grid = (parts // 2,)

    def columns(height):
        return pl.BlockSpec((height, 2 * part_width), lambda i, t: (0, (t[0] >> 1) ^ i))

    router_spec = pl.BlockSpec((1, later_count, routed, part_width), lambda i, t: (i, 0, 0, 0))

    def by_columns(kernel, in_specs, out_specs, out_shape, scratch, name):
        return pl.pallas_call(
            kernel,
            grid_spec=pltpu.PrefetchScalarGridSpec(
                num_scalar_prefetch=1,
                grid=grid,
                in_specs=in_specs,
                out_specs=out_specs,
                scratch_shapes=scratch,
            ),
            out_shape=out_shape,
            compiler_params=params(60),
            name=name,
        )

    def score(kernel, operands, out_shape):
        return pl.pallas_call(
            kernel,
            grid_spec=pltpu.PrefetchScalarGridSpec(
                num_scalar_prefetch=1,
                grid=(1,),
                in_specs=[whole(a.shape) for a in operands],
                out_specs=jax.tree.map(lambda a: whole(a.shape), out_shape),
            ),
            out_shape=out_shape,
            compiler_params=params(60),
            name="scores",
        )(twist, *operands)

    score_width = -(-(later_count * routed + 3) // LANES) * LANES
    sums = [
        jax.ShapeDtypeStruct((later_count * routed, rows), F32),
        jax.ShapeDtypeStruct((rows, LANES), F32),
    ]
    sums = score(score_near_kernel, [expert_out, slots, near], sums)
    scores = exchange(
        score(
            score_far_kernel,
            [expert_out, far, *sums],
            jax.ShapeDtypeStruct((rows, score_width), BF16),
        )
    )

    response_width = -(-(later_count * experts + 3) // LANES) * LANES
    response = pl.pallas_call(
        functools.partial(response_kernel, routed),
        out_shape=jax.ShapeDtypeStruct((rows, response_width), BF16),
        compiler_params=params(12 + 4 * grow),
        name="responses",
    )(scores, *states)
    own, later, picked = pl.pallas_call(
        functools.partial(chain_kernel, routed),
        out_shape=(
            jax.ShapeDtypeStruct((tokens, routed), BF16),
            jax.ShapeDtypeStruct((tokens, wide), BF16),
            jax.ShapeDtypeStruct((rows, wide), BF16),
        ),
        compiler_params=params(12 + 4 * grow),
        name="chain",
    )(response, *pass_down(response, layers), *states)

    slot_later = exchange(picked)

    result = by_columns(
        finish_kernel,
        [
            columns(tokens),
            whole((tokens, wide)),
            whole((tokens, routed)),
            columns(routed),
            router_spec,
            router_spec,
        ],
        columns(tokens),
        jax.ShapeDtypeStruct((tokens, width), BF16),
        [],
        "finish",
    )(twist, out_grad, later, own, router_t, near, far)

    slot_split, scale_grad = by_columns(
        slots_kernel,
        [
            columns(rows),
            pl.BlockSpec((rows, LANES), lambda *_: (0, width // LANES)),
            whole((rows, wide)),
            router_spec,
            router_spec,
            whole((size, rows, groups)),
            whole((span, span)),
        ],
        [whole((size, rows, groups)), whole((size, groups))],
        [
            jax.ShapeDtypeStruct((size, rows, groups), BF16),
            jax.ShapeDtypeStruct((size, groups), F32),
        ],
        [pltpu.VMEM((rows, width), BF16)],
        "slot_grads",
    )(twist, slots, slots, slot_later, near, far, plain_out, order)

    block = 128
    unroll = 64
    book_grad = pl.pallas_call(
        functools.partial(book_kernel, unroll),
        grid=(inner // block,),
        in_specs=[
            pl.BlockSpec((experts * MOST, block), lambda s: (0, s)),
            whole((size, rows, groups)),
            whole((size, groups)),
            pl.BlockSpec((books, block, groups), lambda s: (0, s, 0)),
        ],
        out_specs=whole((books, HIGH, LOW * size)),
        out_shape=jax.ShapeDtypeStruct((books, HIGH, LOW * size), F32),
        scratch_shapes=[
            pltpu.VMEM((groups // LANES, block * size, LANES), F32),
            pltpu.VMEM((books, groups // LANES, block, LANES), jnp.int32),
        ],
        compiler_params=params(60),
        name="book_grads",
    )(hidden, slot_split, scale_split, codes)

    book_grad = book_grad.reshape(books, HIGH * LOW, size)[:, :entries]
    scale_grad = scale_grad.T.reshape(width)
    return (result[None], book_grad[None, None], scale_grad[None, None])


def solution(mesh):
    placed = (
        P("expert", None),
        P("pipe", "expert", None),
        P("pipe", None, None),
        P("pipe", "expert", None),
        P("pipe", "expert", None, None),
        P("pipe", "expert", None, None, None),
        P("pipe", "expert", None, None, None),
        P("pipe", "expert", None),
    )
    return jax.shard_map(
        on_device,
        mesh=mesh,
        in_specs=placed,
        out_specs=(
            P("pipe", "expert", None),
            P("pipe", "expert", None, None, None),
            P("pipe", "expert", None),
        ),
        check_vma=False,
    )
```
